32 devices in a mesh: dp: 4 (over y, core), ctx: 8 (over z, x).
Axes of the slice: x: 2, y: 2, z: 4, core: 2. Of those that a mesh axis runs over, the one named last changes fastest.
Arguments:
- queries: bfloat16 [4, 1024, 1152], P('dp', 'ctx')
- key_states: bfloat16 [4, 1024, 1152], P('dp', 'ctx')
- value_states: bfloat16 [4, 1024, 1152], P('dp', 'ctx'), may hold values from -6 to 6
- out_cotangent: bfloat16 [4, 1024, 1024], P('dp', 'ctx'), may hold values from -0.875 to 0.875
- out_weight: bfloat16 [1024, 1152], replicated, may hold values from -3 to 3
- block_clip: int32 [4, 8], P('dp', 'ctx'), may hold values from 0 to 1, never falling along the last dimension, each value on 1 to 7 neighbouring positions
Outputs:
- sublayer_out: bfloat16 [4, 1024, 1024], P('dp', 'ctx')
- query_grad: bfloat16 [4, 1024, 1152], P('dp', 'ctx')
- key_grad: bfloat16 [4, 1024, 1152], P('dp', 'ctx')
- value_grad: bfloat16 [4, 1024, 1152], P('dp', 'ctx')
- weight_grad: float32 [1024, 1152], P('ctx', 'dp')
The draws below stay inside these ranges and needn't reach their ends.
All inputs are finite; a program needn't handle non-finite values.
Results may differ from the reference program's by a relative error of at most 0.034.
Values may be sent and summed in bfloat16 or wider, within the bound.
No kernel may reach another device: no remote copies, remote signals or barrier semaphores. Data moves between devices by JAX's collectives and lax.ppermute only.
A program may use at most 64 MiB of HBM per device.

```python
import math
import jax
import jax.numpy as jnp
import numpy as np
from jax import lax

HEADS = 18
HDIM = 64
HD = 1152
DOUT = 1024
BLOCK = 128
WIN = 256
TOK_DEV = 128
LENGTH = 1024
SEQS = 4
NBLK = 8
CLIPS = 2
CLIP_MOST = 7
N_CTX = 8


def paired_rows(key):
    shape = (SEQS, LENGTH, HEADS * HDIM)
    base_query = jnp.clip(jax.random.normal(jax.random.fold_in(key, 101), shape, jnp.float32), -6.0, 6.0)
    base_key = jnp.clip(jax.random.normal(jax.random.fold_in(key, 202), shape, jnp.float32), -6.0, 6.0)
    return (base_query, base_key)


def draw_queries(key, part):
    return paired_rows(key)[0].astype(jnp.bfloat16)


def draw_key_states(key, part):
    return paired_rows(key)[1].astype(jnp.bfloat16)


def strengthened(result, key, source, target, shards_of, factor):
    def block_of(dim):
        return (jnp.arange(result.shape[dim]) // (result.shape[dim] // shards_of)).reshape((-1,) + (1,) * (result.ndim - 1 - dim))

    near = jax.random.permutation(key, shards_of)[block_of(target)]
    second = (block_of(target) + shards_of // 2) % shards_of
    return jnp.where((block_of(source) == near) | (block_of(source) == second), factor * result, result)


def shard_levels(rng, shape, split, smallest, top_value):
    def one(position, blocks):
        heights = jax.random.uniform(jax.random.fold_in(jax.random.fold_in(rng, 6), position), (blocks,), jnp.float32, smallest / len(split), top_value / len(split))
        return jnp.repeat(jnp.exp(heights), shape[position] // blocks).reshape((-1,) + (1,) * (len(shape) - position - 1))

    gain = one(*split[0])
    for cut in split[1:]:
        gain = gain * one(*cut)
    return gain


def profile(amount, total, most, lean):
    portions = [(1 << 20) // math.isqrt(rank ** lean) + 1 for rank in range(2, amount + 1)]
    spare, given = total - most - (amount - 1), [1] * (amount - 1)
    while spare > 0:
        free = [i for i in range(amount - 1) if given[i] < most]
        whole, budget = sum([portions[i] for i in free]), spare
        for i in free:
            more = min(most - given[i], max(1, budget * portions[i] // whole), spare)
            given[i] = given[i] + more
            spare = spare - more
    return np.array([most] + given)


def ragged(own_key, amount, total, bound, slope):
    if amount == 2:
        one = jax.random.randint(own_key, (), max(1, total - bound), min(bound, total - 1) + 1)
        return jnp.stack([one, total - one])
    sizes = jnp.asarray(profile(amount, total, bound, slope), jnp.int32)
    pairs = (amount - 1) // 2
    donor, taker = sizes[1:1 + 2 * pairs:2], sizes[2:2 + 2 * pairs:2]
    room = jnp.minimum(donor - 1, bound - taker)
    moved = jax.random.randint(jax.random.fold_in(own_key, 1), (pairs,), 0, 1 << 20) % (room + 1)
    sizes = sizes.at[1:1 + 2 * pairs:2].set(donor - moved).at[2:2 + 2 * pairs:2].set(taker + moved)
    return sizes[jax.random.permutation(jax.random.fold_in(own_key, 2), amount)]


def bell_draw(stream_key, dims, deviation, bound, split=(), held_as=jnp.bfloat16):
    drawn = jax.random.normal(stream_key, dims, jnp.float32) * deviation
    if len(split) > 0:
        drawn = shard_levels(stream_key, dims, split, -0.22, 0.18) * drawn
    return jnp.clip(drawn, min=-bound, max=bound).astype(held_as)


def heavy_noise(own_key, extent, deviation, bound, shards, heavy, kind=jnp.bfloat16):
    result = deviation * jax.random.normal(own_key, extent, jnp.float32)
    if shards:
        result = result * shard_levels(own_key, extent, shards, -0.22, 0.18)
    return jnp.clip(strengthened(result, jax.random.fold_in(own_key, 3), *heavy), -bound, bound).astype(kind)


def setup_inputs(seed: int = 0) -> dict:
    key_list = jax.random.split(jax.random.key(seed), 7)
    queries = draw_queries(jax.random.fold_in(key_list[6], 71), 0)
    key_states = draw_key_states(jax.random.fold_in(key_list[6], 71), 0)
    value_states = bell_draw(key_list[2], (SEQS, LENGTH, HD), 1.0, 6.0, ((0, 4), (1, 8)))
    out_cotangent = heavy_noise(key_list[3], (SEQS, LENGTH, DOUT), 0.1, 0.875, ((0, 4), (1, 8)), (1, 2, 8, 2.0))
    out_weight = bell_draw(key_list[4], (DOUT, HD), (16.0 / HD ** 0.5), 3.0)
    block_clip = jax.vmap(lambda own: jnp.searchsorted(jnp.cumsum(ragged(own, CLIPS, NBLK, CLIP_MOST, 2)), jnp.arange(NBLK), side="right"))(jax.random.split(key_list[5], SEQS)).reshape((SEQS, NBLK)).astype(jnp.int32)
    return {"queries": queries, "key_states": key_states, "value_states": value_states, "out_cotangent": out_cotangent, "out_weight": out_weight, "block_clip": block_clip}


def split_heads(matrix):
    return matrix.reshape(matrix.shape[0], HEADS, HDIM).transpose(1, 0, 2)

def merge_heads(stacked):
    return stacked.transpose(1, 0, 2).reshape(stacked.shape[1], HEADS * HDIM)

def rounded_back(values):
    return lax.optimization_barrier(values.astype(jnp.bfloat16)).astype(jnp.float32)

def reference(queries, key_states, value_states, out_cotangent, out_weight, block_clip):
    scaling = 1.0 / math.sqrt(HDIM)
    width = HEADS * HDIM
    zero_rows = jnp.zeros((WIN, width), jnp.bfloat16)
    weight_f32 = out_weight

    def one_sequence(weight_sum, inputs):
        query_seq, key_seq, value_seq, cotangent_seq, clip_seq = inputs
        clip_steps = jnp.repeat(clip_seq, BLOCK).astype(jnp.int32)
        key_padded = jnp.concatenate([zero_rows, key_seq], axis=0)
        value_padded = jnp.concatenate([zero_rows, value_seq], axis=0)
        clip_padded = jnp.concatenate([jnp.full((WIN,), -1, jnp.int32), clip_steps], axis=0)

        def one_range(carry, index):
            key_acc, value_acc, weight_acc = carry
            start = (index * TOK_DEV).astype(jnp.int32)
            query_rows = lax.dynamic_slice_in_dim(query_seq, start, TOK_DEV, 0)
            cotangent_rows = lax.dynamic_slice_in_dim(cotangent_seq, start, TOK_DEV, 0)
            key_rows = lax.dynamic_slice_in_dim(key_padded, start, TOK_DEV + WIN, 0)
            value_rows = lax.dynamic_slice_in_dim(value_padded, start, TOK_DEV + WIN, 0)
            query_clip = lax.dynamic_slice_in_dim(clip_steps, start, TOK_DEV, 0)
            key_clip = lax.dynamic_slice_in_dim(clip_padded, start, TOK_DEV + WIN, 0)
            query_pos = start + jnp.arange(TOK_DEV, dtype=jnp.int32)
            key_pos = start - WIN + jnp.arange(TOK_DEV + WIN, dtype=jnp.int32)
            visible = (key_pos[None, :] <= query_pos[:, None]) & (query_pos[:, None] - key_pos[None, :] < WIN)
            visible = visible & (key_pos[None, :] >= 0) & (query_clip[:, None] == key_clip[None, :])
            query_heads = split_heads(query_rows).astype(jnp.float32)
            key_heads = split_heads(key_rows).astype(jnp.float32)
            value_heads = split_heads(value_rows).astype(jnp.float32)
            scores = jnp.einsum('hqd,hkd->hqk', query_heads, key_heads) * scaling
            scores = jnp.where(visible[None], scores, -1e+30)
            maximum = lax.optimization_barrier(jnp.max(scores, axis=2, keepdims=True))
            log_total = maximum[:, :, 0] + jnp.log(lax.optimization_barrier(jnp.sum(jnp.exp(scores - maximum), axis=2)))
            probs = jnp.exp(scores - log_total[:, :, None])
            weights = probs.astype(jnp.bfloat16)
            attended = merge_heads(jnp.einsum('hqk,hkd->hqd', weights.astype(jnp.float32), value_heads)).astype(jnp.bfloat16)
            output_rows = jnp.dot(attended, weight_f32.T, preferred_element_type=jnp.float32).astype(jnp.bfloat16)
            d_attended = jnp.dot(cotangent_rows, weight_f32, preferred_element_type=jnp.float32).astype(jnp.bfloat16)
            d_heads = split_heads(d_attended).astype(jnp.float32)
            delta = lax.optimization_barrier(jnp.sum(d_heads * split_heads(attended).astype(jnp.float32), axis=2))
            d_weights = jnp.einsum('hqd,hkd->hqk', d_heads, value_heads)
            d_scores = (probs * (d_weights - delta[:, :, None]) * scaling).astype(jnp.bfloat16)
            query_grad = merge_heads(jnp.einsum('hqk,hkd->hqd', d_scores.astype(jnp.float32), key_heads)).astype(jnp.bfloat16)
            key_part = rounded_back(merge_heads(jnp.einsum('hqk,hqd->hkd', d_scores.astype(jnp.float32), query_heads)))
            value_part = rounded_back(merge_heads(jnp.einsum('hqk,hqd->hkd', weights.astype(jnp.float32), d_heads)))
            current_key = lax.dynamic_slice_in_dim(key_acc, start, TOK_DEV + WIN, 0)
            current_value = lax.dynamic_slice_in_dim(value_acc, start, TOK_DEV + WIN, 0)
            key_acc = lax.dynamic_update_slice_in_dim(key_acc, current_key + key_part, start, 0)
            value_acc = lax.dynamic_update_slice_in_dim(value_acc, current_value + value_part, start, 0)
            weight_part = rounded_back(jnp.dot(cotangent_rows.T, attended, preferred_element_type=jnp.float32))
            return ((key_acc, value_acc, weight_acc + weight_part), (output_rows, query_grad))
        start_acc = jnp.zeros((WIN + LENGTH, width), jnp.float32)
        indices = jnp.arange(N_CTX, dtype=jnp.int32)
        (key_acc, value_acc, weight_sum), (output_rows, query_grad) = lax.scan(one_range, (start_acc, start_acc, weight_sum), indices)
        results = (output_rows.reshape(LENGTH, DOUT), query_grad.reshape(LENGTH, width), key_acc[WIN:].astype(jnp.bfloat16), value_acc[WIN:].astype(jnp.bfloat16))
        return (weight_sum, results)
    weight_start = jnp.zeros((DOUT, width), jnp.float32)
    weight_grad, (sublayer_out, query_grad, key_grad, value_grad) = lax.scan(one_sequence, weight_start, (queries, key_states, value_states, out_cotangent, block_clip))
    return (sublayer_out, query_grad, key_grad, value_grad, weight_grad)
```

```python
import functools
import math

import jax
import jax.numpy as jnp
from jax import lax
from jax.experimental import pallas as pl
from jax.experimental.pallas import tpu as pltpu
from jax.sharding import PartitionSpec as P

HEADS = 18
HDIM = 64
BLOCK = 128
WIN = 256
PAIR = 2 * HDIM
WIDTH = HEADS * HDIM
PAIRS = (HEADS + 2) // 4
PART = PAIRS * PAIR
START = WIDTH - PART
REST = WIDTH - PART
CLIP_ROWS = 16
PAYLOAD = 2 * BLOCK + CLIP_ROWS
SCALING = 1.0 / math.sqrt(HDIM)
VMEM_LIMIT = 48 * 1024 * 1024

big_negative = -1e30
bf16 = jnp.bfloat16
f32 = jnp.float32

SMEM = pl.BlockSpec(memory_space=pltpu.SMEM)
VMEM = pl.BlockSpec(memory_space=pltpu.VMEM)


def shaped(shape, dtype):
    return jax.ShapeDtypeStruct(shape, dtype)


def estimate(flops, moved):
    return pl.CostEstimate(flops=flops, bytes_accessed=moved, transcendentals=0)


def params():
    return pltpu.CompilerParams(vmem_limit_bytes=VMEM_LIMIT)


def at(index, size):
    return pl.ds(pl.multiple_of(index * size, size), size)


def span(start, size, unit):
    return pl.ds(pl.multiple_of(start, unit), size)


def times(a, b, dims):
    return lax.dot_general(a, b, (dims, ((), ())), preferred_element_type=f32)


def pack_kernel(where, clip, query, key, value, swap_kv, own_kv, swap_query):
    half = where[0]
    mine = span(half * START, PART, 128)
    other = span((1 - half) * START, PART, 128)
    clip_rows = jnp.full((CLIP_ROWS, PART), clip[0, 0].astype(f32), f32).astype(bf16)
    swap_kv[0:BLOCK] = key[:, other]
    swap_kv[BLOCK : 2 * BLOCK] = value[:, other]
    swap_kv[2 * BLOCK :] = clip_rows
    own_kv[0:BLOCK] = key[:, mine]
    own_kv[BLOCK : 2 * BLOCK] = value[:, mine]
    own_kv[2 * BLOCK :] = clip_rows
    swap_query[...] = query[:, other]


def pack(where, clip, query, key, value):
    return pl.pallas_call(
        pack_kernel,
        out_shape=(
            shaped((PAYLOAD, PART), bf16),
            shaped((PAYLOAD, PART), bf16),
            shaped((BLOCK, PART), bf16),
        ),
        in_specs=[SMEM, SMEM, VMEM, VMEM, VMEM],
        out_specs=(VMEM, VMEM, VMEM),
        compiler_params=params(),
        cost_estimate=estimate(0, 3_000_000),
        name="pack",
    )(where, clip, query, key, value)


def gather_rows(target, half, offset, own, partner, own_at):
    target[at(offset + half, BLOCK)] = own[own_at : own_at + BLOCK]
    target[at(offset + 1 - half, BLOCK)] = partner[own_at : own_at + BLOCK]


def doubled(rows):
    lane = lax.broadcasted_iota(jnp.int32, (1, PAIR), 1)
    first = jnp.where(lane < HDIM, 1.0, 0.0).astype(bf16)
    second = jnp.where(lane < HDIM, 0.0, 1.0).astype(bf16)
    return jnp.concatenate([rows * first, rows * second], axis=0)


def diagonal(pair):
    return jnp.concatenate([pair[:HDIM, :BLOCK], pair[HDIM:, BLOCK:]], axis=0)


def fill_mask(where, clips, mask):
    row = lax.broadcasted_iota(jnp.int32, (BLOCK, BLOCK), 0)
    lane = lax.broadcasted_iota(jnp.int32, (BLOCK, BLOCK), 1)
    older = jnp.where(row > lane, 1.0, 0.0)
    every = jnp.ones((BLOCK, BLOCK), f32)
    causal = jnp.where(row <= lane, 1.0, 0.0)
    for query_block in range(2):
        at_query = (2 + query_block) * CLIP_ROWS
        query_clip = clips[at_query : at_query + CLIP_ROWS].astype(f32)[0:1]
        for step, shape in enumerate((older, every, causal)):
            block = query_block + step
            key_clip = clips[block * CLIP_ROWS : (block + 1) * CLIP_ROWS].astype(f32)[0:1]
            same = jnp.where(key_clip == query_clip, 1.0, 0.0)
            present = jnp.where(2 * where[1] - 2 + block >= 0, 1.0, 0.0)
            mask[query_block, step * BLOCK : (step + 1) * BLOCK] = shape * same * present


def forward_kernel(
    pieces_wanted,
    where,
    own,
    partner,
    halo,
    halo_other,
    query_own,
    query_partner,
    weights_out,
    att_own,
    att_swap,
    *rest,
):
    pieces = rest[:pieces_wanted]
    att, mask, key_all, value_all, query_all, clips = rest[pieces_wanted:]
    pair = pl.program_id(0)
    half = where[0]
    for target, start in ((key_all, 0), (value_all, BLOCK)):
        gather_rows(target, half, 0, halo, halo_other, start)
        gather_rows(target, half, 2, own, partner, start)
    gather_rows(query_all, half, 0, query_own, query_partner, 0)

    @pl.when(pair == 0)
    def _():
        for offset, mine, theirs in ((0, halo, halo_other), (2, own, partner)):
            clips[at(offset + half, CLIP_ROWS)] = mine[2 * BLOCK :]
            clips[at(offset + 1 - half, CLIP_ROWS)] = theirs[2 * BLOCK :]
        fill_mask(where, clips, mask)

    for query_block in range(2):
        keys = slice(query_block * BLOCK, query_block * BLOCK + WIN + BLOCK)
        steps = slice(query_block * BLOCK, (query_block + 1) * BLOCK)
        scores = times(key_all[keys], doubled(query_all[steps]), ((1,), (1,))) * SCALING
        visible = mask[query_block]
        visible = jnp.concatenate([visible, visible], axis=1)
        scores = jnp.where(visible > 0.5, scores, big_negative)
        maximum = jnp.max(scores, axis=0, keepdims=True)
        powers = jnp.exp(scores - maximum)
        total = jnp.sum(powers, axis=0, keepdims=True)
        weights = (powers * (1.0 / total)).astype(bf16)
        weights_out[0, query_block] = weights
        mixed = times(value_all[keys], weights, ((0,), (0,)))
        att[at(pair, PAIR), steps] = diagonal(mixed).astype(bf16)

    @pl.when(pair == PAIRS - 1)
    def _():
        att_own[...] = att[:, at(half, BLOCK)]
        att_swap[...] = att[span(half * PAIR, REST, PAIR), at(1 - half, BLOCK)]
        if pieces_wanted:
            rows = pieces[0].shape[0]
            for number, piece in enumerate(pieces):
                begin = half * HDIM + rows * jnp.bitwise_xor(where[2], number)
                piece[...] = att[span(begin, rows, 16), :]


def column(rows):
    return pl.BlockSpec((rows, PAIR), lambda pair, where: (0, pair))


def shifted_column(rows):
    return pl.BlockSpec((rows, PAIR), lambda pair, where: (0, where[0] * (START // PAIR) + pair))


def whole(shape):
    return pl.BlockSpec(shape, lambda pair, where: (0,) * len(shape))


def forward(where, pieces_wanted, own, partner, halo, halo_other, query, query_partner):
    piece = (WIDTH // 2 // max(pieces_wanted, 1), 2 * BLOCK)
    return pl.pallas_call(
        functools.partial(forward_kernel, pieces_wanted),
        out_shape=(
            shaped((PAIRS, 2, WIN + BLOCK, 2 * BLOCK), bf16),
            shaped((PART, BLOCK), bf16),
            shaped((REST, BLOCK), bf16),
        )
        + (shaped(piece, bf16),) * pieces_wanted,
        grid_spec=pltpu.PrefetchScalarGridSpec(
            num_scalar_prefetch=1,
            grid=(PAIRS,),
            in_specs=[column(PAYLOAD)] * 4 + [shifted_column(BLOCK), column(BLOCK)],
            out_specs=(
                pl.BlockSpec(
                    (1, 2, WIN + BLOCK, 2 * BLOCK), lambda pair, where: (pair, 0, 0, 0)
                ),
                whole((PART, BLOCK)),
                whole((REST, BLOCK)),
            )
            + (whole(piece),) * pieces_wanted,
            scratch_shapes=[
                pltpu.VMEM((PART, 2 * BLOCK), bf16),
                pltpu.VMEM((2, WIN + BLOCK, BLOCK), f32),
                pltpu.VMEM((4 * BLOCK, PAIR), bf16),
                pltpu.VMEM((4 * BLOCK, PAIR), bf16),
                pltpu.VMEM((2 * BLOCK, PAIR), bf16),
                pltpu.VMEM((4 * CLIP_ROWS, PAIR), bf16),
            ],
        ),
        compiler_params=params(),
        cost_estimate=estimate(2_000_000_000, 6_000_000),
        name="forward",
    )(where, own, partner, halo, halo_other, query, query_partner)


def cotangent_kernel(where, own, partner, weight, d_attended, both):
    half = where[0]

    @pl.when(pl.program_id(0) == 0)
    def _():
        gather_rows(both, half, 0, own, partner, 0)

    d_attended[...] = times(both[...], weight[...], ((1,), (0,))).astype(bf16)


def cotangents(where, own, partner, weight):
    outs = own.shape[1]
    return pl.pallas_call(
        cotangent_kernel,
        out_shape=(shaped((2 * BLOCK, PART), bf16), shaped((2 * BLOCK, outs), bf16)),
        grid_spec=pltpu.PrefetchScalarGridSpec(
            num_scalar_prefetch=1,
            grid=(PAIRS,),
            in_specs=[whole((BLOCK, outs)), whole((BLOCK, outs)), shifted_column(outs)],
            out_specs=(column(2 * BLOCK), whole((2 * BLOCK, outs))),
        ),
        compiler_params=params(),
        cost_estimate=estimate(700_000_000, 3_000_000),
        name="cotangents",
    )(where, own, partner, weight)


def backward_kernel(
    where,
    own,
    partner,
    halo,
    halo_other,
    query_own,
    query_partner,
    weights_in,
    d_attended,
    dq_own,
    dq_swap,
    halo_grads,
    halo_other_grads,
    own_grads,
    partner_grads,
    key_all,
    value_all,
    query_all,
    dq_all,
    dk_all,
    dv_all,
):
    pair = pl.program_id(0)
    half = where[0]
    for target, start in ((key_all, 0), (value_all, BLOCK)):
        gather_rows(target, half, 0, halo, halo_other, start)
        gather_rows(target, half, 2, own, partner, start)
    gather_rows(query_all, half, 0, query_own, query_partner, 0)
    for query_block in range(2):
        keys = slice(query_block * BLOCK, query_block * BLOCK + WIN + BLOCK)
        steps = slice(query_block * BLOCK, (query_block + 1) * BLOCK)
        d_rows = doubled(d_attended[steps])
        query_rows = doubled(query_all[steps])
        weights = weights_in[0, query_block]
        d_weights = times(value_all[keys], d_rows, ((1,), (1,)))
        wide = weights.astype(f32)
        delta = jnp.sum(wide * d_weights, axis=0, keepdims=True)
        d_scores = (wide * (d_weights - delta) * SCALING).astype(bf16)
        dv = times(weights, d_rows, ((1,), (0,)))
        dk = times(d_scores, query_rows, ((1,), (0,)))
        dq = diagonal(times(key_all[keys], d_scores, ((0,), (0,))))
        dq_all[steps] = dq.T
        if query_block == 0:
            dk_all[: WIN + BLOCK] = dk
            dv_all[: WIN + BLOCK] = dv
        else:
            dk_all[BLOCK : WIN + BLOCK] += dk[:WIN]
            dv_all[BLOCK : WIN + BLOCK] += dv[:WIN]
            dk_all[WIN + BLOCK :] = dk[WIN:]
            dv_all[WIN + BLOCK :] = dv[WIN:]
    dq_own[...] = dq_all[at(half, BLOCK)].astype(bf16)

    @pl.when((pair >= half) & (pair - half < REST // PAIR))
    def _():
        dq_swap[...] = dq_all[at(1 - half, BLOCK)].astype(bf16)

    for start, grads in ((0, dk_all), (BLOCK, dv_all)):
        rows = slice(start, start + BLOCK)
        halo_grads[rows] = grads[at(half, BLOCK)].astype(bf16)
        halo_other_grads[rows] = grads[at(1 - half, BLOCK)].astype(bf16)
        own_grads[rows] = grads[at(2 + half, BLOCK)]
        partner_grads[rows] = grads[at(3 - half, BLOCK)]


def backward(where, own, partner, halo, halo_other, query, query_partner, weights, d_attended):
    return pl.pallas_call(
        backward_kernel,
        out_shape=(
            shaped((BLOCK, PART), bf16),
            shaped((BLOCK, REST), bf16),
            shaped((2 * BLOCK, PART), bf16),
            shaped((2 * BLOCK, PART), bf16),
            shaped((2 * BLOCK, PART), f32),
            shaped((2 * BLOCK, PART), f32),
        ),
        grid_spec=pltpu.PrefetchScalarGridSpec(
            num_scalar_prefetch=1,
            grid=(PAIRS,),
            in_specs=[column(PAYLOAD)] * 4
            + [
                shifted_column(BLOCK),
                column(BLOCK),
                pl.BlockSpec(
                    (1, 2, WIN + BLOCK, 2 * BLOCK), lambda pair, where: (pair, 0, 0, 0)
                ),
                column(2 * BLOCK),
            ],
            out_specs=(
                column(BLOCK),
                pl.BlockSpec(
                    (BLOCK, PAIR),
                    lambda pair, where: (0, jnp.clip(pair - where[0], 0, REST // PAIR - 1)),
                ),
                column(2 * BLOCK),
                column(2 * BLOCK),
                column(2 * BLOCK),
                column(2 * BLOCK),
            ),
            scratch_shapes=[
                pltpu.VMEM((4 * BLOCK, PAIR), bf16),
                pltpu.VMEM((4 * BLOCK, PAIR), bf16),
                pltpu.VMEM((2 * BLOCK, PAIR), bf16),
                pltpu.VMEM((2 * BLOCK, PAIR), f32),
                pltpu.VMEM((4 * BLOCK, PAIR), f32),
                pltpu.VMEM((4 * BLOCK, PAIR), f32),
            ],
        ),
        compiler_params=params(),
        cost_estimate=estimate(4_000_000_000, 8_000_000),
        name="backward",
    )(where, own, partner, halo, halo_other, query, query_partner, weights, d_attended)


def output_kernel(where, att_own, att_rest, weight, out, full):
    half = where[0]

    @pl.when(pl.program_id(0) == 0)
    def _():
        full[span(half * START, PART, 128)] = att_own[...]
        full[span((1 - half) * PART, REST, 128)] = att_rest[...]

    out[...] = times(weight[...], full[...], ((1,), (0,))).T.astype(bf16)


def output_rows(where, att_own, att_rest, weight):
    outs = weight.shape[0]
    rows = 256
    return pl.pallas_call(
        output_kernel,
        out_shape=(shaped((BLOCK, outs), bf16), shaped((WIDTH, BLOCK), bf16)),
        grid_spec=pltpu.PrefetchScalarGridSpec(
            num_scalar_prefetch=1,
            grid=(outs // rows,),
            in_specs=[
                whole((PART, BLOCK)),
                whole((REST, BLOCK)),
                pl.BlockSpec((rows, WIDTH), lambda step, where: (step, 0)),
            ],
            out_specs=(
                pl.BlockSpec((BLOCK, rows), lambda step, where: (0, step)),
                whole((WIDTH, BLOCK)),
            ),
        ),
        compiler_params=params(),
        cost_estimate=estimate(300_000_000, 3_000_000),
        name="output",
    )(where, att_own, att_rest, weight)


def add_partner_kernel(where, partner_grads, received, out):
    columns = span(where[0] * PAIR, REST, PAIR)
    out[...] = (partner_grads[:, columns] + received[:, columns].astype(f32)).astype(bf16)


def add_partner(where, partner_grads, received):
    return pl.pallas_call(
        add_partner_kernel,
        out_shape=shaped((2 * BLOCK, REST), bf16),
        in_specs=[SMEM, VMEM, VMEM],
        out_specs=VMEM,
        compiler_params=params(),
        cost_estimate=estimate(0, 1_000_000),
        name="add_partner",
    )(where, partner_grads, received)


def place_query_kernel(where, mine, theirs, out):
    half = where[0]
    out[:, span(half * START, PART, 128)] = mine[...]
    out[:, span((1 - half) * PART, REST, 128)] = theirs[...]


def place_query(where, mine, theirs):
    return pl.pallas_call(
        place_query_kernel,
        out_shape=shaped((BLOCK, WIDTH), bf16),
        in_specs=[SMEM, VMEM, VMEM],
        out_specs=VMEM,
        compiler_params=params(),
        cost_estimate=estimate(0, 600_000),
        name="place_query",
    )(where, mine, theirs)


def place_keys_kernel(where, mine, received, theirs, key_out, value_out):
    half = where[0]
    total = (mine[...] + received[...].astype(f32)).astype(bf16)
    for rows, out in ((slice(0, BLOCK), key_out), (slice(BLOCK, 2 * BLOCK), value_out)):
        out[:, span(half * START, PART, 128)] = total[rows]
        out[:, span((1 - half) * PART, REST, 128)] = theirs[rows]


def place_keys(where, mine, received, theirs):
    return pl.pallas_call(
        place_keys_kernel,
        out_shape=(shaped((BLOCK, WIDTH), bf16),) * 2,
        in_specs=[SMEM, VMEM, VMEM, VMEM],
        out_specs=(VMEM, VMEM),
        compiler_params=params(),
        cost_estimate=estimate(0, 2_000_000),
        name="place_keys",
    )(where, mine, received, theirs)


def weight_kernel(where, piece0, piece1, piece2, piece3, cot0, cot1, cot2, cot3, kept, *sent):
    products = None
    for piece, cot in ((piece0, cot0), (piece1, cot1), (piece2, cot2), (piece3, cot3)):
        product = times(piece[...], cot[...], ((1,), (0,)))
        products = product if products is None else products + product
    total = sent[-1]
    total[...] = products
    group = where[1]
    lanes = kept.shape[1]
    kept[...] = total[:, at(group, lanes)]
    for number, out in enumerate(sent[:-1]):
        target = jnp.bitwise_xor(group, number + 1)
        out[...] = total[:, at(target, lanes)].astype(bf16)


def weight_products(where, pieces, cots, groups):
    rows = pieces[0].shape[0]
    outs = cots[0].shape[1]
    part = (rows, outs // groups)
    return pl.pallas_call(
        weight_kernel,
        out_shape=(shaped(part, f32),) + (shaped(part, bf16),) * (groups - 1),
        in_specs=[SMEM] + [VMEM] * 8,
        out_specs=(VMEM,) * groups,
        scratch_shapes=[pltpu.VMEM((rows, outs), f32)],
        compiler_params=params(),
        cost_estimate=estimate(300_000_000, 3_000_000),
        name="weight_products",
    )(where, *pieces, *cots)


def weight_sum_kernel(where, kept, *rest):
    received, (first, second, total) = rest[:-3], rest[-3:]
    value = kept[...]
    for part in received:
        value = value + part[...].astype(f32)
    total[...] = value
    lanes = first.shape[1]
    odd = jnp.bitwise_and(where[2], 1)
    first[...] = total[:, at(odd, lanes)]
    second[...] = total[:, at(1 - odd, lanes)]


def weight_sum(where, kept, received):
    rows, lanes = kept.shape
    return pl.pallas_call(
        weight_sum_kernel,
        out_shape=(shaped((rows, lanes // 2), f32),) * 2,
        in_specs=[SMEM, VMEM] + [VMEM] * len(received),
        out_specs=(VMEM, VMEM),
        scratch_shapes=[pltpu.VMEM((rows, lanes), f32)],
        compiler_params=params(),
        cost_estimate=estimate(0, 800_000),
        name="weight_sum",
    )(where, kept, *received)


def weight_place_kernel(where, first, second, out, stacked):
    half = where[0]
    rows = first.shape[0]
    stacked[span(half * rows, rows, 16)] = first[...]
    stacked[span((1 - half) * rows, rows, 16)] = second[...]
    out[...] = stacked[...].T


def weight_place(where, first, second):
    rows, lanes = first.shape
    return pl.pallas_call(
        weight_place_kernel,
        out_shape=shaped((lanes, 2 * rows), f32),
        in_specs=[SMEM, VMEM, VMEM],
        out_specs=VMEM,
        scratch_shapes=[pltpu.VMEM((2 * rows, lanes), f32)],
        compiler_params=params(),
        cost_estimate=estimate(0, 400_000),
        name="weight_place",
    )(where, first, second)


def swapped(value, axis, bits):
    count = lax.axis_size(axis)
    return lax.ppermute(value, axis, [(source, source ^ bits) for source in range(count)])


def moved(value, axis, steps):
    count = lax.axis_size(axis)
    first, last = (max(0, -steps), min(count, count - steps))
    return lax.ppermute(value, axis, [(source, source + steps) for source in range(first, last)])


def placed(value, flip):
    lanes = lax.axis_size("ctx")
    moves = []
    for source in range(lax.axis_size("dp")):
        for index in range(lanes):
            group, half = index // 2, index % 2
            target_half = (source % 2) ^ flip
            target = 2 * half + source // 2
            moves.append((source * lanes + index, target * lanes + 2 * group + target_half))
    return lax.ppermute(value, ("dp", "ctx"), moves)


def per_device(queries, key_states, value_states, out_cotangent, out_weight, block_clip):
    sequences = lax.axis_size("dp")
    groups = lax.axis_size("ctx") // 2
    short = sequences == 4 and groups in (2, 4)
    index = lax.axis_index("ctx")
    where = jnp.stack([index % 2, index // 2, lax.axis_index("dp")]).astype(jnp.int32)
    query, cotangent = queries[0], out_cotangent[0]

    swap_kv, own, swap_query = pack(where, block_clip, query, key_states[0], value_states[0])
    partner = swapped(swap_kv, "ctx", 1)
    halo = moved(own, "ctx", 2)
    cot_partner = swapped(cotangent, "ctx", 1)
    halo_other = moved(partner, "ctx", 2)
    query_partner = swapped(swap_query, "ctx", 1)
    d_attended, cot_pair = cotangents(where, cotangent, cot_partner, out_weight)
    sources = (own, partner, halo, halo_other, query, query_partner)

    weights, att_own, att_swap, *pieces = forward(where, 4 if short else 0, *sources)
    if short:
        cot_y = swapped(cot_pair, "dp", 2)
        cots = (cot_pair, swapped(cot_pair, "dp", 1), cot_y, swapped(cot_y, "dp", 1))
        received = [pieces[0]] + [swapped(pieces[n], "dp", n) for n in (1, 2, 3)]
    att_rest = swapped(att_swap, "ctx", 1)
    dq_own, dq_swap, halo_grads, halo_other_grads, own_grads, partner_grads = backward(
        where, *sources, weights, d_attended
    )
    partner_late = moved(halo_other_grads, "ctx", -2)
    own_late = moved(halo_grads, "ctx", -2)
    dq_rest = swapped(dq_swap, "ctx", 1)
    sublayer_out, att_full = output_rows(where, att_own, att_rest, out_weight)
    if short:
        kept, *sent = weight_products(where, received, cots, groups)
        arrived = [swapped(part, "ctx", 2 * (n + 1)) for n, part in enumerate(sent)]
        first, second = weight_sum(where, kept, arrived)
        weight_grad = weight_place(where, placed(first, 0), placed(second, 1))
    else:
        product = lax.dot_general(
            cotangent, att_full, (((0,), (1,)), ((), ())), preferred_element_type=f32
        ).astype(bf16)
        sequence_grad = lax.psum_scatter(product, "ctx", scatter_dimension=0, tiled=True)
        weight_grad = lax.psum_scatter(
            sequence_grad.astype(f32), "dp", scatter_dimension=1, tiled=True
        )
    query_grad = place_query(where, dq_own, dq_rest)
    kv_rest = swapped(add_partner(where, partner_grads, partner_late), "ctx", 1)
    key_grad, value_grad = place_keys(where, own_grads, own_late, kv_rest)
    return (
        sublayer_out[None],
        query_grad[None],
        key_grad[None],
        value_grad[None],
        weight_grad,
    )


def solution(mesh):
    return jax.shard_map(
        per_device,
        mesh=mesh,
        in_specs=(
            P("dp", "ctx", None),
            P("dp", "ctx", None),
            P("dp", "ctx", None),
            P("dp", "ctx", None),
            P(),
            P("dp", "ctx"),
        ),
        out_specs=(
            P("dp", "ctx", None),
            P("dp", "ctx", None),
            P("dp", "ctx", None),
            P("dp", "ctx", None),
            P("ctx", "dp"),
        ),
        check_vma=False,
    )
```

```python
import functools
import math

import jax
import jax.numpy as jnp
from jax import lax
from jax.experimental import pallas as pl
from jax.experimental.pallas import tpu as pltpu
from jax.sharding import PartitionSpec as P

HEADS = 18
HDIM = 64
BLOCK = 128
WIN = 256
PAIR = 2 * HDIM
WIDTH = HEADS * HDIM
PAIRS = (HEADS + 2) // 4
PART = PAIRS * PAIR
START = WIDTH - PART
REST = WIDTH - PART
CLIP_ROWS = 16
CHUNKS = 4
DELTA_ROWS = (2 * PAIRS + 7) // 8 * 8
PAYLOAD = 2 * BLOCK + CLIP_ROWS
SCALING = 1.0 / math.sqrt(HDIM)
VMEM_LIMIT = 24 * 1024 * 1024

big_negative = -1e30
bf16 = jnp.bfloat16
f32 = jnp.float32

SMEM = pl.BlockSpec(memory_space=pltpu.SMEM)
VMEM = pl.BlockSpec(memory_space=pltpu.VMEM)
HBM = pl.BlockSpec(memory_space=pltpu.HBM)


def shaped(shape, dtype):
    return jax.ShapeDtypeStruct(shape, dtype)


def estimate(flops, moved):
    return pl.CostEstimate(flops=flops, bytes_accessed=moved, transcendentals=0)


def params():
    return pltpu.CompilerParams(vmem_limit_bytes=VMEM_LIMIT)


def in_hbm(value):
    return pltpu.with_memory_space_constraint(value, pltpu.HBM)


def my_half():
    return jnp.bitwise_and(lax.axis_index("ctx"), 1)


def my_group():
    return jnp.right_shift(lax.axis_index("ctx"), 1)


def at(index, size):
    return pl.ds(pl.multiple_of(index * size, size), size)


def span(start, size, unit):
    return pl.ds(pl.multiple_of(start, unit), size)


def times(a, b, dims):
    return lax.dot_general(a, b, (dims, ((), ())), preferred_element_type=f32)


def pack_kernel(clip, query, key, value, swap_kv, own_kv, swap_query, query_kept, sems):
    half = my_half()
    mine = span(half * START, PART, 128)
    other = span((1 - half) * START, PART, 128)
    first, second = pl.ds(0, BLOCK), pl.ds(BLOCK, BLOCK)
    copies = [
        pltpu.make_async_copy(source.at[:, columns], target, sems.at[number])
        for number, (source, columns, target) in enumerate(
            (
                (key, other, swap_kv.at[first]),
                (value, other, swap_kv.at[second]),
                (key, mine, own_kv.at[first]),
                (value, mine, own_kv.at[second]),
                (query, other, swap_query),
                (query, mine, query_kept),
            )
        )
    ]
    for copy in copies:
        copy.start()
    clip_rows = jnp.full((CLIP_ROWS, PART), clip[0, 0].astype(f32), f32).astype(bf16)
    swap_kv[2 * BLOCK :] = clip_rows
    own_kv[2 * BLOCK :] = clip_rows
    for copy in copies:
        copy.wait()


def pack(clip, query, key, value):
    return pl.pallas_call(
        pack_kernel,
        out_shape=(
            shaped((PAYLOAD, PART), bf16),
            shaped((PAYLOAD, PART), bf16),
            shaped((BLOCK, PART), bf16),
            shaped((BLOCK, PART), bf16),
        ),
        in_specs=[SMEM, HBM, HBM, HBM],
        out_specs=(VMEM,) * 4,
        scratch_shapes=[pltpu.SemaphoreType.DMA((6,))],
        compiler_params=params(),
        cost_estimate=estimate(1_000_000, 10_000),
        name="pack",
    )(clip, in_hbm(query), in_hbm(key), in_hbm(value))


def gather_rows(target, half, offset, own, partner, start=0):
    target[at(offset + half, BLOCK)] = own[start : start + BLOCK]
    target[at(offset + 1 - half, BLOCK)] = partner[start : start + BLOCK]


def doubled(rows, factor=1.0):
    lane = lax.broadcasted_iota(jnp.int32, (1, PAIR), 1)
    first = jnp.where(lane < HDIM, factor, 0.0).astype(bf16)
    second = jnp.where(lane < HDIM, 0.0, factor).astype(bf16)
    return jnp.concatenate([rows * first, rows * second], axis=0)


def diagonal(pair):
    return jnp.concatenate([pair[:HDIM, :BLOCK], pair[HDIM:, BLOCK:]], axis=0)


def fill_mask(clips, mask):
    row = lax.broadcasted_iota(jnp.int32, (BLOCK, BLOCK), 0)
    lane = lax.broadcasted_iota(jnp.int32, (BLOCK, BLOCK), 1)
    older = jnp.where(row > lane, 1.0, 0.0)
    every = jnp.ones((BLOCK, BLOCK), f32)
    causal = jnp.where(row <= lane, 1.0, 0.0)
    for query_block in range(2):
        at_query = (2 + query_block) * CLIP_ROWS
        query_clip = clips[at_query : at_query + CLIP_ROWS].astype(f32)[0:1]
        for step, shape in enumerate((older, every, causal)):
            block = query_block + step
            key_clip = clips[block * CLIP_ROWS : (block + 1) * CLIP_ROWS].astype(f32)[0:1]
            same = jnp.where(key_clip == query_clip, 1.0, 0.0)
            present = jnp.where(2 * my_group() - 2 + block >= 0, 1.0, 0.0)
            mask[query_block, step * BLOCK : (step + 1) * BLOCK] = shape * same * present


def forward_kernel(
    pieces_wanted,
    own,
    partner,
    halo,
    halo_other,
    query_own,
    query_partner,
    d_turned_own,
    d_turned_partner,
    weights_out,
    delta_out,
    att_own,
    att_swap,
    *rest,
):
    pieces = rest[:pieces_wanted]
    att, mask, key_all, value_all, query_all, clips, d_turned = rest[pieces_wanted:]
    half = my_half()
    for target, start in ((key_all, 0), (value_all, BLOCK)):
        gather_rows(target, half, 0, halo, halo_other, start)
        gather_rows(target, half, 2, own, partner, start)
    gather_rows(query_all, half, 0, query_own, query_partner)
    d_turned[:, at(half, BLOCK)] = d_turned_own[...]
    d_turned[:, at(1 - half, BLOCK)] = d_turned_partner[...]
    for offset, mine, theirs in ((0, halo, halo_other), (2, own, partner)):
        clips[at(offset + half, CLIP_ROWS)] = mine[2 * BLOCK :, :PAIR]
        clips[at(offset + 1 - half, CLIP_ROWS)] = theirs[2 * BLOCK :, :PAIR]
    fill_mask(clips, mask)

    for pair in range(PAIRS):
        columns = slice(pair * PAIR, (pair + 1) * PAIR)
        for query_block in range(2):
            keys = slice(query_block * BLOCK, query_block * BLOCK + WIN + BLOCK)
            steps = slice(query_block * BLOCK, (query_block + 1) * BLOCK)
            query_rows = doubled(query_all[steps, columns], SCALING)
            scores = times(key_all[keys, columns], query_rows, ((1,), (1,)))
            visible = mask[query_block]
            visible = jnp.concatenate([visible, visible], axis=1)
            scores = jnp.where(visible > 0.5, scores, big_negative)
            maximum = jnp.max(scores, axis=0, keepdims=True)
            powers = jnp.exp(scores - maximum)
            total = jnp.sum(powers, axis=0, keepdims=True)
            weights = (powers * (1.0 / total)).astype(bf16)
            weights_out[pair, query_block] = weights
            mixed = times(value_all[keys, columns], weights, ((0,), (0,)))
            attended = diagonal(mixed).astype(bf16)
            att[columns, steps] = attended
            dots = d_turned[columns, steps].astype(f32) * attended.astype(f32)
            number = 2 * pair + query_block
            delta_out[number : number + 1, :BLOCK] = jnp.sum(dots[:HDIM], axis=0, keepdims=True)
            delta_out[number : number + 1, BLOCK:] = jnp.sum(dots[HDIM:], axis=0, keepdims=True)

    att_own[...] = att[:, at(half, BLOCK)]
    att_swap[...] = att[span(half * PAIR, REST, PAIR), at(1 - half, BLOCK)]
    if pieces_wanted:
        rows = pieces[0].shape[0]
        for number, piece in enumerate(pieces):
            begin = half * HDIM + rows * jnp.bitwise_xor(lax.axis_index("dp"), number)
            piece[...] = att[span(begin, rows, 16), :]


def forward(pieces_wanted, *sources):
    piece = (WIDTH // 2 // max(pieces_wanted, 1), 2 * BLOCK)
    return pl.pallas_call(
        functools.partial(forward_kernel, pieces_wanted),
        out_shape=(
            shaped((PAIRS, 2, WIN + BLOCK, 2 * BLOCK), bf16),
            shaped((DELTA_ROWS, 2 * BLOCK), f32),
            shaped((PART, BLOCK), bf16),
            shaped((REST, BLOCK), bf16),
        )
        + (shaped(piece, bf16),) * pieces_wanted,
        in_specs=[VMEM] * 8,
        out_specs=(VMEM,) * (4 + pieces_wanted),
        scratch_shapes=[
            pltpu.VMEM((PART, 2 * BLOCK), bf16),
            pltpu.VMEM((2, WIN + BLOCK, BLOCK), f32),
            pltpu.VMEM((4 * BLOCK, PART), bf16),
            pltpu.VMEM((4 * BLOCK, PART), bf16),
            pltpu.VMEM((2 * BLOCK, PART), bf16),
            pltpu.VMEM((4 * CLIP_ROWS, PAIR), bf16),
            pltpu.VMEM((PART, 2 * BLOCK), bf16),
        ],
        compiler_params=params(),
        cost_estimate=estimate(1_000_000, 10_000),
        name="forward",
    )(*sources)


def own_cotangent_kernel(cotangent, weight, d_attended, d_turned, kept, rows, sems):
    chunk = rows.shape[1] // CHUNKS
    copies = [pltpu.make_async_copy(cotangent, rows, sems.at[CHUNKS])]
    for number in range(CHUNKS):
        part = pl.ds(number * chunk, chunk)
        copies.append(pltpu.make_async_copy(weight.at[part], kept.at[part], sems.at[number]))
    for copy in copies:
        copy.start()
    copies[0].wait()
    mine = span(my_half() * START, PART, 128)
    value = None
    for number in range(CHUNKS):
        copies[number + 1].wait()
        part = slice(number * chunk, (number + 1) * chunk)
        product = times(rows[:, part], kept[part, mine], ((1,), (0,)))
        value = product if value is None else value + product
    value = value.astype(bf16)
    d_attended[...] = value
    d_turned[...] = value.T


def own_cotangents(cotangent, weight):
    return pl.pallas_call(
        own_cotangent_kernel,
        out_shape=(
            shaped((BLOCK, PART), bf16),
            shaped((PART, BLOCK), bf16),
            shaped(weight.shape, bf16),
        ),
        in_specs=[HBM, HBM],
        out_specs=(VMEM,) * 3,
        scratch_shapes=[
            pltpu.VMEM(cotangent.shape, bf16),
            pltpu.SemaphoreType.DMA((CHUNKS + 1,)),
        ],
        compiler_params=params(),
        cost_estimate=estimate(1_000_000, 10_000),
        name="own_cotangents",
    )(in_hbm(cotangent), in_hbm(weight))


def cotangent_kernel(cotangent, weight, d_attended, d_turned):
    mine = span(my_half() * START, PART, 128)
    value = times(cotangent[...], weight[:, mine], ((1,), (0,))).astype(bf16)
    d_attended[...] = value
    d_turned[...] = value.T


def cotangents(cotangent, weight):
    return pl.pallas_call(
        cotangent_kernel,
        out_shape=(shaped((BLOCK, PART), bf16), shaped((PART, BLOCK), bf16)),
        in_specs=[VMEM, VMEM],
        out_specs=(VMEM,) * 2,
        compiler_params=params(),
        cost_estimate=estimate(1_000_000, 10_000),
        name="cotangents",
    )(cotangent, weight)


def halo_kernel(
    halo,
    halo_other,
    query_own,
    query_partner,
    d_own,
    d_partner,
    weights_in,
    delta_in,
    halo_grads,
    halo_other_grads,
    dq_part,
    key_all,
    value_all,
    query_all,
    d_all,
    dk_all,
    dv_all,
):
    half = my_half()
    gather_rows(key_all, half, 0, halo, halo_other)
    gather_rows(value_all, half, 0, halo, halo_other, BLOCK)
    gather_rows(query_all, half, 0, query_own, query_partner)
    gather_rows(d_all, half, 0, d_own, d_partner)
    for pair in range(PAIRS):
        columns = slice(pair * PAIR, (pair + 1) * PAIR)
        for query_block in range(2):
            keys = slice(query_block * BLOCK, WIN)
            steps = slice(query_block * BLOCK, (query_block + 1) * BLOCK)
            weights = weights_in[pair, query_block, : WIN - query_block * BLOCK]
            delta = delta_in[2 * pair + query_block : 2 * pair + query_block + 1]
            dq, dk, dv = gradients(
                key_all[keys, columns],
                value_all[keys, columns],
                query_all[steps, columns],
                d_all[steps, columns],
                weights,
                delta,
            )
            dq_part[columns, steps] = dq
            if query_block == 0:
                dk_all[:, columns] = dk
                dv_all[:, columns] = dv
            else:
                dk_all[BLOCK:, columns] += dk
                dv_all[BLOCK:, columns] += dv
    for start, grads in ((0, dk_all), (BLOCK, dv_all)):
        rows = slice(start, start + BLOCK)
        halo_grads[rows] = grads[at(half, BLOCK)].astype(bf16)
        halo_other_grads[rows] = grads[at(1 - half, BLOCK)].astype(bf16)


def gradients(keys, values, query_rows, d_rows, weights, delta):
    d_rows = doubled(d_rows)
    d_weights = times(values, d_rows, ((1,), (1,)))
    d_scores = (weights.astype(f32) * (d_weights - delta)).astype(bf16)
    dv = times(weights, d_rows, ((1,), (0,)))
    dk = times(d_scores, doubled(query_rows, SCALING), ((1,), (0,)))
    dq = diagonal(times(keys, d_scores, ((0,), (0,))))
    return dq, dk, dv


def halo_gradients(*sources):
    return pl.pallas_call(
        halo_kernel,
        out_shape=(
            shaped((2 * BLOCK, PART), bf16),
            shaped((2 * BLOCK, PART), bf16),
            shaped((PART, 2 * BLOCK), f32),
        ),
        in_specs=[VMEM] * 8,
        out_specs=(VMEM,) * 3,
        scratch_shapes=[pltpu.VMEM((2 * BLOCK, PART), bf16)] * 4
        + [pltpu.VMEM((2 * BLOCK, PART), f32)] * 2,
        compiler_params=params(),
        cost_estimate=estimate(1_000_000, 10_000),
        name="halo_gradients",
    )(*sources)


def own_kernel(
    own,
    partner,
    query_own,
    query_partner,
    d_own,
    d_partner,
    weights_in,
    delta_in,
    dq_part,
    att_swap,
    dq_own,
    swap,
    own_grads,
    partner_grads,
    key_all,
    value_all,
    query_all,
    d_all,
    dq_all,
    dk_all,
    dv_all,
):
    half = my_half()
    gather_rows(key_all, half, 0, own, partner)
    gather_rows(value_all, half, 0, own, partner, BLOCK)
    gather_rows(query_all, half, 0, query_own, query_partner)
    gather_rows(d_all, half, 0, d_own, d_partner)
    for pair in range(PAIRS):
        columns = slice(pair * PAIR, (pair + 1) * PAIR)
        for query_block in (1, 0):
            keys = slice(0, (query_block + 1) * BLOCK)
            steps = slice(query_block * BLOCK, (query_block + 1) * BLOCK)
            weights = weights_in[pair, query_block, WIN - query_block * BLOCK :]
            delta = delta_in[2 * pair + query_block : 2 * pair + query_block + 1]
            dq, dk, dv = gradients(
                key_all[keys, columns],
                value_all[keys, columns],
                query_all[steps, columns],
                d_all[steps, columns],
                weights,
                delta,
            )
            dq = dq + dq_part[columns, steps]
            dq_all[columns, steps] = (dq * SCALING).astype(bf16)
            if query_block == 1:
                dk_all[:, columns] = dk
                dv_all[:, columns] = dv
            else:
                dk_all[:BLOCK, columns] += dk
                dv_all[:BLOCK, columns] += dv
    dq_own[...] = dq_all[:, at(half, BLOCK)].T
    swap[:, :BLOCK] = att_swap[...]
    swap[:, BLOCK:] = dq_all[span(half * PAIR, REST, PAIR), at(1 - half, BLOCK)]
    for start, grads in ((0, dk_all), (BLOCK, dv_all)):
        rows = slice(start, start + BLOCK)
        own_grads[rows] = grads[at(half, BLOCK)]
        partner_grads[rows] = grads[at(1 - half, BLOCK)]


def own_gradients(*sources):
    return pl.pallas_call(
        own_kernel,
        out_shape=(
            shaped((BLOCK, PART), bf16),
            shaped((REST, 2 * BLOCK), bf16),
            shaped((2 * BLOCK, PART), f32),
            shaped((2 * BLOCK, PART), f32),
        ),
        in_specs=[VMEM] * 10,
        out_specs=(VMEM,) * 4,
        scratch_shapes=[pltpu.VMEM((2 * BLOCK, PART), bf16)] * 4
        + [pltpu.VMEM((PART, 2 * BLOCK), bf16)]
        + [pltpu.VMEM((2 * BLOCK, PART), f32)] * 2,
        compiler_params=params(),
        cost_estimate=estimate(1_000_000, 10_000),
        name="own_gradients",
    )(*sources)


def output_kernel(att_own, received, weight, out, full, dq_rest):
    half = my_half()
    full[span(half * START, PART, 128)] = att_own[...]
    full[span((1 - half) * PART, REST, 128)] = received[:, :BLOCK]
    out[...] = times(weight[...], full[...], ((1,), (0,))).T.astype(bf16)
    dq_rest[...] = received[:, BLOCK:].T


def output_rows(att_own, received, weight):
    outs = weight.shape[0]
    return pl.pallas_call(
        output_kernel,
        out_shape=(
            shaped((BLOCK, outs), bf16),
            shaped((WIDTH, BLOCK), bf16),
            shaped((BLOCK, REST), bf16),
        ),
        in_specs=[VMEM] * 3,
        out_specs=(VMEM,) * 3,
        compiler_params=params(),
        cost_estimate=estimate(1_000_000, 10_000),
        name="output",
    )(att_own, received, weight)


def add_partner_kernel(partner_grads, received, out):
    columns = span(my_half() * PAIR, REST, PAIR)
    out[...] = (partner_grads[:, columns] + received[:, columns].astype(f32)).astype(bf16)


def add_partner(partner_grads, received):
    return pl.pallas_call(
        add_partner_kernel,
        out_shape=shaped((2 * BLOCK, REST), bf16),
        in_specs=[VMEM, VMEM],
        out_specs=VMEM,
        compiler_params=params(),
        cost_estimate=estimate(1_000_000, 10_000),
        name="add_partner",
    )(partner_grads, received)


def weight_kernel(count, *refs):
    pieces, cots = refs[:count], refs[count : 3 * count]
    kept, *sent = refs[3 * count :]
    total = sent.pop()
    half = my_half()
    products = None
    for piece, first, second in zip(pieces, cots[:count], cots[count:]):
        att = jnp.concatenate([piece[:, at(half, BLOCK)], piece[:, at(1 - half, BLOCK)]], axis=1)
        product = times(att, jnp.concatenate([first[...], second[...]], axis=0), ((1,), (0,)))
        products = product if products is None else products + product
    total[...] = products
    group = my_group()
    lanes = kept.shape[1]
    kept[...] = total[:, at(group, lanes)]
    for number, out in enumerate(sent):
        target = jnp.bitwise_xor(group, number + 1)
        out[...] = total[:, at(target, lanes)].astype(bf16)


def weight_products(pieces, cots, groups):
    rows = pieces[0].shape[0]
    outs = cots[0].shape[1]
    part = (rows, outs // groups)
    return pl.pallas_call(
        functools.partial(weight_kernel, len(pieces)),
        out_shape=(shaped(part, f32),) + (shaped(part, bf16),) * (groups - 1),
        in_specs=[VMEM] * (3 * len(pieces)),
        out_specs=(VMEM,) * groups,
        scratch_shapes=[pltpu.VMEM((rows, outs), f32)],
        compiler_params=params(),
        cost_estimate=estimate(1_000_000, 10_000),
        name="weight_products",
    )(*pieces, *cots)


def weight_sum_kernel(kept, *rest):
    received, (first, second, total) = rest[:-3], rest[-3:]
    value = kept[...]
    for part in received:
        value = value + part[...].astype(f32)
    total[...] = value
    lanes = first.shape[1]
    odd = jnp.bitwise_and(lax.axis_index("dp"), 1)
    first[...] = total[:, at(odd, lanes)]
    second[...] = total[:, at(1 - odd, lanes)]


def weight_sum(kept, received):
    rows, lanes = kept.shape
    return pl.pallas_call(
        weight_sum_kernel,
        out_shape=(shaped((rows, lanes // 2), f32),) * 2,
        in_specs=[VMEM] + [VMEM] * len(received),
        out_specs=(VMEM, VMEM),
        scratch_shapes=[pltpu.VMEM((rows, lanes), f32)],
        compiler_params=params(),
        cost_estimate=estimate(1_000_000, 10_000),
        name="weight_sum",
    )(kept, *received)


def place_kernel(
    dq_mine,
    dq_theirs,
    mine,
    received,
    theirs,
    first,
    second,
    query_out,
    key_out,
    value_out,
    weight_out,
    total,
    sems,
):
    half = my_half()
    rows = first.shape[0]
    left, right = span(half * START, PART, 128), span((1 - half) * PART, REST, 128)
    upper, lower = pl.ds(0, BLOCK), pl.ds(BLOCK, BLOCK)
    moves = [
        (first, weight_out.at[span(half * rows, rows, 16)]),
        (second, weight_out.at[span((1 - half) * rows, rows, 16)]),
        (dq_mine, query_out.at[:, left]),
        (dq_theirs, query_out.at[:, right]),
        (theirs.at[upper], key_out.at[:, right]),
        (theirs.at[lower], value_out.at[:, right]),
        (total.at[upper], key_out.at[:, left]),
        (total.at[lower], value_out.at[:, left]),
    ]
    copies = [
        pltpu.make_async_copy(source, target, sems.at[number])
        for number, (source, target) in enumerate(moves)
    ]
    for copy in copies[:6]:
        copy.start()
    total[...] = (mine[...] + received[...].astype(f32)).astype(bf16)
    for copy in copies[6:]:
        copy.start()
    for copy in copies:
        copy.wait()


def place(*sources):
    rows, lanes = sources[-1].shape
    *grads, weight = pl.pallas_call(
        place_kernel,
        out_shape=(shaped((BLOCK, WIDTH), bf16),) * 3 + (shaped((2 * rows, lanes), f32),),
        in_specs=[VMEM] * 7,
        out_specs=(HBM,) * 4,
        scratch_shapes=[
            pltpu.VMEM((2 * BLOCK, PART), bf16),
            pltpu.SemaphoreType.DMA((8,)),
        ],
        compiler_params=params(),
        cost_estimate=estimate(1_000_000, 10_000),
        name="place",
    )(*sources)
    return *grads, weight.T


def swapped(value, axis, bits):
    count = lax.axis_size(axis)
    return lax.ppermute(value, axis, [(source, source ^ bits) for source in range(count)])


def moved(value, axis, steps):
    count = lax.axis_size(axis)
    first, last = (max(0, -steps), min(count, count - steps))
    return lax.ppermute(value, axis, [(source, source + steps) for source in range(first, last)])


def placed(value, flip):
    lanes = lax.axis_size("ctx")
    moves = []
    for source in range(lax.axis_size("dp")):
        for index in range(lanes):
            group, half = index // 2, index % 2
            target_half = (source % 2) ^ flip
            target = 2 * half + source // 2
            moves.append((source * lanes + index, target * lanes + 2 * group + target_half))
    return lax.ppermute(value, ("dp", "ctx"), moves)


def after(*values):
    return lax.optimization_barrier(values)


def per_device(queries, key_states, value_states, out_cotangent, out_weight, block_clip):
    sequences = lax.axis_size("dp")
    groups = lax.axis_size("ctx") // 2
    short = sequences == 4 and groups in (2, 4)
    query, cotangent = queries[0], out_cotangent[0]

    swap_kv, own, swap_query, query = pack(block_clip, query, key_states[0], value_states[0])
    partner = swapped(swap_kv, "ctx", 1)
    halo = moved(own, "ctx", 2)
    d_own, d_turned_own, weight = own_cotangents(cotangent, out_weight)
    cots, later = [cotangent], []
    if short:
        cots += [swapped(cotangent, "dp", n) for n in (1, 2)]
    partner, halo, d_own, swap_query, cot_late = after(
        partner, halo, d_own, swap_query, cotangent
    )

    halo_other = moved(partner, "ctx", 2)
    cot_partner = swapped(cot_late, "ctx", 1)
    query_partner = swapped(swap_query, "ctx", 1)
    if short:
        cots.append(swapped(cots[2], "dp", 1))
    d_partner, d_turned_partner = cotangents(cot_partner, weight)
    halo_other, query_partner, d_partner, cot_partner, *cots = after(
        halo_other, query_partner, d_partner, cot_partner, *cots
    )

    if short:
        later = [cot_partner, swapped(cot_partner, "dp", 2)]
    queries_pair, d_pair = (query, query_partner), (d_own, d_partner)
    weights, delta, att_own, att_swap, *pieces = forward(
        4 if short else 0,
        own,
        partner,
        halo,
        halo_other,
        *queries_pair,
        d_turned_own,
        d_turned_partner,
    )
    delta, *rest = after(delta, *pieces, *later)
    pieces, later = rest[: len(pieces)], rest[len(pieces) :]

    if short:
        pieces[1:] = [swapped(pieces[n], "dp", n) for n in (1, 2, 3)]
        later.insert(1, swapped(later[0], "dp", 1))
        later.append(swapped(later[2], "dp", 1))
    halo_grads, halo_other_grads, dq_part = halo_gradients(
        halo, halo_other, *queries_pair, *d_pair, weights, delta
    )
    halo_grads, halo_other_grads, dq_part, *pieces = after(
        halo_grads, halo_other_grads, dq_part, *pieces
    )

    partner_late = moved(halo_other_grads, "ctx", -2)
    own_late = moved(halo_grads, "ctx", -2)
    if short:
        kept, *sent = weight_products(pieces, [*cots, *later], groups)
        arrived = [swapped(part, "ctx", 2 * (n + 1)) for n, part in enumerate(sent)]
        kept, dq_part = after(kept, dq_part)
    dq_own, swap, own_grads, partner_grads = own_gradients(
        own, partner, *queries_pair, *d_pair, weights, delta, dq_part, att_swap
    )
    received = swapped(swap, "ctx", 1)
    if short:
        partner_late, dq_own, kept, *arrived = after(partner_late, dq_own, kept, *arrived)
        first, second = weight_sum(kept, arrived)
        first, second = placed(first, 0), placed(second, 1)
    kv_rest = swapped(add_partner(partner_grads, partner_late), "ctx", 1)
    sublayer_out, att_full, dq_rest = output_rows(att_own, received, weight)
    if not short:
        product = lax.dot_general(
            cotangent, att_full, (((0,), (1,)), ((), ())), preferred_element_type=f32
        ).astype(bf16)
        sequence_grad = lax.psum_scatter(product, "ctx", scatter_dimension=0, tiled=True)
        weight_grad = lax.psum_scatter(
            sequence_grad.astype(f32), "dp", scatter_dimension=1, tiled=True
        )
        first = second = jnp.zeros((16, 128), f32)
    query_grad, key_grad, value_grad, placed_weight = place(
        dq_own, dq_rest, own_grads, own_late, kv_rest, first, second
    )
    if short:
        weight_grad = placed_weight
    return (
        sublayer_out[None],
        query_grad[None],
        key_grad[None],
        value_grad[None],
        weight_grad,
    )


def solution(mesh):
    return jax.shard_map(
        per_device,
        mesh=mesh,
        in_specs=(
            P("dp", "ctx", None),
            P("dp", "ctx", None),
            P("dp", "ctx", None),
            P("dp", "ctx", None),
            P(),
            P("dp", "ctx"),
        ),
        out_specs=(
            P("dp", "ctx", None),
            P("dp", "ctx", None),
            P("dp", "ctx", None),
            P("dp", "ctx", None),
            P("ctx", "dp"),
        ),
        check_vma=False,
    )
```

```python
import functools
import math

import jax
import jax.numpy as jnp
from jax import lax
from jax.experimental import pallas as pl
from jax.experimental.pallas import tpu as pltpu
from jax.sharding import PartitionSpec as P

HEADS = 18
HDIM = 64
BLOCK = 128
WIN = 256
PAIR = 2 * HDIM
WIDTH = HEADS * HDIM
HALF = WIDTH // 2
PAIRS = HEADS // 4
SHARED = PAIRS * PAIR
MIXED = 2 * PAIRS
ROWS = (MIXED + 1) * BLOCK
CLIP_ROWS = 16
CLIP_STAT = 2 * PAIRS + 2
DELTA_STAT = CLIP_STAT + 2
STAT_ROWS = 24
SENT_ROWS = ROWS + 6 * STAT_ROWS
CHUNKS = 4
SCALING = 1.0 / math.sqrt(HDIM)
COST_GATHER = 2_000_000_000
COST_KEYS = 1_000_000
COST_FIRST = 2_000_000_000
COST_SUM = 2_000_000_000
VMEM_LIMIT = 24 * 1024 * 1024

big_negative = -1e30
bf16 = jnp.bfloat16
f32 = jnp.float32

SMEM = pl.BlockSpec(memory_space=pltpu.SMEM)
VMEM = pl.BlockSpec(memory_space=pltpu.VMEM)
HBM = pl.BlockSpec(memory_space=pltpu.HBM)


def shaped(shape, dtype):
    return jax.ShapeDtypeStruct(shape, dtype)


def kernel(body, name, ins, outs, scratch=(), out_space=VMEM, flops=1_000_000):
    return pl.pallas_call(
        body,
        out_shape=tuple(outs),
        in_specs=list(ins),
        out_specs=(out_space,) * len(outs),
        scratch_shapes=list(scratch),
        compiler_params=pltpu.CompilerParams(vmem_limit_bytes=VMEM_LIMIT),
        cost_estimate=pl.CostEstimate(flops=flops, bytes_accessed=10_000, transcendentals=0),
        name=name,
    )


def in_hbm(value):
    return pltpu.with_memory_space_constraint(value, pltpu.HBM)


def my_half():
    return jnp.bitwise_and(lax.axis_index("ctx"), 1)


def my_group():
    return jnp.right_shift(lax.axis_index("ctx"), 1)


def at(index, size):
    return pl.ds(pl.multiple_of(index * size, size), size)


def span(start, size, unit):
    return pl.ds(pl.multiple_of(start, unit), size)


def rows_of(block):
    return slice(block * BLOCK, (block + 1) * BLOCK)


def columns_of(half, pair):
    return span(half * (SHARED + PAIR) + pair * PAIR, PAIR, PAIR)


def head_rows(half, pair):
    return span(half * HDIM + pair * PAIR, PAIR, HDIM)


def single_rows(half):
    return span((1 - half) * SHARED, HDIM, HDIM)


def times(a, b, dims):
    return lax.dot_general(a, b, (dims, ((), ())), preferred_element_type=f32)


def is_low():
    return lax.broadcasted_iota(jnp.int32, (1, PAIR), 1) < HDIM


def low_or_high(low_value, high_value):
    return jnp.where(is_low(), low_value, high_value)


def turned(value):
    return pltpu.roll(value, HDIM, 1)


def pack_kernel(clip, query, key, value, swap_kv, own_kv, swap_query, own_query, *scratch):
    query_all, key_all, value_all, mixed, single, sems = scratch
    half = my_half()
    pairs = ((key, key_all), (value, value_all), (query, query_all))
    copies = [pltpu.make_async_copy(a, b, sems.at[n]) for n, (a, b) in enumerate(pairs)]
    for copy in copies:
        copy.start()
    clip_rows = jnp.full((CLIP_ROWS, PAIR), clip[0, 0].astype(f32), f32).astype(bf16)
    shared = slice(SHARED, SHARED + PAIR)
    for copy in copies:
        copy.wait()
    for side, target in ((1 - half, swap_kv), (half, own_kv)):
        for pair in range(PAIRS):
            target[rows_of(pair)] = key_all[:, columns_of(side, pair)]
            target[rows_of(PAIRS + pair)] = value_all[:, columns_of(side, pair)]
        target[ROWS:] = clip_rows
    key_shared = key_all[:, shared].astype(f32)
    value_shared = value_all[:, shared].astype(f32)
    mixed[0] = low_or_high(key_shared, turned(value_shared)).astype(bf16)
    mixed[1] = low_or_high(turned(key_shared), value_shared).astype(bf16)
    swap_kv[rows_of(MIXED)] = mixed[1 - half]
    own_kv[rows_of(MIXED)] = mixed[half]
    for pair in range(PAIRS):
        swap_query[rows_of(pair)] = query_all[:, columns_of(1 - half, pair)]
        own_query[rows_of(pair)] = query_all[:, columns_of(half, pair)]
    query_shared = query_all[:, shared].astype(f32)
    single[0] = low_or_high(query_shared, 0.0)
    single[1] = low_or_high(turned(query_shared), 0.0)
    own_query[rows_of(PAIRS)] = single[half].astype(bf16)
    theirs = single[1 - half]
    swap_query[SHARED:] = low_or_high(theirs[:HDIM], turned(theirs[HDIM:])).astype(bf16)


def pack(clip, query, key, value):
    wide = pltpu.VMEM((BLOCK, WIDTH), bf16)
    return kernel(
        pack_kernel,
        "pack",
        [SMEM, HBM, HBM, HBM],
        [shaped((ROWS + CLIP_ROWS, PAIR), bf16)] * 2
        + [shaped((HALF, PAIR), bf16), shaped((SHARED + PAIR, PAIR), bf16)],
        [
            wide,
            wide,
            wide,
            pltpu.VMEM((2, BLOCK, PAIR), bf16),
            pltpu.VMEM((2, BLOCK, PAIR), f32),
            pltpu.SemaphoreType.DMA((3,)),
        ],
    )(clip, in_hbm(query), in_hbm(key), in_hbm(value))


def unpacked_single(packed):
    packed = packed.astype(f32)
    top, bottom = low_or_high(packed, 0.0), low_or_high(turned(packed), 0.0)
    return jnp.concatenate([top, bottom], axis=0).astype(bf16)


def join_query(target, d_turned, single, query, query_single, d_pairs, d_shared):
    half = my_half()
    for pair in range(PAIRS):
        d_pair = d_pairs[:, pair * PAIR : (pair + 1) * PAIR].astype(bf16)
        target[rows_of(pair)] = query[rows_of(pair)]
        target[rows_of(PAIRS + pair)] = d_pair
        d_turned[head_rows(half, pair)] = d_pair.T
    single[0] = low_or_high(0.0, turned(d_shared)).astype(bf16)
    single[1] = low_or_high(0.0, d_shared).astype(bf16)
    d_single = single[half]
    target[rows_of(MIXED)] = query_single + d_single
    d_turned[single_rows(half)] = d_single.T[HDIM:]


def own_cotangent_kernel(cotangent, weight, query, both, d_turned, kept, rows, single, sems):
    half = my_half()
    chunk = rows.shape[1] // CHUNKS
    copies = [pltpu.make_async_copy(cotangent, rows, sems.at[CHUNKS])]
    for number in range(CHUNKS):
        part = pl.ds(number * chunk, chunk)
        copies.append(pltpu.make_async_copy(weight.at[part], kept.at[part], sems.at[number]))
    for copy in copies:
        copy.start()
    copies[0].wait()
    pairs = shared = None
    for number in range(CHUNKS):
        copies[number + 1].wait()
        part = slice(number * chunk, (number + 1) * chunk)
        wide = times(rows[:, part], kept[part, span(half * (SHARED + PAIR), SHARED, PAIR)], ((1,), (0,)))
        narrow = times(rows[:, part], kept[part, SHARED : SHARED + PAIR], ((1,), (0,)))
        pairs = wide if pairs is None else pairs + wide
        shared = narrow if shared is None else shared + narrow
    join_query(both, d_turned, single, query, query[rows_of(PAIRS)], pairs, shared)


def own_cotangents(cotangent, weight, query):
    return kernel(
        own_cotangent_kernel,
        "own_cotangents",
        [HBM, HBM, VMEM],
        [shaped((ROWS, PAIR), bf16), shaped((HALF, BLOCK), bf16), shaped(weight.shape, bf16)],
        [
            pltpu.VMEM(cotangent.shape, bf16),
            pltpu.VMEM((2, BLOCK, PAIR), bf16),
            pltpu.SemaphoreType.DMA((CHUNKS + 1,)),
        ],
    )(in_hbm(cotangent), in_hbm(weight), query)


def cotangent_kernel(
    cotangent, weight, query, att, d_turned_own, totals, both, stats, d_turned, d_all, single
):
    half = my_half()
    rows = cotangent[...]
    pairs = times(rows, weight[:, span(half * (SHARED + PAIR), SHARED, PAIR)], ((1,), (0,)))
    shared = times(rows, weight[:, SHARED : SHARED + PAIR], ((1,), (0,)))
    query_single = unpacked_single(query[SHARED:])
    join_query(both, d_turned, single, query, query_single, pairs, shared)
    d_all[:, at(half, BLOCK)] = d_turned_own[...]
    d_all[:, at(1 - half, BLOCK)] = d_turned[...]
    stats[...] = totals[...]
    for query_block in range(2):
        steps = rows_of(query_block)
        for pair in range(PAIRS):
            which = head_rows(half, pair)
            dots = d_all[which, steps].astype(f32) * att[which, steps].astype(f32)
            row = DELTA_STAT + 2 * pair + query_block
            stats[row : row + 1, :BLOCK] = jnp.sum(dots[:HDIM], axis=0, keepdims=True)
            stats[row : row + 1, BLOCK:] = jnp.sum(dots[HDIM:], axis=0, keepdims=True)
        which = single_rows(half)
        dots = d_all[which, steps].astype(f32) * att[which, steps].astype(f32)
        row = DELTA_STAT + 2 * PAIRS + query_block
        stats[row : row + 1, :BLOCK] = jnp.sum(dots, axis=0, keepdims=True)
    rest = jnp.concatenate([stats[:, :BLOCK], stats[:, BLOCK:]], axis=0)
    for number in range(3):
        begin = ROWS + 2 * STAT_ROWS * number
        part = rest.astype(bf16)
        both[begin : begin + 2 * STAT_ROWS] = part
        rest = rest - part.astype(f32)


def stats_of(both):
    parts = []
    for number in range(3):
        begin = ROWS + 2 * STAT_ROWS * number
        parts.append(both[begin : begin + 2 * STAT_ROWS].astype(f32))
    total = (parts[0] + parts[1]) + parts[2]
    return jnp.concatenate([total[:STAT_ROWS], total[STAT_ROWS:]], axis=1)


def cotangents(cotangent, weight, query, att, d_turned_own, totals):
    return kernel(
        cotangent_kernel,
        "cotangents",
        [VMEM] * 6,
        [shaped((SENT_ROWS, PAIR), bf16), shaped((STAT_ROWS, 2 * BLOCK), f32)],
        [
            pltpu.VMEM((HALF, BLOCK), bf16),
            pltpu.VMEM((HALF, 2 * BLOCK), bf16),
            pltpu.VMEM((2, BLOCK, PAIR), bf16),
        ],
    )(cotangent, weight, query, att, d_turned_own, totals)


def gather_blocks(target, offset, own, partner):
    half = my_half()
    for block in range(target.shape[0]):
        target[block, at(offset + half, BLOCK)] = own[rows_of(block)]
        target[block, at(offset + 1 - half, BLOCK)] = partner[rows_of(block)]


def doubled(rows, factor=1.0):
    first = low_or_high(factor, 0.0).astype(bf16)
    second = low_or_high(0.0, factor).astype(bf16)
    return jnp.concatenate([rows * first, rows * second], axis=0)


def diagonal(pair):
    return jnp.concatenate([pair[:HDIM, :BLOCK], pair[HDIM:, BLOCK:]], axis=0)


def triangles():
    row = lax.broadcasted_iota(jnp.int32, (BLOCK, BLOCK), 0)
    lane = lax.broadcasted_iota(jnp.int32, (BLOCK, BLOCK), 1)
    older = jnp.where(row > lane, 1.0, 0.0)
    return older, jnp.ones((BLOCK, BLOCK), f32), 1.0 - older


def hidden(scores, visible):
    if scores.shape[1] > visible.shape[1]:
        visible = jnp.concatenate([visible, visible], axis=1)
    return jnp.where(visible > 0.5, scores, big_negative)


def gather_kernel(
    own, partner, halo, halo_other, query_own, query_partner, keys_all, query_all, mask, clip_row, clips
):
    half = my_half()
    gather_blocks(keys_all, 0, halo, halo_other)
    gather_blocks(keys_all, 2, own, partner)
    for pair in range(PAIRS):
        query_all[pair, at(half, BLOCK)] = query_own[rows_of(pair)]
        query_all[pair, at(1 - half, BLOCK)] = query_partner[rows_of(pair)]
    query_all[PAIRS, at(half, BLOCK)] = query_own[rows_of(PAIRS)]
    query_all[PAIRS, at(1 - half, BLOCK)] = unpacked_single(query_partner[SHARED:])
    for offset, mine, theirs in ((0, halo, halo_other), (2, own, partner)):
        clips[at(offset + half, CLIP_ROWS)] = mine[ROWS:]
        clips[at(offset + 1 - half, CLIP_ROWS)] = theirs[ROWS:]

    def clip_of(block):
        return clips[block * CLIP_ROWS : (block + 1) * CLIP_ROWS].astype(f32)[0:1]

    for query_block in range(2):
        query_clip = clip_of(2 + query_block)
        for step, shape in enumerate(triangles()):
            block = query_block + step
            same = jnp.where(clip_of(block) == query_clip, 1.0, 0.0)
            present = jnp.where(2 * my_group() - 2 + block >= 0, 1.0, 0.0)
            mask[query_block, rows_of(step)] = shape * same * present
        clip_row[:, rows_of(query_block)] = query_clip


def gathered(*sources):
    return kernel(
        gather_kernel,
        "gathered",
        [VMEM] * 6,
        [
            shaped((MIXED + 1, 4 * BLOCK, PAIR), bf16),
            shaped((PAIRS + 1, 2 * BLOCK, PAIR), bf16),
            shaped((2, WIN + BLOCK, BLOCK), f32),
            shaped((1, 2 * BLOCK), f32),
        ],
        [pltpu.VMEM((4 * CLIP_ROWS, PAIR), bf16)],
        flops=COST_GATHER,
    )(*sources)


def forward_kernel(
    pieces_wanted,
    keys_all,
    query_all,
    mask,
    clip_row,
    weights_out,
    single_out,
    totals,
    att,
    att_own,
    att_swap,
    *pieces,
):
    half = my_half()
    totals[CLIP_STAT : CLIP_STAT + 1] = clip_row[...]

    def softmax(scores, row):
        lanes = slice(0, scores.shape[1])
        maximum = jnp.max(scores, axis=0, keepdims=True)
        powers = jnp.exp(scores - maximum)
        total = jnp.sum(powers, axis=0, keepdims=True)
        totals[row : row + 1, lanes] = maximum + jnp.log(total)
        return (powers * (1.0 / total)).astype(bf16)

    for pair in range(PAIRS):
        for query_block in range(2):
            keys = slice(query_block * BLOCK, query_block * BLOCK + WIN + BLOCK)
            steps = rows_of(query_block)
            query_rows = doubled(query_all[pair, steps], SCALING)
            scores = times(keys_all[pair, keys], query_rows, ((1,), (1,)))
            weights = softmax(hidden(scores, mask[query_block]), 2 * pair + query_block)
            weights_out[pair, query_block] = weights
            mixed = times(keys_all[PAIRS + pair, keys], weights, ((0,), (0,)))
            att[head_rows(half, pair), steps] = diagonal(mixed).astype(bf16)
    for query_block in range(2):
        keys = slice(query_block * BLOCK, query_block * BLOCK + WIN + BLOCK)
        steps = rows_of(query_block)
        query_rows = query_all[PAIRS, steps] * low_or_high(SCALING, 0.0).astype(bf16)
        scores = times(keys_all[MIXED, keys], query_rows, ((1,), (1,)))
        weights = softmax(hidden(scores, mask[query_block]), 2 * PAIRS + query_block)
        single_out[query_block] = weights
        mixed = times(keys_all[MIXED, keys], weights, ((0,), (0,)))
        att[single_rows(half), steps] = mixed[HDIM:].astype(bf16)

    att_own[...] = att[:, at(half, BLOCK)]
    att_swap[...] = att[:, at(1 - half, BLOCK)]
    if pieces_wanted:
        rows = pieces[0].shape[0]
        for number, piece in enumerate(pieces):
            begin = rows * jnp.bitwise_xor(lax.axis_index("dp"), number)
            piece[...] = att[span(begin, rows, 16), :]


def forward(pieces_wanted, *sources):
    piece = (HALF // max(pieces_wanted, 1), 2 * BLOCK)
    return kernel(
        functools.partial(forward_kernel, pieces_wanted),
        "forward",
        [VMEM] * 4,
        [
            shaped((PAIRS, 2, WIN + BLOCK, 2 * BLOCK), bf16),
            shaped((2, WIN + BLOCK, BLOCK), bf16),
            shaped((STAT_ROWS, 2 * BLOCK), f32),
            shaped((HALF, 2 * BLOCK), bf16),
            shaped((HALF, BLOCK), bf16),
            shaped((HALF, BLOCK), bf16),
        ]
        + [shaped(piece, bf16)] * pieces_wanted,
    )(*sources)


def score_gradients(weights, values, d_rows, delta):
    d_weights = times(values, d_rows, ((1,), (1,)))
    return (weights.astype(f32) * (d_weights - delta)).astype(bf16)


def own_kernel(
    keys_all,
    both_own,
    both_partner,
    weights_in,
    single_in,
    stats,
    att_swap,
    dq_own,
    swap,
    own_grads,
    partner_grads,
    query_all,
    dq_all,
    grads,
):
    half = my_half()
    gather_blocks(query_all, 0, both_own, both_partner)

    def delta_of(row, lanes):
        return stats[DELTA_STAT + row : DELTA_STAT + row + 1, :lanes]

    def accumulate(block, query_block, value):
        if query_block == 1:
            grads[block] = value
        else:
            grads[block, :BLOCK] += value

    for query_block in (1, 0):
        keys = slice(query_block * BLOCK, query_block * BLOCK + WIN + BLOCK)
        mine = slice(WIN - query_block * BLOCK, WIN + BLOCK)
        steps = rows_of(query_block)
        for pair in range(PAIRS):
            query_rows = doubled(query_all[pair, steps], SCALING)
            d_rows = doubled(query_all[PAIRS + pair, steps])
            weights = weights_in[pair, query_block]
            d_scores = score_gradients(
                weights,
                keys_all[PAIRS + pair, keys],
                d_rows,
                delta_of(2 * pair + query_block, 2 * BLOCK),
            )
            dq = diagonal(times(keys_all[pair, keys], d_scores, ((0,), (0,))))
            dq_all[head_rows(half, pair), steps] = (dq * SCALING).astype(bf16)
            accumulate(pair, query_block, times(d_scores[mine], query_rows, ((1,), (0,))))
            accumulate(PAIRS + pair, query_block, times(weights[mine], d_rows, ((1,), (0,))))
        rows = query_all[MIXED, steps]
        query_rows = rows * low_or_high(SCALING, 0.0).astype(bf16)
        d_rows = rows * low_or_high(0.0, 1.0).astype(bf16)
        weights = single_in[query_block]
        mixed = keys_all[MIXED, keys]
        d_scores = score_gradients(
            weights, mixed, d_rows, delta_of(2 * PAIRS + query_block, BLOCK)
        )
        dq = times(mixed, d_scores, ((0,), (0,)))[:HDIM]
        dq_all[single_rows(half), steps] = (dq * SCALING).astype(bf16)
        value = times(d_scores[mine], query_rows, ((1,), (0,)))
        accumulate(MIXED, query_block, value + times(weights[mine], d_rows, ((1,), (0,))))
    dq_own[...] = dq_all[:, at(half, BLOCK)]
    swap[:, :BLOCK] = att_swap[...]
    swap[:, BLOCK:] = dq_all[:, at(1 - half, BLOCK)]
    for block in range(MIXED + 1):
        own_grads[rows_of(block)] = grads[block, at(half, BLOCK)]
        partner_grads[rows_of(block)] = grads[block, at(1 - half, BLOCK)]


def own_gradients(*sources):
    return kernel(
        own_kernel,
        "own_gradients",
        [VMEM] * 7,
        [shaped((HALF, BLOCK), bf16), shaped((HALF, 2 * BLOCK), bf16)]
        + [shaped((ROWS, PAIR), f32)] * 2,
        [
            pltpu.VMEM((MIXED + 1, 2 * BLOCK, PAIR), bf16),
            pltpu.VMEM((HALF, 2 * BLOCK), bf16),
            pltpu.VMEM((MIXED + 1, 2 * BLOCK, PAIR), f32),
        ],
    )(*sources)


def next_kernel(
    groups,
    own,
    partner,
    both_own,
    both_partner,
    own_grads,
    partner_grads,
    mine,
    swap,
    keys_all,
    query_all,
    mask,
    grads,
    clips,
    stats,
):
    half = my_half()
    stats[...] = stats_of(both_partner)
    gather_blocks(keys_all, 0, own, partner)
    gather_blocks(query_all, 0, both_own, both_partner)
    for block in range(MIXED + 1):
        grads[block, at(half, BLOCK)] = own_grads[rows_of(block)]
        grads[block, at(1 - half, BLOCK)] = partner_grads[rows_of(block)]
    clips[at(half, CLIP_ROWS)] = own[ROWS:]
    clips[at(1 - half, CLIP_ROWS)] = partner[ROWS:]
    present = jnp.where(my_group() < groups - 1, 1.0, 0.0)
    older, every, _ = triangles()
    for query_block, block, shape in ((0, 0, older), (0, 1, every), (1, 1, older)):
        query_clip = stats[CLIP_STAT : CLIP_STAT + 1, rows_of(query_block)]
        key_clip = clips[block * CLIP_ROWS : (block + 1) * CLIP_ROWS].astype(f32)[0:1]
        same = jnp.where(key_clip == query_clip, 1.0, 0.0)
        mask[query_block, rows_of(block)] = shape * same * present

    for query_block in range(2):
        keys = slice(query_block * BLOCK, WIN)
        steps = rows_of(query_block)
        visible = mask[query_block, keys]
        for pair in range(PAIRS + 1):
            row = 2 * pair + query_block
            lanes = slice(0, 2 * BLOCK if pair < PAIRS else BLOCK)
            if pair < PAIRS:
                key_rows, value_rows = keys_all[pair, keys], keys_all[PAIRS + pair, keys]
                query_rows = doubled(query_all[pair, steps], SCALING)
                d_rows = doubled(query_all[PAIRS + pair, steps])
            else:
                key_rows = value_rows = keys_all[MIXED, keys]
                query_rows = query_all[MIXED, steps] * low_or_high(SCALING, 0.0).astype(bf16)
                d_rows = query_all[MIXED, steps] * low_or_high(0.0, 1.0).astype(bf16)
            scores = hidden(times(key_rows, query_rows, ((1,), (1,))), visible)
            weights = jnp.exp(scores - stats[row : row + 1, lanes]).astype(bf16)
            delta = stats[DELTA_STAT + row : DELTA_STAT + row + 1, lanes]
            d_scores = score_gradients(weights, value_rows, d_rows, delta)
            dk = times(d_scores, query_rows, ((1,), (0,)))
            dv = times(weights, d_rows, ((1,), (0,)))
            if pair < PAIRS:
                grads[pair, keys] += dk
                grads[PAIRS + pair, keys] += dv
            else:
                grads[MIXED, keys] += dk + dv
    for block in range(MIXED + 1):
        mine[rows_of(block)] = grads[block, at(half, BLOCK)].astype(bf16)
        swap[rows_of(block)] = grads[block, at(1 - half, BLOCK)].astype(bf16)


def next_gradients(groups, *sources):
    return kernel(
        functools.partial(next_kernel, groups),
        "next_gradients",
        [VMEM] * 6,
        [shaped((ROWS, PAIR), bf16)] * 2,
        [
            pltpu.VMEM((MIXED + 1, 2 * BLOCK, PAIR), bf16),
            pltpu.VMEM((MIXED + 1, 2 * BLOCK, PAIR), bf16),
            pltpu.VMEM((2, 2 * BLOCK, BLOCK), f32),
            pltpu.VMEM((MIXED + 1, 2 * BLOCK, PAIR), f32),
            pltpu.VMEM((2 * CLIP_ROWS, PAIR), bf16),
            pltpu.VMEM((STAT_ROWS, 2 * BLOCK), f32),
        ],
    )(*sources)


def output_kernel(att_own, received, weight, out, full):
    half = my_half()
    full[at(half, HALF)] = att_own[...]
    full[at(1 - half, HALF)] = received[:, :BLOCK]
    out[...] = times(weight[...], full[...], ((1,), (0,))).T.astype(bf16)


def output_rows(att_own, received, weight):
    return kernel(
        output_kernel,
        "output",
        [VMEM] * 3,
        [shaped((BLOCK, weight.shape[0]), bf16), shaped((WIDTH, BLOCK), bf16)],
    )(att_own, received, weight)


def place_keys_kernel(mine, theirs, key_out, value_out, key, value, mixed, sems):
    half = my_half()
    for side, source in ((half, mine), (1 - half, theirs)):
        for pair in range(PAIRS):
            key[:, columns_of(side, pair)] = source[rows_of(pair)]
            value[:, columns_of(side, pair)] = source[rows_of(PAIRS + pair)]
        mixed[side] = source[rows_of(MIXED)].astype(f32)
    shared = slice(SHARED, SHARED + PAIR)
    key[:, shared] = low_or_high(mixed[0], turned(mixed[1])).astype(bf16)
    value[:, shared] = low_or_high(turned(mixed[0]), mixed[1]).astype(bf16)
    pairs = ((key, key_out), (value, value_out))
    copies = [pltpu.make_async_copy(a, b, sems.at[n]) for n, (a, b) in enumerate(pairs)]
    for copy in copies:
        copy.start()
    for copy in copies:
        copy.wait()


def place_keys(*sources):
    wide = pltpu.VMEM((BLOCK, WIDTH), bf16)
    mixed = pltpu.VMEM((2, BLOCK, PAIR), f32)
    return kernel(
        place_keys_kernel,
        "place_keys",
        [VMEM] * 2,
        [shaped((BLOCK, WIDTH), bf16)] * 2,
        [wide, wide, mixed, pltpu.SemaphoreType.DMA((2,))],
        HBM,
        COST_KEYS,
    )(*sources)


def place_kernel(dq_mine, received, first, second, query_out, weight_out, dq_all, query, both, sems):
    half = my_half()
    rows = first.shape[0]
    moves = [(both, weight_out), (query, query_out)]
    copies = [pltpu.make_async_copy(a, b, sems.at[n]) for n, (a, b) in enumerate(moves)]
    both[span(half * rows, rows, 16)] = first[...].astype(f32)
    both[span((1 - half) * rows, rows, 16)] = second[...].astype(f32)
    copies[0].start()
    dq_all[at(half, HALF)] = dq_mine[...]
    dq_all[at(1 - half, HALF)] = received[:, BLOCK:]
    for block in range(WIDTH // PAIR):
        query[:, block * PAIR : (block + 1) * PAIR] = dq_all[rows_of(block)].T
    copies[1].start()
    for copy in copies:
        copy.wait()


def place(*sources):
    rows, lanes = sources[-1].shape
    query, weight = kernel(
        place_kernel,
        "place",
        [VMEM] * 4,
        [shaped((BLOCK, WIDTH), bf16), shaped((2 * rows, lanes), f32)],
        [
            pltpu.VMEM((WIDTH, BLOCK), bf16),
            pltpu.VMEM((BLOCK, WIDTH), bf16),
            pltpu.VMEM((2 * rows, lanes), f32),
            pltpu.SemaphoreType.DMA((2,)),
        ],
        HBM,
    )(*sources)
    return query, weight.T


def weight_kernel(count, *refs):
    pieces, cots, products = refs[:count], refs[count : 2 * count], refs[-1]
    half = my_half()
    att = jnp.concatenate([piece[:, at(half, BLOCK)] for piece in pieces], axis=1)
    products[...] = times(att, jnp.concatenate([cot[...] for cot in cots], axis=0), ((1,), (0,)))


def weight_products(pieces, cots):
    return kernel(
        functools.partial(weight_kernel, len(pieces)),
        "weight_products",
        [VMEM] * (2 * len(pieces)),
        [shaped((pieces[0].shape[0], cots[0].shape[1]), f32)],
        flops=COST_FIRST,
    )(*pieces, *cots)[0]


def weight_rest_kernel(count, products, *refs):
    pieces, cots = refs[:count], refs[count : 2 * count]
    kept, *sent = refs[2 * count :]
    total = sent.pop()
    half = my_half()
    att = jnp.concatenate([piece[:, at(1 - half, BLOCK)] for piece in pieces], axis=1)
    cot = jnp.concatenate([cot[...] for cot in cots], axis=0)
    total[...] = products[...] + times(att, cot, ((1,), (0,)))
    group = my_group()
    lanes = kept.shape[1]
    kept[...] = total[:, at(group, lanes)]
    for number, out in enumerate(sent):
        target = jnp.bitwise_xor(group, number + 1)
        out[...] = total[:, at(target, lanes)].astype(bf16)


def weight_rest(products, pieces, cots, groups):
    rows, outs = products.shape
    part = (rows, outs // groups)
    return kernel(
        functools.partial(weight_rest_kernel, len(pieces)),
        "weight_rest",
        [VMEM] * (1 + 2 * len(pieces)),
        [shaped(part, f32)] + [shaped(part, bf16)] * (groups - 1),
        [pltpu.VMEM((rows, outs), f32)],
    )(products, *pieces, *cots)


def weight_sum_kernel(kept, *rest):
    received, (first, second, total) = rest[:-3], rest[-3:]
    value = kept[...]
    for part in received:
        value = value + part[...].astype(f32)
    total[...] = value
    lanes = first.shape[1]
    odd = jnp.bitwise_and(lax.axis_index("dp"), 1)
    first[...] = total[:, at(odd, lanes)].astype(bf16)
    second[...] = total[:, at(1 - odd, lanes)].astype(bf16)


def weight_sum(kept, received):
    rows, lanes = kept.shape
    return kernel(
        weight_sum_kernel,
        "weight_sum",
        [VMEM] * (1 + len(received)),
        [shaped((rows, lanes // 2), bf16)] * 2,
        [pltpu.VMEM((rows, lanes), f32)],
        flops=COST_SUM,
    )(kept, *received)


def swapped(value, axis, bits):
    count = lax.axis_size(axis)
    return lax.ppermute(value, axis, [(source, source ^ bits) for source in range(count)])


def rotated(value, axis, steps):
    count = lax.axis_size(axis)
    return lax.ppermute(
        value, axis, [(source, (source + steps) % count) for source in range(count)]
    )


def moved(value, axis, steps):
    count = lax.axis_size(axis)
    first, last = (max(0, -steps), min(count, count - steps))
    return lax.ppermute(value, axis, [(source, source + steps) for source in range(first, last)])


def placed(value, flip):
    lanes = lax.axis_size("ctx")
    moves = []
    for source in range(lax.axis_size("dp")):
        for index in range(lanes):
            group, half = index // 2, index % 2
            target_half = (source % 2) ^ flip
            target = 2 * half + source // 2
            moves.append((source * lanes + index, target * lanes + 2 * group + target_half))
    return lax.ppermute(value, ("dp", "ctx"), moves)


def after(*values):
    return lax.optimization_barrier(values)


def per_device(queries, key_states, value_states, out_cotangent, out_weight, block_clip):
    sequences = lax.axis_size("dp")
    groups = lax.axis_size("ctx") // 2
    short = sequences == 4 and groups in (2, 4)
    cotangent = out_cotangent[0]

    swap_kv, own, swap_query, query = pack(
        block_clip, queries[0], key_states[0], value_states[0]
    )
    swap_kv, cot_early = after(swap_kv, cotangent)
    partner = swapped(swap_kv, "ctx", 1)
    halo = rotated(own, "ctx", 2)
    both_own, d_turned_own, weight = own_cotangents(cotangent, out_weight, query)
    cots = [cotangent]
    if short:
        cots += [swapped(cot_early, "dp", n) for n in (1, 2)]

    partner, both_own, swap_query = after(partner, both_own, swap_query)
    halo_other = rotated(partner, "ctx", 2)
    query_partner = swapped(swap_query, "ctx", 1)
    halo, both_own, cot_late, *cots = after(halo, both_own, cotangent, *cots)
    cot_partner = swapped(cot_late, "ctx", 1)
    next_own = moved(both_own, "ctx", -2)
    if short:
        cots.append(swapped(cots[2], "dp", 1))
    keys_all, query_all, mask, clip_row = gathered(
        own, partner, halo, halo_other, query, query_partner
    )
    keys_all, cot_partner = after(keys_all, cot_partner)

    later = [cot_partner]
    if short:
        later += [swapped(cot_partner, "dp", n) for n in (1, 2)]
    weights, single, totals, att, att_own, att_swap, *pieces = forward(
        4 if short else 0, keys_all, query_all, mask, clip_row
    )
    weights, next_own, *rest = after(weights, next_own, *pieces, *cots)
    pieces, cots = rest[: len(pieces)], rest[len(pieces) :]

    if short:
        pieces[1:] = [swapped(pieces[n], "dp", n) for n in (1, 2, 3)]
        weights, *later = after(weights, *later)
        later.append(swapped(later[2], "dp", 1))
    both_partner, stats = cotangents(
        cot_partner, weight, query_partner, att, d_turned_own, totals
    )
    next_partner = rotated(both_partner, "ctx", -2)
    dq_own, swap, own_grads, partner_grads = own_gradients(
        keys_all, both_own, both_partner, weights, single, stats, att_swap
    )
    own_grads, swap, *pieces = after(own_grads, swap, *pieces)

    if short:
        products = weight_products(pieces, cots)
        products, *later = after(products, *later)
        kept, *sent = weight_rest(products, pieces, later, groups)
        sent[-1], next_partner = after(sent[-1], next_partner)
        arrived = [swapped(part, "ctx", 2 * (n + 1)) for n, part in enumerate(sent)]
        kept, own_grads = after(kept, own_grads)
    received = swapped(swap, "ctx", 1)
    kv_own, kv_swap = next_gradients(
        groups, own, partner, next_own, next_partner, own_grads, partner_grads
    )
    kv_rest = swapped(kv_swap, "ctx", 1)
    if short:
        kept, kv_own, received, *arrived = after(kept, kv_own, received, *arrived)
        first, second = weight_sum(kept, arrived)
        first, second = placed(first, 0), placed(second, 1)
    sublayer_out, att_full = output_rows(att_own, received, weight)
    if not short:
        product = lax.dot_general(
            cotangent, att_full, (((0,), (1,)), ((), ())), preferred_element_type=f32
        ).astype(bf16)
        sequence_grad = lax.psum_scatter(product, "ctx", scatter_dimension=0, tiled=True)
        weight_grad = lax.psum_scatter(
            sequence_grad.astype(f32), "dp", scatter_dimension=1, tiled=True
        )
        first = second = jnp.zeros((16, 128), bf16)
    kv_own, sublayer_out = after(kv_own, sublayer_out)
    key_grad, value_grad = place_keys(kv_own, kv_rest)
    dq_own, key_grad = after(dq_own, key_grad)
    query_grad, placed_weight = place(dq_own, received, first, second)
    if short:
        weight_grad = placed_weight
    return (
        sublayer_out[None],
        query_grad[None],
        key_grad[None],
        value_grad[None],
        weight_grad,
    )


def solution(mesh):
    return jax.shard_map(
        per_device,
        mesh=mesh,
        in_specs=(
            P("dp", "ctx", None),
            P("dp", "ctx", None),
            P("dp", "ctx", None),
            P("dp", "ctx", None),
            P(),
            P("dp", "ctx"),
        ),
        out_specs=(
            P("dp", "ctx", None),
            P("dp", "ctx", None),
            P("dp", "ctx", None),
            P("dp", "ctx", None),
            P("ctx", "dp"),
        ),
        check_vma=False,
    )
```

```python
import functools
import math

import jax
import jax.numpy as jnp
from jax import lax
from jax.experimental import pallas as pl
from jax.experimental.pallas import tpu as pltpu
from jax.sharding import PartitionSpec as P

HEADS = 18
HDIM = 64
BLOCK = 128
WIN = 256
PAIR = 2 * HDIM
WIDTH = HEADS * HDIM
HALF = WIDTH // 2
PAIRS = HEADS // 4
SHARED = PAIRS * PAIR
MIXED = 2 * PAIRS
ROWS = (MIXED + 1) * BLOCK
CLIP_ROWS = 16
CLIP_STAT = 2 * PAIRS + 2
DELTA_STAT = CLIP_STAT + 2
STAT_ROWS = 24
SENT_ROWS = ROWS + 6 * STAT_ROWS
CHUNKS = 4
SCALING = 1.0 / math.sqrt(HDIM)
COST_GATHER = 2_000_000_000
COST_KEYS = 1_000_000
COST_FIRST = 2_000_000_000
COST_NEXT = 4_000_000_000
COST_SUM = 2_000_000_000
VMEM_LIMIT = 24 * 1024 * 1024

big_negative = -1e30
bf16 = jnp.bfloat16
f32 = jnp.float32

VMEM = pl.BlockSpec(memory_space=pltpu.VMEM)
HBM = pl.BlockSpec(memory_space=pltpu.HBM)


def shaped(shape, dtype):
    return jax.ShapeDtypeStruct(shape, dtype)


def kernel(body, name, ins, outs, scratch=(), out_space=VMEM, flops=1_000_000):
    return pl.pallas_call(
        body,
        out_shape=tuple(outs),
        in_specs=list(ins),
        out_specs=(out_space,) * len(outs),
        scratch_shapes=list(scratch),
        compiler_params=pltpu.CompilerParams(vmem_limit_bytes=VMEM_LIMIT),
        cost_estimate=pl.CostEstimate(flops=flops, bytes_accessed=10_000, transcendentals=0),
        name=name,
    )


def in_hbm(value):
    return pltpu.with_memory_space_constraint(value, pltpu.HBM)


def my_half():
    return jnp.bitwise_and(lax.axis_index("ctx"), 1)


def my_group():
    return jnp.right_shift(lax.axis_index("ctx"), 1)


def at(index, size):
    return pl.ds(pl.multiple_of(index * size, size), size)


def span(start, size, unit):
    return pl.ds(pl.multiple_of(start, unit), size)


def rows_of(block):
    return slice(block * BLOCK, (block + 1) * BLOCK)


def columns_of(half, pair):
    return span(half * (SHARED + PAIR) + pair * PAIR, PAIR, PAIR)


def head_rows(half, pair):
    return span(half * HDIM + pair * PAIR, PAIR, HDIM)


def single_rows(half):
    return span((1 - half) * SHARED, HDIM, HDIM)


def times(a, b, dims):
    return lax.dot_general(a, b, (dims, ((), ())), preferred_element_type=f32)


def is_low():
    return lax.broadcasted_iota(jnp.int32, (1, PAIR), 1) < HDIM


def low_or_high(low_value, high_value):
    return jnp.where(is_low(), low_value, high_value)


def turned(value):
    return pltpu.roll(value, HDIM, 1)


def pack_kernel(clip, query, key, value, swap_kv, own_kv, swap_query, own_query, *scratch):
    query_all, key_all, value_all, mixed, single, sems = scratch
    half = my_half()
    pairs = ((key, key_all), (value, value_all), (query, query_all))
    copies = [pltpu.make_async_copy(a, b, sems.at[n]) for n, (a, b) in enumerate(pairs)]
    for copy in copies:
        copy.start()
    shared = slice(SHARED, SHARED + PAIR)
    for copy in copies:
        copy.wait()
    clip_rows = jnp.broadcast_to(clip[...].astype(f32), (CLIP_ROWS, PAIR)).astype(bf16)
    for side, target in ((1 - half, swap_kv), (half, own_kv)):
        for pair in range(PAIRS):
            target[rows_of(pair)] = key_all[:, columns_of(side, pair)]
            target[rows_of(PAIRS + pair)] = value_all[:, columns_of(side, pair)]
        target[ROWS:] = clip_rows
    key_shared = key_all[:, shared].astype(f32)
    value_shared = value_all[:, shared].astype(f32)
    mixed[0] = low_or_high(key_shared, turned(value_shared)).astype(bf16)
    mixed[1] = low_or_high(turned(key_shared), value_shared).astype(bf16)
    swap_kv[rows_of(MIXED)] = mixed[1 - half]
    own_kv[rows_of(MIXED)] = mixed[half]
    for pair in range(PAIRS):
        swap_query[rows_of(pair)] = query_all[:, columns_of(1 - half, pair)]
        own_query[rows_of(pair)] = query_all[:, columns_of(half, pair)]
    query_shared = query_all[:, shared].astype(f32)
    single[0] = low_or_high(query_shared, 0.0)
    single[1] = low_or_high(turned(query_shared), 0.0)
    own_query[rows_of(PAIRS)] = single[half].astype(bf16)
    theirs = single[1 - half]
    swap_query[SHARED:] = low_or_high(theirs[:HDIM], turned(theirs[HDIM:])).astype(bf16)


def pack(clip, query, key, value):
    wide = pltpu.VMEM((BLOCK, WIDTH), bf16)
    return kernel(
        pack_kernel,
        "pack",
        [VMEM, HBM, HBM, HBM],
        [shaped((ROWS + CLIP_ROWS, PAIR), bf16)] * 2
        + [shaped((HALF, PAIR), bf16), shaped((SHARED + PAIR, PAIR), bf16)],
        [
            wide,
            wide,
            wide,
            pltpu.VMEM((2, BLOCK, PAIR), bf16),
            pltpu.VMEM((2, BLOCK, PAIR), f32),
            pltpu.SemaphoreType.DMA((3,)),
        ],
    )(clip, in_hbm(query), in_hbm(key), in_hbm(value))


def unpacked_single(packed):
    packed = packed.astype(f32)
    top, bottom = low_or_high(packed, 0.0), low_or_high(turned(packed), 0.0)
    return jnp.concatenate([top, bottom], axis=0).astype(bf16)


def join_query(target, d_turned, single, query, query_single, d_pairs, d_shared):
    half = my_half()
    for pair in range(PAIRS):
        d_pair = d_pairs[:, pair * PAIR : (pair + 1) * PAIR].astype(bf16)
        target[rows_of(pair)] = query[rows_of(pair)]
        target[rows_of(PAIRS + pair)] = d_pair
        d_turned[head_rows(half, pair)] = d_pair.T
    single[0] = low_or_high(0.0, turned(d_shared)).astype(bf16)
    single[1] = low_or_high(0.0, d_shared).astype(bf16)
    d_single = single[half]
    target[rows_of(MIXED)] = query_single + d_single
    d_turned[single_rows(half)] = d_single.T[HDIM:]


def own_cotangent_kernel(cotangent, weight, query, both, d_turned, kept, rows, single, sems):
    half = my_half()
    chunk = rows.shape[1] // CHUNKS
    copies = [pltpu.make_async_copy(cotangent, rows, sems.at[CHUNKS])]
    for number in range(CHUNKS):
        part = pl.ds(number * chunk, chunk)
        copies.append(pltpu.make_async_copy(weight.at[part], kept.at[part], sems.at[number]))
    for copy in copies:
        copy.start()
    copies[0].wait()
    pairs = shared = None
    for number in range(CHUNKS):
        copies[number + 1].wait()
        part = slice(number * chunk, (number + 1) * chunk)
        wide = times(rows[:, part], kept[part, span(half * (SHARED + PAIR), SHARED, PAIR)], ((1,), (0,)))
        narrow = times(rows[:, part], kept[part, SHARED : SHARED + PAIR], ((1,), (0,)))
        pairs = wide if pairs is None else pairs + wide
        shared = narrow if shared is None else shared + narrow
    join_query(both, d_turned, single, query, query[rows_of(PAIRS)], pairs, shared)


def own_cotangents(cotangent, weight, query):
    return kernel(
        own_cotangent_kernel,
        "own_cotangents",
        [HBM, HBM, VMEM],
        [shaped((ROWS, PAIR), bf16), shaped((HALF, BLOCK), bf16), shaped(weight.shape, bf16)],
        [
            pltpu.VMEM(cotangent.shape, bf16),
            pltpu.VMEM((2, BLOCK, PAIR), bf16),
            pltpu.SemaphoreType.DMA((CHUNKS + 1,)),
        ],
    )(in_hbm(cotangent), in_hbm(weight), query)


def cotangent_kernel(
    cotangent, weight, query, att, d_turned_own, totals, both, stats, d_turned, d_all, single
):
    half = my_half()
    rows = cotangent[...]
    pairs = times(rows, weight[:, span(half * (SHARED + PAIR), SHARED, PAIR)], ((1,), (0,)))
    shared = times(rows, weight[:, SHARED : SHARED + PAIR], ((1,), (0,)))
    query_single = unpacked_single(query[SHARED:])
    join_query(both, d_turned, single, query, query_single, pairs, shared)
    d_all[:, at(half, BLOCK)] = d_turned_own[...]
    d_all[:, at(1 - half, BLOCK)] = d_turned[...]
    stats[...] = totals[...]
    for query_block in range(2):
        steps = rows_of(query_block)
        for pair in range(PAIRS):
            which = head_rows(half, pair)
            dots = d_all[which, steps].astype(f32) * att[which, steps].astype(f32)
            row = DELTA_STAT + 2 * pair + query_block
            stats[row : row + 1, :BLOCK] = jnp.sum(dots[:HDIM], axis=0, keepdims=True)
            stats[row : row + 1, BLOCK:] = jnp.sum(dots[HDIM:], axis=0, keepdims=True)
        which = single_rows(half)
        dots = d_all[which, steps].astype(f32) * att[which, steps].astype(f32)
        row = DELTA_STAT + 2 * PAIRS + query_block
        stats[row : row + 1, :BLOCK] = jnp.sum(dots, axis=0, keepdims=True)
    rest = jnp.concatenate([stats[:, :BLOCK], stats[:, BLOCK:]], axis=0)
    for number in range(3):
        begin = ROWS + 2 * STAT_ROWS * number
        part = rest.astype(bf16)
        both[begin : begin + 2 * STAT_ROWS] = part
        rest = rest - part.astype(f32)


def stats_of(both):
    parts = []
    for number in range(3):
        begin = ROWS + 2 * STAT_ROWS * number
        parts.append(both[begin : begin + 2 * STAT_ROWS].astype(f32))
    total = (parts[0] + parts[1]) + parts[2]
    return jnp.concatenate([total[:STAT_ROWS], total[STAT_ROWS:]], axis=1)


def cotangents(cotangent, weight, query, att, d_turned_own, totals):
    return kernel(
        cotangent_kernel,
        "cotangents",
        [VMEM] * 6,
        [shaped((SENT_ROWS, PAIR), bf16), shaped((STAT_ROWS, 2 * BLOCK), f32)],
        [
            pltpu.VMEM((HALF, BLOCK), bf16),
            pltpu.VMEM((HALF, 2 * BLOCK), bf16),
            pltpu.VMEM((2, BLOCK, PAIR), bf16),
        ],
    )(cotangent, weight, query, att, d_turned_own, totals)


def gather_blocks(target, offset, own, partner):
    half = my_half()
    for block in range(target.shape[0]):
        target[block, at(offset + half, BLOCK)] = own[rows_of(block)]
        target[block, at(offset + 1 - half, BLOCK)] = partner[rows_of(block)]


def doubled(rows, factor=1.0):
    first = low_or_high(factor, 0.0).astype(bf16)
    second = low_or_high(0.0, factor).astype(bf16)
    return jnp.concatenate([rows * first, rows * second], axis=0)


def diagonal(pair):
    return jnp.concatenate([pair[:HDIM, :BLOCK], pair[HDIM:, BLOCK:]], axis=0)


def triangles():
    row = lax.broadcasted_iota(jnp.int32, (BLOCK, BLOCK), 0)
    lane = lax.broadcasted_iota(jnp.int32, (BLOCK, BLOCK), 1)
    older = jnp.where(row > lane, 1.0, 0.0)
    return older, jnp.ones((BLOCK, BLOCK), f32), 1.0 - older


def hidden(scores, visible):
    if scores.shape[1] > visible.shape[1]:
        visible = jnp.concatenate([visible, visible], axis=1)
    return jnp.where(visible > 0.5, scores, big_negative)


def gather_kernel(
    own, partner, halo, halo_other, query_own, query_partner, keys_all, query_all, mask, clip_row, clips
):
    half = my_half()
    gather_blocks(keys_all, 0, halo, halo_other)
    gather_blocks(keys_all, 2, own, partner)
    for pair in range(PAIRS):
        query_all[pair, at(half, BLOCK)] = query_own[rows_of(pair)]
        query_all[pair, at(1 - half, BLOCK)] = query_partner[rows_of(pair)]
    query_all[PAIRS, at(half, BLOCK)] = query_own[rows_of(PAIRS)]
    query_all[PAIRS, at(1 - half, BLOCK)] = unpacked_single(query_partner[SHARED:])
    for offset, mine, theirs in ((0, halo, halo_other), (2, own, partner)):
        clips[at(offset + half, CLIP_ROWS)] = mine[ROWS:]
        clips[at(offset + 1 - half, CLIP_ROWS)] = theirs[ROWS:]

    def clip_of(block):
        return clips[block * CLIP_ROWS : (block + 1) * CLIP_ROWS].astype(f32)[0:1]

    for query_block in range(2):
        query_clip = clip_of(2 + query_block)
        for step, shape in enumerate(triangles()):
            block = query_block + step
            same = jnp.where(clip_of(block) == query_clip, 1.0, 0.0)
            present = jnp.where(2 * my_group() - 2 + block >= 0, 1.0, 0.0)
            mask[query_block, rows_of(step)] = shape * same * present
        clip_row[:, rows_of(query_block)] = query_clip


def gathered(*sources):
    return kernel(
        gather_kernel,
        "gathered",
        [VMEM] * 6,
        [
            shaped((MIXED + 1, 4 * BLOCK, PAIR), bf16),
            shaped((PAIRS + 1, 2 * BLOCK, PAIR), bf16),
            shaped((2, WIN + BLOCK, BLOCK), f32),
            shaped((1, 2 * BLOCK), f32),
        ],
        [pltpu.VMEM((4 * CLIP_ROWS, PAIR), bf16)],
        flops=COST_GATHER,
    )(*sources)


def staggered(items, *stages):
    values = [None] * len(items)
    for step in range(len(items) + len(stages) - 1):
        for number, stage in enumerate(stages):
            index = step - number
            if 0 <= index < len(items):
                values[index] = stage(*items[index], values[index])


def forward_kernel(
    pieces_wanted,
    keys_all,
    query_all,
    mask,
    clip_row,
    weights_out,
    single_out,
    totals,
    att,
    att_own,
    att_swap,
    *pieces,
):
    half = my_half()
    totals[CLIP_STAT : CLIP_STAT + 1] = clip_row[...]

    def softmax(scores, row):
        lanes = slice(0, scores.shape[1])
        maximum = jnp.max(scores, axis=0, keepdims=True)
        powers = jnp.exp(scores - maximum)
        total = jnp.sum(powers, axis=0, keepdims=True)
        totals[row : row + 1, lanes] = maximum + jnp.log(total)
        return (powers * (1.0 / total)).astype(bf16)

    def keys_of(query_block):
        return slice(query_block * BLOCK, query_block * BLOCK + WIN + BLOCK)

    def score(pair, query_block, _):
        rows = query_all[pair, rows_of(query_block)]
        if pair < PAIRS:
            key_rows, rows = keys_all[pair, keys_of(query_block)], doubled(rows, SCALING)
        else:
            key_rows = keys_all[MIXED, keys_of(query_block)]
            rows = rows * low_or_high(SCALING, 0.0).astype(bf16)
        return times(key_rows, rows, ((1,), (1,)))

    def weigh(pair, query_block, scores):
        return softmax(hidden(scores, mask[query_block]), 2 * pair + query_block)

    def mix(pair, query_block, weights):
        steps = rows_of(query_block)
        if pair < PAIRS:
            weights_out[pair, query_block] = weights
            mixed = times(keys_all[PAIRS + pair, keys_of(query_block)], weights, ((0,), (0,)))
            att[head_rows(half, pair), steps] = diagonal(mixed).astype(bf16)
        else:
            single_out[query_block] = weights
            mixed = times(keys_all[MIXED, keys_of(query_block)], weights, ((0,), (0,)))
            att[single_rows(half), steps] = mixed[HDIM:].astype(bf16)

    items = [(pair, query_block) for pair in range(PAIRS + 1) for query_block in range(2)]
    staggered(items, score, weigh, mix)

    att_own[...] = att[:, at(half, BLOCK)]
    att_swap[...] = att[:, at(1 - half, BLOCK)]
    if pieces_wanted:
        rows = pieces[0].shape[0]
        for number, piece in enumerate(pieces):
            begin = rows * jnp.bitwise_xor(lax.axis_index("dp"), number)
            piece[...] = att[span(begin, rows, 16), :]


def forward(pieces_wanted, *sources):
    piece = (HALF // max(pieces_wanted, 1), 2 * BLOCK)
    return kernel(
        functools.partial(forward_kernel, pieces_wanted),
        "forward",
        [VMEM] * 4,
        [
            shaped((PAIRS, 2, WIN + BLOCK, 2 * BLOCK), bf16),
            shaped((2, WIN + BLOCK, BLOCK), bf16),
            shaped((STAT_ROWS, 2 * BLOCK), f32),
            shaped((HALF, 2 * BLOCK), bf16),
            shaped((HALF, BLOCK), bf16),
            shaped((HALF, BLOCK), bf16),
        ]
        + [shaped(piece, bf16)] * pieces_wanted,
    )(*sources)


def own_kernel(
    keys_all,
    both_own,
    both_partner,
    weights_in,
    single_in,
    stats,
    att_swap,
    dq_own,
    swap,
    own_grads,
    partner_grads,
    query_all,
    dq_all,
    grads,
):
    half = my_half()
    gather_blocks(query_all, 0, both_own, both_partner)

    def delta_of(row, lanes):
        return stats[DELTA_STAT + row : DELTA_STAT + row + 1, :lanes]

    def accumulate(block, query_block, value):
        if query_block == 1:
            grads[block] = value
        else:
            grads[block, :BLOCK] += value

    def keys_of(query_block):
        return slice(query_block * BLOCK, query_block * BLOCK + WIN + BLOCK)

    def operands(pair, query_block):
        steps = rows_of(query_block)
        if pair < PAIRS:
            query_rows = doubled(query_all[pair, steps], SCALING)
            return query_rows, doubled(query_all[PAIRS + pair, steps]), weights_in[pair, query_block]
        rows = query_all[MIXED, steps]
        query_rows = rows * low_or_high(SCALING, 0.0).astype(bf16)
        d_rows = rows * low_or_high(0.0, 1.0).astype(bf16)
        return query_rows, d_rows, single_in[query_block]

    def d_weights_of(pair, query_block, _):
        block = PAIRS + pair if pair < PAIRS else MIXED
        _, d_rows, _ = operands(pair, query_block)
        return times(keys_all[block, keys_of(query_block)], d_rows, ((1,), (1,)))

    def d_scores_of(pair, query_block, d_weights):
        _, _, weights = operands(pair, query_block)
        delta = delta_of(2 * pair + query_block, d_weights.shape[1])
        return (weights.astype(f32) * (d_weights - delta)).astype(bf16)

    def products(pair, query_block, d_scores):
        query_rows, d_rows, weights = operands(pair, query_block)
        mine = slice(WIN - query_block * BLOCK, WIN + BLOCK)
        steps = rows_of(query_block)
        block = pair if pair < PAIRS else MIXED
        dq = times(keys_all[block, keys_of(query_block)], d_scores, ((0,), (0,)))
        dk = times(d_scores[mine], query_rows, ((1,), (0,)))
        dv = times(weights[mine], d_rows, ((1,), (0,)))
        if pair < PAIRS:
            dq_all[head_rows(half, pair), steps] = (diagonal(dq) * SCALING).astype(bf16)
            accumulate(pair, query_block, dk)
            accumulate(PAIRS + pair, query_block, dv)
        else:
            dq_all[single_rows(half), steps] = (dq[:HDIM] * SCALING).astype(bf16)
            accumulate(MIXED, query_block, dk + dv)

    items = [(pair, query_block) for pair in range(PAIRS + 1) for query_block in (1, 0)]
    staggered(items, d_weights_of, d_scores_of, products)
    dq_own[...] = dq_all[:, at(half, BLOCK)]
    swap[:, :BLOCK] = att_swap[...]
    swap[:, BLOCK:] = dq_all[:, at(1 - half, BLOCK)]
    for block in range(MIXED + 1):
        own_grads[rows_of(block)] = grads[block, at(half, BLOCK)]
        partner_grads[rows_of(block)] = grads[block, at(1 - half, BLOCK)]


def own_gradients(*sources):
    return kernel(
        own_kernel,
        "own_gradients",
        [VMEM] * 7,
        [shaped((HALF, BLOCK), bf16), shaped((HALF, 2 * BLOCK), bf16)]
        + [shaped((ROWS, PAIR), f32)] * 2,
        [
            pltpu.VMEM((MIXED + 1, 2 * BLOCK, PAIR), bf16),
            pltpu.VMEM((HALF, 2 * BLOCK), bf16),
            pltpu.VMEM((MIXED + 1, 2 * BLOCK, PAIR), f32),
        ],
    )(*sources)


def next_kernel(
    groups,
    own,
    partner,
    both_own,
    both_partner,
    own_grads,
    partner_grads,
    mine,
    swap,
    keys_all,
    query_all,
    mask,
    grads,
    clips,
    stats,
):
    half = my_half()
    stats[...] = stats_of(both_partner)
    gather_blocks(keys_all, 0, own, partner)
    gather_blocks(query_all, 0, both_own, both_partner)
    for block in range(MIXED + 1):
        grads[block, at(half, BLOCK)] = own_grads[rows_of(block)]
        grads[block, at(1 - half, BLOCK)] = partner_grads[rows_of(block)]
    clips[at(half, CLIP_ROWS)] = own[ROWS:]
    clips[at(1 - half, CLIP_ROWS)] = partner[ROWS:]
    present = jnp.where(my_group() < groups - 1, 1.0, 0.0)
    older, every, _ = triangles()
    for query_block, block, shape in ((0, 0, older), (0, 1, every), (1, 1, older)):
        query_clip = stats[CLIP_STAT : CLIP_STAT + 1, rows_of(query_block)]
        key_clip = clips[block * CLIP_ROWS : (block + 1) * CLIP_ROWS].astype(f32)[0:1]
        same = jnp.where(key_clip == query_clip, 1.0, 0.0)
        mask[query_block, rows_of(block)] = shape * same * present

    def operands(pair, query_block):
        steps = rows_of(query_block)
        if pair < PAIRS:
            query_rows = doubled(query_all[pair, steps], SCALING)
            return query_rows, doubled(query_all[PAIRS + pair, steps])
        rows = query_all[MIXED, steps]
        query_rows = rows * low_or_high(SCALING, 0.0).astype(bf16)
        return query_rows, rows * low_or_high(0.0, 1.0).astype(bf16)

    def score(pair, query_block, _):
        keys = slice(query_block * BLOCK, WIN)
        query_rows, d_rows = operands(pair, query_block)
        key_block, value_block = (pair, PAIRS + pair) if pair < PAIRS else (MIXED, MIXED)
        scores = times(keys_all[key_block, keys], query_rows, ((1,), (1,)))
        return scores, times(keys_all[value_block, keys], d_rows, ((1,), (1,)))

    def weigh(pair, query_block, values):
        scores, d_weights = values
        row = 2 * pair + query_block
        lanes = slice(0, scores.shape[1])
        scores = hidden(scores, mask[query_block, query_block * BLOCK : WIN])
        weights = jnp.exp(scores - stats[row : row + 1, lanes]).astype(bf16)
        delta = stats[DELTA_STAT + row : DELTA_STAT + row + 1, lanes]
        return weights, (weights.astype(f32) * (d_weights - delta)).astype(bf16)

    def products(pair, query_block, values):
        weights, d_scores = values
        keys = slice(query_block * BLOCK, WIN)
        query_rows, d_rows = operands(pair, query_block)
        dk = times(d_scores, query_rows, ((1,), (0,)))
        dv = times(weights, d_rows, ((1,), (0,)))
        if pair < PAIRS:
            grads[pair, keys] += dk
            grads[PAIRS + pair, keys] += dv
        else:
            grads[MIXED, keys] += dk + dv

    items = [(pair, query_block) for pair in range(PAIRS + 1) for query_block in range(2)]
    staggered(items, score, weigh, products)
    for block in range(MIXED + 1):
        mine[rows_of(block)] = grads[block, at(half, BLOCK)].astype(bf16)
        swap[rows_of(block)] = grads[block, at(1 - half, BLOCK)].astype(bf16)


def next_gradients(groups, *sources):
    return kernel(
        functools.partial(next_kernel, groups),
        "next_gradients",
        [VMEM] * 6,
        [shaped((ROWS, PAIR), bf16)] * 2,
        [
            pltpu.VMEM((MIXED + 1, 2 * BLOCK, PAIR), bf16),
            pltpu.VMEM((MIXED + 1, 2 * BLOCK, PAIR), bf16),
            pltpu.VMEM((2, 2 * BLOCK, BLOCK), f32),
            pltpu.VMEM((MIXED + 1, 2 * BLOCK, PAIR), f32),
            pltpu.VMEM((2 * CLIP_ROWS, PAIR), bf16),
            pltpu.VMEM((STAT_ROWS, 2 * BLOCK), f32),
        ],
        flops=COST_NEXT,
    )(*sources)


def output_kernel(att_own, received, weight, out, full):
    half = my_half()
    full[at(half, HALF)] = att_own[...]
    full[at(1 - half, HALF)] = received[:, :BLOCK]
    out[...] = times(weight[...], full[...], ((1,), (0,))).T.astype(bf16)


def output_rows(att_own, received, weight):
    return kernel(
        output_kernel,
        "output",
        [VMEM] * 3,
        [shaped((BLOCK, weight.shape[0]), bf16), shaped((WIDTH, BLOCK), bf16)],
    )(att_own, received, weight)


def place_keys_kernel(mine, theirs, key_out, value_out, key, value, mixed, sems):
    half = my_half()
    for side, source in ((half, mine), (1 - half, theirs)):
        for pair in range(PAIRS):
            key[:, columns_of(side, pair)] = source[rows_of(pair)]
            value[:, columns_of(side, pair)] = source[rows_of(PAIRS + pair)]
        mixed[side] = source[rows_of(MIXED)].astype(f32)
    shared = slice(SHARED, SHARED + PAIR)
    key[:, shared] = low_or_high(mixed[0], turned(mixed[1])).astype(bf16)
    value[:, shared] = low_or_high(turned(mixed[0]), mixed[1]).astype(bf16)
    pairs = ((key, key_out), (value, value_out))
    copies = [pltpu.make_async_copy(a, b, sems.at[n]) for n, (a, b) in enumerate(pairs)]
    for copy in copies:
        copy.start()
    for copy in copies:
        copy.wait()


def place_keys(*sources):
    wide = pltpu.VMEM((BLOCK, WIDTH), bf16)
    mixed = pltpu.VMEM((2, BLOCK, PAIR), f32)
    return kernel(
        place_keys_kernel,
        "place_keys",
        [VMEM] * 2,
        [shaped((BLOCK, WIDTH), bf16)] * 2,
        [wide, wide, mixed, pltpu.SemaphoreType.DMA((2,))],
        HBM,
        COST_KEYS,
    )(*sources)


def place_kernel(dq_mine, received, stays, first, second, query_out, weight_out, dq_all, query, both, sems):
    half = my_half()
    rows = first.shape[0]
    moves = [(both, weight_out), (query, query_out)]
    copies = [pltpu.make_async_copy(a, b, sems.at[n]) for n, (a, b) in enumerate(moves)]
    both[span(half * rows, rows, 16)] = first[...].astype(f32)

    @pl.when(lax.axis_index("dp") == 3 * half)
    def _():
        both[span(half * rows, rows, 16)] = stays[...].astype(f32)

    both[span((1 - half) * rows, rows, 16)] = second[...].astype(f32)
    copies[0].start()
    dq_all[at(half, HALF)] = dq_mine[...]
    dq_all[at(1 - half, HALF)] = received[:, BLOCK:]
    for block in range(WIDTH // PAIR):
        query[:, block * PAIR : (block + 1) * PAIR] = dq_all[rows_of(block)].T
    copies[1].start()
    for copy in copies:
        copy.wait()


def place(*sources):
    rows, lanes = sources[-1].shape
    query, weight = kernel(
        place_kernel,
        "place",
        [VMEM] * 5,
        [shaped((BLOCK, WIDTH), bf16), shaped((2 * rows, lanes), f32)],
        [
            pltpu.VMEM((WIDTH, BLOCK), bf16),
            pltpu.VMEM((BLOCK, WIDTH), bf16),
            pltpu.VMEM((2 * rows, lanes), f32),
            pltpu.SemaphoreType.DMA((2,)),
        ],
        HBM,
    )(*sources)
    return query, weight.T


def weight_kernel(count, *refs):
    pieces, cots, products = refs[:count], refs[count : 2 * count], refs[-1]
    half = my_half()
    att = jnp.concatenate([piece[:, at(half, BLOCK)] for piece in pieces], axis=1)
    products[...] = times(att, jnp.concatenate([cot[...] for cot in cots], axis=0), ((1,), (0,)))


def weight_products(pieces, cots):
    return kernel(
        functools.partial(weight_kernel, len(pieces)),
        "weight_products",
        [VMEM] * (2 * len(pieces)),
        [shaped((pieces[0].shape[0], cots[0].shape[1]), f32)],
        flops=COST_FIRST,
    )(*pieces, *cots)[0]


def weight_rest_kernel(count, products, *refs):
    pieces, cots = refs[:count], refs[count : 2 * count]
    kept, *sent = refs[2 * count :]
    total = sent.pop()
    half = my_half()
    att = jnp.concatenate([piece[:, at(1 - half, BLOCK)] for piece in pieces], axis=1)
    cot = jnp.concatenate([cot[...] for cot in cots], axis=0)
    total[...] = products[...] + times(att, cot, ((1,), (0,)))
    group = my_group()
    lanes = kept.shape[1]
    kept[...] = total[:, at(group, lanes)]
    for number, out in enumerate(sent):
        target = jnp.bitwise_xor(group, number + 1)
        out[...] = total[:, at(target, lanes)].astype(bf16)


def weight_rest(products, pieces, cots, groups):
    rows, outs = products.shape
    part = (rows, outs // groups)
    return kernel(
        functools.partial(weight_rest_kernel, len(pieces)),
        "weight_rest",
        [VMEM] * (1 + 2 * len(pieces)),
        [shaped(part, f32)] + [shaped(part, bf16)] * (groups - 1),
        [pltpu.VMEM((rows, outs), f32)],
    )(products, *pieces, *cots)


def weight_sum_kernel(kept, *rest):
    received, (first, second, total) = rest[:-3], rest[-3:]
    value = kept[...]
    for part in received:
        value = value + part[...].astype(f32)
    total[...] = value
    lanes = first.shape[1]
    odd = jnp.bitwise_and(lax.axis_index("dp"), 1)
    first[...] = total[:, at(odd, lanes)].astype(bf16)
    second[...] = total[:, at(1 - odd, lanes)].astype(bf16)


def weight_sum(kept, received):
    rows, lanes = kept.shape
    return kernel(
        weight_sum_kernel,
        "weight_sum",
        [VMEM] * (1 + len(received)),
        [shaped((rows, lanes // 2), bf16)] * 2,
        [pltpu.VMEM((rows, lanes), f32)],
        flops=COST_SUM,
    )(kept, *received)


def swapped(value, axis, bits):
    count = lax.axis_size(axis)
    return lax.ppermute(value, axis, [(source, source ^ bits) for source in range(count)])


def rotated(value, axis, steps):
    count = lax.axis_size(axis)
    return lax.ppermute(
        value, axis, [(source, (source + steps) % count) for source in range(count)]
    )


def moved(value, axis, steps):
    count = lax.axis_size(axis)
    first, last = (max(0, -steps), min(count, count - steps))
    return lax.ppermute(value, axis, [(source, source + steps) for source in range(first, last)])


def placed(value, flip):
    lanes = lax.axis_size("ctx")
    moves = []
    for source in range(lax.axis_size("dp")):
        for index in range(lanes):
            group, half = index // 2, index % 2
            target_half = (source % 2) ^ flip
            target = 2 * half + source // 2
            if (target, target_half) == (source, half):
                target, target_half = 3 - target, 1 - target_half
            moves.append((source * lanes + index, target * lanes + 2 * group + target_half))
    return lax.ppermute(value, ("dp", "ctx"), moves)


def after(*values):
    return lax.optimization_barrier(values)


def per_device(queries, key_states, value_states, out_cotangent, out_weight, block_clip):
    sequences = lax.axis_size("dp")
    groups = lax.axis_size("ctx") // 2
    short = sequences == 4 and groups in (2, 4)
    cotangent = out_cotangent[0]

    swap_kv, own, swap_query, query = pack(
        block_clip, queries[0], key_states[0], value_states[0]
    )
    swap_kv, cot_early = after(swap_kv, cotangent)
    partner = swapped(swap_kv, "ctx", 1)
    halo = rotated(own, "ctx", 2)
    both_own, d_turned_own, weight = own_cotangents(cotangent, out_weight, query)
    cots = [cotangent]
    if short:
        cots += [swapped(cot_early, "dp", n) for n in (1, 2)]

    partner, both_own, swap_query, cot_late = after(partner, both_own, swap_query, cotangent)
    cot_partner = swapped(cot_late, "ctx", 1)
    halo_other = rotated(partner, "ctx", 2)
    query_partner = swapped(swap_query, "ctx", 1)
    halo, both_own, *cots = after(halo, both_own, *cots)
    next_own = moved(both_own, "ctx", -2)
    if short:
        cots.append(swapped(cots[2], "dp", 1))
    keys_all, query_all, mask, clip_row = gathered(
        own, partner, halo, halo_other, query, query_partner
    )
    weights, single, totals, att, att_own, att_swap, *pieces = forward(
        4 if short else 0, keys_all, query_all, mask, clip_row
    )
    if short:
        cot_across = swapped(cot_partner, "dp", 2)
    weights, cot_partner, *rest = after(weights, cot_partner, *pieces, *cots)
    pieces, cots = rest[: len(pieces)], rest[len(pieces) :]

    if short:
        pieces[1:] = [swapped(pieces[n], "dp", n) for n in (1, 2, 3)]
    both_partner, stats = cotangents(
        cot_partner, weight, query_partner, att, d_turned_own, totals
    )
    both_partner, next_own = after(both_partner, next_own)
    next_partner = rotated(both_partner, "ctx", -2)
    dq_own, swap, own_grads, partner_grads = own_gradients(
        keys_all, both_own, both_partner, weights, single, stats, att_swap
    )
    own_grads, swap, *pieces = after(own_grads, swap, *pieces)

    if short:
        own_grads, cot_partner, cot_across = after(own_grads, cot_partner, cot_across)
        later = [cot_partner, swapped(cot_partner, "dp", 1), cot_across]
        later.append(swapped(cot_across, "dp", 1))
        products = weight_products(pieces, cots)
        products, *later = after(products, *later)
        kept, *sent = weight_rest(products, pieces, later, groups)
        arrived = [swapped(part, "ctx", 2 * (n + 1)) for n, part in enumerate(sent)]
        kept, own_grads = after(kept, own_grads)
    received = swapped(swap, "ctx", 1)
    kv_own, kv_swap = next_gradients(
        groups, own, partner, next_own, next_partner, own_grads, partner_grads
    )
    kv_rest = swapped(kv_swap, "ctx", 1)
    kv_own, received = after(kv_own, received)
    sublayer_out, att_full = output_rows(att_own, received, weight)
    if short:
        kept, kv_own, sublayer_out, *arrived = after(kept, kv_own, sublayer_out, *arrived)
        stays, second = weight_sum(kept, arrived)
        first, second = placed(stays, 0), placed(second, 1)
    if not short:
        product = lax.dot_general(
            cotangent, att_full, (((0,), (1,)), ((), ())), preferred_element_type=f32
        ).astype(bf16)
        sequence_grad = lax.psum_scatter(product, "ctx", scatter_dimension=0, tiled=True)
        weight_grad = lax.psum_scatter(
            sequence_grad.astype(f32), "dp", scatter_dimension=1, tiled=True
        )
        stays = first = second = jnp.zeros((16, 128), bf16)
    key_grad, value_grad = place_keys(kv_own, kv_rest)
    dq_own, key_grad = after(dq_own, key_grad)
    query_grad, placed_weight = place(dq_own, received, stays, first, second)
    if short:
        weight_grad = placed_weight
    return (
        sublayer_out[None],
        query_grad[None],
        key_grad[None],
        value_grad[None],
        weight_grad,
    )


def solution(mesh):
    return jax.shard_map(
        per_device,
        mesh=mesh,
        in_specs=(
            P("dp", "ctx", None),
            P("dp", "ctx", None),
            P("dp", "ctx", None),
            P("dp", "ctx", None),
            P(),
            P("dp", "ctx"),
        ),
        out_specs=(
            P("dp", "ctx", None),
            P("dp", "ctx", None),
            P("dp", "ctx", None),
            P("dp", "ctx", None),
            P("ctx", "dp"),
        ),
        check_vma=False,
    )
```

```python
import functools
import math

import jax
import jax.numpy as jnp
from jax import lax
from jax.experimental import pallas as pl
from jax.experimental.pallas import tpu as pltpu
from jax.sharding import PartitionSpec as P

HEADS = 18
HDIM = 64
BLOCK = 128
WIN = 256
PAIR = 2 * HDIM
WIDTH = HEADS * HDIM
HALF = WIDTH // 2
PAIRS = HEADS // 4
SHARED = PAIRS * PAIR
MIXED = 2 * PAIRS
ROWS = (MIXED + 1) * BLOCK
FIRST_BLOCKS = (0, 2, 5, 7)
HEAD_STARTS = (0, 128, 320, 448)
SINGLE_START = 256
PIECE_ROWS = 160
ATT_ROWS = HEAD_STARTS[-1] + PIECE_ROWS
SEGMENTS = (
    ((0, 0, 128, 0), (0, 128, 32, 256), (1, 0, 128, 128)),
    ((0, 0, 96, 0), (0, 96, 64, 224), (1, 0, 128, 96)),
    ((0, 0, 128, 64), (1, 0, 64, 0), (1, 64, 96, 192)),
    ((0, 0, 128, 32), (1, 0, 32, 0), (1, 32, 128, 160)),
)
CLIP_ROWS = 16
CLIP_STAT = 2 * PAIRS + 2
DELTA_STAT = CLIP_STAT + 2
STAT_ROWS = 24
SENT_ROWS = ROWS + 6 * STAT_ROWS
CHUNKS = 4
SCALING = 1.0 / math.sqrt(HDIM)
COST_GATHER = 2_000_000_000
COST_KEYS = 1_000_000
COST_FIRST = 2_000_000_000
COST_NEXT = 4_000_000_000
COST_SUM = 2_000_000_000
VMEM_LIMIT = 24 * 1024 * 1024

big_negative = -1e30
bf16 = jnp.bfloat16
f32 = jnp.float32

VMEM = pl.BlockSpec(memory_space=pltpu.VMEM)
HBM = pl.BlockSpec(memory_space=pltpu.HBM)


def shaped(shape, dtype):
    return jax.ShapeDtypeStruct(shape, dtype)


def kernel(body, name, ins, outs, scratch=(), spaces=None, flops=1_000_000):
    return pl.pallas_call(
        body,
        out_shape=tuple(outs),
        in_specs=list(ins),
        out_specs=spaces or (VMEM,) * len(outs),
        scratch_shapes=list(scratch),
        compiler_params=pltpu.CompilerParams(vmem_limit_bytes=VMEM_LIMIT),
        cost_estimate=pl.CostEstimate(flops=flops, bytes_accessed=10_000, transcendentals=0),
        name=name,
    )


def in_hbm(value):
    return pltpu.with_memory_space_constraint(value, pltpu.HBM)


def my_half():
    return jnp.bitwise_and(lax.axis_index("ctx"), 1)


def my_group():
    return jnp.right_shift(lax.axis_index("ctx"), 1)


def at(index, size):
    return pl.ds(pl.multiple_of(index * size, size), size)


def span(start, size, unit):
    return pl.ds(pl.multiple_of(start, unit), size)


def rows_of(block):
    return slice(block * BLOCK, (block + 1) * BLOCK)


def columns_of(half, pair):
    return span((FIRST_BLOCKS[pair] + half) * PAIR, PAIR, PAIR)


def head_rows(pair):
    return slice(HEAD_STARTS[pair], HEAD_STARTS[pair] + PAIR)


def single_rows():
    return slice(SINGLE_START, SINGLE_START + HDIM)


def times(a, b, dims):
    return lax.dot_general(a, b, (dims, ((), ())), preferred_element_type=f32)


def is_low():
    return lax.broadcasted_iota(jnp.int32, (1, PAIR), 1) < HDIM


def low_or_high(low_value, high_value):
    return jnp.where(is_low(), low_value, high_value)


def turned(value):
    return pltpu.roll(value, HDIM, 1)


def pack_kernel(clip, query, key, value, swap_kv, own_kv, swap_query, own_query, *scratch):
    query_all, key_all, value_all, mixed, single, sems = scratch
    half = my_half()
    pairs = ((key, key_all), (value, value_all), (query, query_all))
    copies = [pltpu.make_async_copy(a, b, sems.at[n]) for n, (a, b) in enumerate(pairs)]
    for copy in copies:
        copy.start()
    shared = slice(SHARED, SHARED + PAIR)
    for copy in copies:
        copy.wait()
    clip_rows = jnp.broadcast_to(clip[...].astype(f32), (CLIP_ROWS, PAIR)).astype(bf16)
    for side, target in ((1 - half, swap_kv), (half, own_kv)):
        for pair in range(PAIRS):
            target[rows_of(pair)] = key_all[:, columns_of(side, pair)]
            target[rows_of(PAIRS + pair)] = value_all[:, columns_of(side, pair)]
        target[ROWS:] = clip_rows
    key_shared = key_all[:, shared].astype(f32)
    value_shared = value_all[:, shared].astype(f32)
    mixed[0] = low_or_high(key_shared, turned(value_shared)).astype(bf16)
    mixed[1] = low_or_high(turned(key_shared), value_shared).astype(bf16)
    swap_kv[rows_of(MIXED)] = mixed[1 - half]
    own_kv[rows_of(MIXED)] = mixed[half]
    for pair in range(PAIRS):
        swap_query[rows_of(pair)] = query_all[:, columns_of(1 - half, pair)]
        own_query[rows_of(pair)] = query_all[:, columns_of(half, pair)]
    query_shared = query_all[:, shared].astype(f32)
    single[0] = low_or_high(query_shared, 0.0)
    single[1] = low_or_high(turned(query_shared), 0.0)
    own_query[rows_of(PAIRS)] = single[half].astype(bf16)
    theirs = single[1 - half]
    swap_query[SHARED:] = low_or_high(theirs[:HDIM], turned(theirs[HDIM:])).astype(bf16)


def pack(clip, query, key, value):
    wide = pltpu.VMEM((BLOCK, WIDTH), bf16)
    return kernel(
        pack_kernel,
        "pack",
        [VMEM, HBM, HBM, HBM],
        [shaped((ROWS + CLIP_ROWS, PAIR), bf16)] * 2
        + [shaped((HALF, PAIR), bf16), shaped((SHARED + PAIR, PAIR), bf16)],
        [
            wide,
            wide,
            wide,
            pltpu.VMEM((2, BLOCK, PAIR), bf16),
            pltpu.VMEM((2, BLOCK, PAIR), f32),
            pltpu.SemaphoreType.DMA((3,)),
        ],
    )(clip, in_hbm(query), in_hbm(key), in_hbm(value))


def unpacked_single(packed):
    packed = packed.astype(f32)
    top, bottom = low_or_high(packed, 0.0), low_or_high(turned(packed), 0.0)
    return jnp.concatenate([top, bottom], axis=0).astype(bf16)


def join_query(target, d_turned, single, query, query_single, d_pairs, d_shared):
    half = my_half()
    for pair in range(PAIRS):
        d_pair = d_pairs[:, pair * PAIR : (pair + 1) * PAIR].astype(bf16)
        target[rows_of(pair)] = query[rows_of(pair)]
        target[rows_of(PAIRS + pair)] = d_pair
        d_turned[head_rows(pair)] = d_pair.T
    single[0] = low_or_high(0.0, turned(d_shared)).astype(bf16)
    single[1] = low_or_high(0.0, d_shared).astype(bf16)
    d_single = single[half]
    target[rows_of(MIXED)] = query_single + d_single
    d_turned[single_rows()] = d_single.T[HDIM:]


def own_cotangent_kernel(cotangent, weight, query, both, d_turned, kept, rows, single, sems):
    half = my_half()
    chunk = rows.shape[1] // CHUNKS
    copies = [pltpu.make_async_copy(cotangent, rows, sems.at[CHUNKS])]
    for number in range(CHUNKS):
        part = pl.ds(number * chunk, chunk)
        copies.append(pltpu.make_async_copy(weight.at[part], kept.at[part], sems.at[number]))
    for copy in copies:
        copy.start()
    copies[0].wait()
    pairs = shared = None
    for number in range(CHUNKS):
        copies[number + 1].wait()
        part = slice(number * chunk, (number + 1) * chunk)
        columns = [kept[part, columns_of(half, pair)] for pair in range(PAIRS)]
        wide = times(rows[:, part], jnp.concatenate(columns, axis=1), ((1,), (0,)))
        narrow = times(rows[:, part], kept[part, SHARED : SHARED + PAIR], ((1,), (0,)))
        pairs = wide if pairs is None else pairs + wide
        shared = narrow if shared is None else shared + narrow
    join_query(both, d_turned, single, query, query[rows_of(PAIRS)], pairs, shared)


def own_cotangents(cotangent, weight, query):
    return kernel(
        own_cotangent_kernel,
        "own_cotangents",
        [HBM, HBM, VMEM],
        [shaped((ROWS, PAIR), bf16), shaped((HALF, BLOCK), bf16), shaped(weight.shape, bf16)],
        [
            pltpu.VMEM(cotangent.shape, bf16),
            pltpu.VMEM((2, BLOCK, PAIR), bf16),
            pltpu.SemaphoreType.DMA((CHUNKS + 1,)),
        ],
    )(in_hbm(cotangent), in_hbm(weight), query)


def cotangent_kernel(
    cotangent, weight, query, att, d_turned_own, totals, both, stats, d_turned, d_all, single
):
    half = my_half()
    rows = cotangent[...]
    columns = [weight[:, columns_of(half, pair)] for pair in range(PAIRS)]
    pairs = times(rows, jnp.concatenate(columns, axis=1), ((1,), (0,)))
    shared = times(rows, weight[:, SHARED : SHARED + PAIR], ((1,), (0,)))
    query_single = unpacked_single(query[SHARED:])
    join_query(both, d_turned, single, query, query_single, pairs, shared)
    d_all[:, at(half, BLOCK)] = d_turned_own[...]
    d_all[:, at(1 - half, BLOCK)] = d_turned[...]
    stats[...] = totals[...]
    for query_block in range(2):
        steps = rows_of(query_block)
        for pair in range(PAIRS):
            which = head_rows(pair)
            dots = d_all[which, steps].astype(f32) * att[which, steps].astype(f32)
            row = DELTA_STAT + 2 * pair + query_block
            stats[row : row + 1, :BLOCK] = jnp.sum(dots[:HDIM], axis=0, keepdims=True)
            stats[row : row + 1, BLOCK:] = jnp.sum(dots[HDIM:], axis=0, keepdims=True)
        which = single_rows()
        dots = d_all[which, steps].astype(f32) * att[which, steps].astype(f32)
        row = DELTA_STAT + 2 * PAIRS + query_block
        stats[row : row + 1, :BLOCK] = jnp.sum(dots, axis=0, keepdims=True)
    rest = jnp.concatenate([stats[:, :BLOCK], stats[:, BLOCK:]], axis=0)
    for number in range(3):
        begin = ROWS + 2 * STAT_ROWS * number
        part = rest.astype(bf16)
        both[begin : begin + 2 * STAT_ROWS] = part
        rest = rest - part.astype(f32)


def stats_of(both):
    parts = []
    for number in range(3):
        begin = ROWS + 2 * STAT_ROWS * number
        parts.append(both[begin : begin + 2 * STAT_ROWS].astype(f32))
    total = (parts[0] + parts[1]) + parts[2]
    return jnp.concatenate([total[:STAT_ROWS], total[STAT_ROWS:]], axis=1)


def cotangents(cotangent, weight, query, att, d_turned_own, totals):
    return kernel(
        cotangent_kernel,
        "cotangents",
        [VMEM] * 6,
        [shaped((SENT_ROWS, PAIR), bf16), shaped((STAT_ROWS, 2 * BLOCK), f32)],
        [
            pltpu.VMEM((HALF, BLOCK), bf16),
            pltpu.VMEM((HALF, 2 * BLOCK), bf16),
            pltpu.VMEM((2, BLOCK, PAIR), bf16),
        ],
    )(cotangent, weight, query, att, d_turned_own, totals)


def gather_blocks(target, offset, own, partner):
    half = my_half()
    for block in range(target.shape[0]):
        target[block, at(offset + half, BLOCK)] = own[rows_of(block)]
        target[block, at(offset + 1 - half, BLOCK)] = partner[rows_of(block)]


def doubled(rows, factor=1.0):
    first = low_or_high(factor, 0.0).astype(bf16)
    second = low_or_high(0.0, factor).astype(bf16)
    return jnp.concatenate([rows * first, rows * second], axis=0)


def diagonal(pair):
    return jnp.concatenate([pair[:HDIM, :BLOCK], pair[HDIM:, BLOCK:]], axis=0)


def triangles():
    row = lax.broadcasted_iota(jnp.int32, (BLOCK, BLOCK), 0)
    lane = lax.broadcasted_iota(jnp.int32, (BLOCK, BLOCK), 1)
    older = jnp.where(row > lane, 1.0, 0.0)
    return older, jnp.ones((BLOCK, BLOCK), f32), 1.0 - older


def hidden(scores, visible):
    if scores.shape[1] > visible.shape[1]:
        visible = jnp.concatenate([visible, visible], axis=1)
    return jnp.where(visible > 0.5, scores, big_negative)


def gather_kernel(
    own, partner, halo, halo_other, query_own, query_partner, keys_all, query_all, mask, clip_row, clips
):
    half = my_half()
    gather_blocks(keys_all, 0, halo, halo_other)
    gather_blocks(keys_all, 2, own, partner)
    for pair in range(PAIRS):
        query_all[pair, at(half, BLOCK)] = query_own[rows_of(pair)]
        query_all[pair, at(1 - half, BLOCK)] = query_partner[rows_of(pair)]
    query_all[PAIRS, at(half, BLOCK)] = query_own[rows_of(PAIRS)]
    query_all[PAIRS, at(1 - half, BLOCK)] = unpacked_single(query_partner[SHARED:])
    for offset, mine, theirs in ((0, halo, halo_other), (2, own, partner)):
        clips[at(offset + half, CLIP_ROWS)] = mine[ROWS:]
        clips[at(offset + 1 - half, CLIP_ROWS)] = theirs[ROWS:]

    def clip_of(block):
        return clips[block * CLIP_ROWS : (block + 1) * CLIP_ROWS].astype(f32)[0:1]

    for query_block in range(2):
        query_clip = clip_of(2 + query_block)
        for step, shape in enumerate(triangles()):
            block = query_block + step
            same = jnp.where(clip_of(block) == query_clip, 1.0, 0.0)
            present = jnp.where(2 * my_group() - 2 + block >= 0, 1.0, 0.0)
            mask[query_block, rows_of(step)] = shape * same * present
        clip_row[:, rows_of(query_block)] = query_clip


def gathered(*sources):
    return kernel(
        gather_kernel,
        "gathered",
        [VMEM] * 6,
        [
            shaped((MIXED + 1, 4 * BLOCK, PAIR), bf16),
            shaped((PAIRS + 1, 2 * BLOCK, PAIR), bf16),
            shaped((2, WIN + BLOCK, BLOCK), f32),
            shaped((1, 2 * BLOCK), f32),
        ],
        [pltpu.VMEM((4 * CLIP_ROWS, PAIR), bf16)],
        flops=COST_GATHER,
    )(*sources)


def staggered(items, *stages):
    values = [None] * len(items)
    for step in range(len(items) + 2 * len(stages) - 2):
        for number, stage in enumerate(stages):
            index = step - 2 * number
            if 0 <= index < len(items):
                values[index] = stage(*items[index], values[index])


def forward_kernel(
    pieces_wanted,
    keys_all,
    query_all,
    mask,
    clip_row,
    weights_out,
    single_out,
    totals,
    att,
    att_own,
    att_swap,
    *pieces,
):
    half = my_half()
    totals[CLIP_STAT : CLIP_STAT + 1] = clip_row[...]

    def softmax(scores, row):
        lanes = slice(0, scores.shape[1])
        maximum = jnp.max(scores, axis=0, keepdims=True)
        powers = jnp.exp(scores - maximum)
        total = jnp.sum(powers, axis=0, keepdims=True)
        totals[row : row + 1, lanes] = maximum + jnp.log(total)
        return (powers * (1.0 / total)).astype(bf16)

    def keys_of(query_block):
        return slice(query_block * BLOCK, query_block * BLOCK + WIN + BLOCK)

    def score(pair, query_block, _):
        rows = query_all[pair, rows_of(query_block)]
        if pair < PAIRS:
            key_rows, rows = keys_all[pair, keys_of(query_block)], doubled(rows, SCALING)
        else:
            key_rows = keys_all[MIXED, keys_of(query_block)]
            rows = rows * low_or_high(SCALING, 0.0).astype(bf16)
        return times(key_rows, rows, ((1,), (1,)))

    def weigh(pair, query_block, scores):
        return softmax(hidden(scores, mask[query_block]), 2 * pair + query_block)

    def mix(pair, query_block, weights):
        steps = rows_of(query_block)
        if pair < PAIRS:
            weights_out[pair, query_block] = weights
            mixed = times(keys_all[PAIRS + pair, keys_of(query_block)], weights, ((0,), (0,)))
            att[head_rows(pair), steps] = diagonal(mixed).astype(bf16)
        else:
            single_out[query_block] = weights
            mixed = times(keys_all[MIXED, keys_of(query_block)], weights, ((0,), (0,)))
            att[single_rows(), steps] = mixed[HDIM:].astype(bf16)

    items = [(pair, query_block) for pair in range(PAIRS + 1) for query_block in range(2)]
    staggered(items, score, weigh, mix)

    att[HALF:] = jnp.zeros((ATT_ROWS - HALF, 2 * BLOCK), bf16)
    att_own[...] = att[:HALF, at(half, BLOCK)]
    att_swap[...] = att[:HALF, at(1 - half, BLOCK)]
    for number, piece in enumerate(pieces):
        target = jnp.bitwise_xor(lax.axis_index("dp"), number)
        late = 32 * jnp.maximum(target - 2, 0)
        begin = jnp.where(half == 0, 160 * target - late, 128 * target + late)
        piece[...] = att[span(begin, PIECE_ROWS, 32), :]


def forward(pieces_wanted, *sources):
    piece = (PIECE_ROWS, 2 * BLOCK)
    return kernel(
        functools.partial(forward_kernel, pieces_wanted),
        "forward",
        [VMEM] * 4,
        [
            shaped((PAIRS, 2, WIN + BLOCK, 2 * BLOCK), bf16),
            shaped((2, WIN + BLOCK, BLOCK), bf16),
            shaped((STAT_ROWS, 2 * BLOCK), f32),
            shaped((ATT_ROWS, 2 * BLOCK), bf16),
            shaped((HALF, BLOCK), bf16),
            shaped((HALF, BLOCK), bf16),
        ]
        + [shaped(piece, bf16)] * pieces_wanted,
    )(*sources)


def own_kernel(
    keys_all,
    both_own,
    both_partner,
    weights_in,
    single_in,
    stats,
    att_swap,
    dq_own,
    swap,
    own_grads,
    partner_grads,
    query_all,
    dq_all,
    grads,
):
    half = my_half()
    gather_blocks(query_all, 0, both_own, both_partner)

    def delta_of(row, lanes):
        return stats[DELTA_STAT + row : DELTA_STAT + row + 1, :lanes]

    def accumulate(block, query_block, value):
        if query_block == 1:
            grads[block] = value
        else:
            grads[block, :BLOCK] += value

    def keys_of(query_block):
        return slice(query_block * BLOCK, query_block * BLOCK + WIN + BLOCK)

    def operands(pair, query_block):
        steps = rows_of(query_block)
        if pair < PAIRS:
            query_rows = doubled(query_all[pair, steps], SCALING)
            return query_rows, doubled(query_all[PAIRS + pair, steps]), weights_in[pair, query_block]
        rows = query_all[MIXED, steps]
        query_rows = rows * low_or_high(SCALING, 0.0).astype(bf16)
        d_rows = rows * low_or_high(0.0, 1.0).astype(bf16)
        return query_rows, d_rows, single_in[query_block]

    def d_weights_of(pair, query_block, _):
        block = PAIRS + pair if pair < PAIRS else MIXED
        _, d_rows, _ = operands(pair, query_block)
        return times(keys_all[block, keys_of(query_block)], d_rows, ((1,), (1,)))

    def d_scores_of(pair, query_block, d_weights):
        _, _, weights = operands(pair, query_block)
        delta = delta_of(2 * pair + query_block, d_weights.shape[1])
        return (weights.astype(f32) * (d_weights - delta)).astype(bf16)

    def products(pair, query_block, d_scores):
        query_rows, d_rows, weights = operands(pair, query_block)
        mine = slice(WIN - query_block * BLOCK, WIN + BLOCK)
        steps = rows_of(query_block)
        block = pair if pair < PAIRS else MIXED
        dq = times(keys_all[block, keys_of(query_block)], d_scores, ((0,), (0,)))
        dk = times(d_scores[mine], query_rows, ((1,), (0,)))
        dv = times(weights[mine], d_rows, ((1,), (0,)))
        if pair < PAIRS:
            dq_all[head_rows(pair), steps] = (diagonal(dq) * SCALING).astype(bf16)
            accumulate(pair, query_block, dk)
            accumulate(PAIRS + pair, query_block, dv)
        else:
            dq_all[single_rows(), steps] = (dq[:HDIM] * SCALING).astype(bf16)
            accumulate(MIXED, query_block, dk + dv)

    items = [(pair, query_block) for pair in range(PAIRS + 1) for query_block in (1, 0)]
    staggered(items, d_weights_of, d_scores_of, products)
    dq_own[...] = dq_all[:, at(half, BLOCK)]
    swap[:, :BLOCK] = att_swap[...]
    swap[:, BLOCK:] = dq_all[:, at(1 - half, BLOCK)]
    for block in range(MIXED + 1):
        own_grads[rows_of(block)] = grads[block, at(half, BLOCK)]
        partner_grads[rows_of(block)] = grads[block, at(1 - half, BLOCK)]


def own_gradients(*sources):
    return kernel(
        own_kernel,
        "own_gradients",
        [VMEM] * 7,
        [shaped((HALF, BLOCK), bf16), shaped((HALF, 2 * BLOCK), bf16)]
        + [shaped((ROWS, PAIR), f32)] * 2,
        [
            pltpu.VMEM((MIXED + 1, 2 * BLOCK, PAIR), bf16),
            pltpu.VMEM((HALF, 2 * BLOCK), bf16),
            pltpu.VMEM((MIXED + 1, 2 * BLOCK, PAIR), f32),
        ],
    )(*sources)


def next_kernel(
    groups,
    own,
    partner,
    both_own,
    both_partner,
    own_grads,
    partner_grads,
    mine,
    swap,
    keys_all,
    query_all,
    mask,
    grads,
    clips,
    stats,
):
    half = my_half()
    stats[...] = stats_of(both_partner)
    gather_blocks(keys_all, 0, own, partner)
    gather_blocks(query_all, 0, both_own, both_partner)
    for block in range(MIXED + 1):
        grads[block, at(half, BLOCK)] = own_grads[rows_of(block)]
        grads[block, at(1 - half, BLOCK)] = partner_grads[rows_of(block)]
    clips[at(half, CLIP_ROWS)] = own[ROWS:]
    clips[at(1 - half, CLIP_ROWS)] = partner[ROWS:]
    present = jnp.where(my_group() < groups - 1, 1.0, 0.0)
    older, every, _ = triangles()
    for query_block, block, shape in ((0, 0, older), (0, 1, every), (1, 1, older)):
        query_clip = stats[CLIP_STAT : CLIP_STAT + 1, rows_of(query_block)]
        key_clip = clips[block * CLIP_ROWS : (block + 1) * CLIP_ROWS].astype(f32)[0:1]
        same = jnp.where(key_clip == query_clip, 1.0, 0.0)
        mask[query_block, rows_of(block)] = shape * same * present

    def operands(pair, query_block):
        steps = rows_of(query_block)
        if pair < PAIRS:
            query_rows = doubled(query_all[pair, steps], SCALING)
            return query_rows, doubled(query_all[PAIRS + pair, steps])
        rows = query_all[MIXED, steps]
        query_rows = rows * low_or_high(SCALING, 0.0).astype(bf16)
        return query_rows, rows * low_or_high(0.0, 1.0).astype(bf16)

    def score(pair, query_block, _):
        keys = slice(query_block * BLOCK, WIN)
        query_rows, d_rows = operands(pair, query_block)
        key_block, value_block = (pair, PAIRS + pair) if pair < PAIRS else (MIXED, MIXED)
        scores = times(keys_all[key_block, keys], query_rows, ((1,), (1,)))
        return scores, times(keys_all[value_block, keys], d_rows, ((1,), (1,)))

    def weigh(pair, query_block, values):
        scores, d_weights = values
        row = 2 * pair + query_block
        lanes = slice(0, scores.shape[1])
        scores = hidden(scores, mask[query_block, query_block * BLOCK : WIN])
        weights = jnp.exp(scores - stats[row : row + 1, lanes]).astype(bf16)
        delta = stats[DELTA_STAT + row : DELTA_STAT + row + 1, lanes]
        return weights, (weights.astype(f32) * (d_weights - delta)).astype(bf16)

    def products(pair, query_block, values):
        weights, d_scores = values
        keys = slice(query_block * BLOCK, WIN)
        query_rows, d_rows = operands(pair, query_block)
        dk = times(d_scores, query_rows, ((1,), (0,)))
        dv = times(weights, d_rows, ((1,), (0,)))
        if pair < PAIRS:
            grads[pair, keys] += dk
            grads[PAIRS + pair, keys] += dv
        else:
            grads[MIXED, keys] += dk + dv

    items = [(pair, query_block) for pair in range(PAIRS + 1) for query_block in range(2)]
    staggered(items, score, weigh, products)
    for block in range(MIXED + 1):
        mine[rows_of(block)] = grads[block, at(half, BLOCK)].astype(bf16)
        swap[rows_of(block)] = grads[block, at(1 - half, BLOCK)].astype(bf16)


def next_gradients(groups, *sources):
    return kernel(
        functools.partial(next_kernel, groups),
        "next_gradients",
        [VMEM] * 6,
        [shaped((ROWS, PAIR), bf16)] * 2,
        [
            pltpu.VMEM((MIXED + 1, 2 * BLOCK, PAIR), bf16),
            pltpu.VMEM((MIXED + 1, 2 * BLOCK, PAIR), bf16),
            pltpu.VMEM((2, 2 * BLOCK, BLOCK), f32),
            pltpu.VMEM((MIXED + 1, 2 * BLOCK, PAIR), f32),
            pltpu.VMEM((2 * CLIP_ROWS, PAIR), bf16),
            pltpu.VMEM((STAT_ROWS, 2 * BLOCK), f32),
        ],
        flops=COST_NEXT,
    )(*sources)


def join_halves(full, halves, mine, theirs):
    half = my_half()
    halves[half] = mine
    halves[1 - half] = theirs
    for side in range(2):
        for pair in range(PAIRS):
            full[rows_of(FIRST_BLOCKS[pair] + side)] = halves[side, head_rows(pair)]
        begin = SHARED + side * HDIM
        full[begin : begin + HDIM] = halves[side, single_rows()]


def output_kernel(att_own, received, dq_mine, weight, out, query_out, full, dq_all, halves, query, sem):
    join_halves(dq_all, halves, dq_mine[...], received[:, BLOCK:])
    for block in range(WIDTH // PAIR):
        query[:, block * PAIR : (block + 1) * PAIR] = dq_all[rows_of(block)].T
    copy = pltpu.make_async_copy(query, query_out, sem)
    copy.start()
    join_halves(full, halves, att_own[...], received[:, :BLOCK])
    out[...] = times(weight[...], full[...], ((1,), (0,))).T.astype(bf16)
    copy.wait()


def output_rows(att_own, received, dq_mine, weight):
    return kernel(
        output_kernel,
        "output",
        [VMEM] * 4,
        [
            shaped((BLOCK, weight.shape[0]), bf16),
            shaped((BLOCK, WIDTH), bf16),
            shaped((WIDTH, BLOCK), bf16),
        ],
        [
            pltpu.VMEM((WIDTH, BLOCK), bf16),
            pltpu.VMEM((2, HALF, BLOCK), bf16),
            pltpu.VMEM((BLOCK, WIDTH), bf16),
            pltpu.SemaphoreType.DMA,
        ],
        (VMEM, HBM, VMEM),
    )(att_own, received, dq_mine, weight)


def place_kernel(
    mine, theirs, kept, arrived, key_out, value_out, weight_out, key, value, mixed, parts, total, sems
):
    half = my_half()
    moves = [(total, weight_out), (key, key_out), (value, value_out)]
    copies = [pltpu.make_async_copy(a, b, sems.at[n]) for n, (a, b) in enumerate(moves)]
    for side, source in ((half, mine), (1 - half, theirs)):
        for pair in range(PAIRS):
            key[:, columns_of(side, pair)] = source[rows_of(pair)]
            value[:, columns_of(side, pair)] = source[rows_of(PAIRS + pair)]
        mixed[side] = source[rows_of(MIXED)].astype(f32)
    shared = slice(SHARED, SHARED + PAIR)
    key[:, shared] = low_or_high(mixed[0], turned(mixed[1])).astype(bf16)
    copies[1].start()
    value[:, shared] = low_or_high(turned(mixed[0]), mixed[1]).astype(bf16)
    copies[2].start()
    parts[half] = kept[...]
    parts[1 - half] = arrived[...].astype(f32)
    for sequence, segments in enumerate(SEGMENTS):

        @pl.when(lax.axis_index("dp") == sequence)
        def _():
            for side, source, size, target in segments:
                total[target : target + size] = parts[side, source : source + size]

    copies[0].start()
    for copy in copies:
        copy.wait()


def place(*sources):
    weight_rows = 2 * HALF // len(SEGMENTS)
    wide = pltpu.VMEM((BLOCK, WIDTH), bf16)
    *grads, weight = kernel(
        place_kernel,
        "place",
        [VMEM] * 4,
        [shaped((BLOCK, WIDTH), bf16)] * 2 + [shaped((weight_rows, BLOCK), f32)],
        [
            wide,
            wide,
            pltpu.VMEM((2, BLOCK, PAIR), f32),
            pltpu.VMEM((2, PIECE_ROWS, BLOCK), f32),
            pltpu.VMEM((weight_rows, BLOCK), f32),
            pltpu.SemaphoreType.DMA((3,)),
        ],
        (HBM,) * 3,
    )(*sources)
    return *grads, weight.T


def weight_kernel(count, *refs):
    pieces, cots, products = refs[:count], refs[count : 2 * count], refs[-1]
    half = my_half()
    att = jnp.concatenate([piece[:, at(half, BLOCK)] for piece in pieces], axis=1)
    products[...] = times(att, jnp.concatenate([cot[...] for cot in cots], axis=0), ((1,), (0,)))


def weight_products(pieces, cots):
    return kernel(
        functools.partial(weight_kernel, len(pieces)),
        "weight_products",
        [VMEM] * (2 * len(pieces)),
        [shaped((pieces[0].shape[0], cots[0].shape[1]), f32)],
        flops=COST_FIRST,
    )(*pieces, *cots)[0]


def weight_rest_kernel(count, products, *refs):
    pieces, cots = refs[:count], refs[count : 2 * count]
    kept, *sent = refs[2 * count :]
    total = sent.pop()
    half = my_half()
    att = jnp.concatenate([piece[:, at(1 - half, BLOCK)] for piece in pieces], axis=1)
    cot = jnp.concatenate([cot[...] for cot in cots], axis=0)
    total[...] = products[...] + times(att, cot, ((1,), (0,)))
    group = my_group()
    lanes = kept.shape[1]
    kept[...] = total[:, at(group, lanes)]
    for number, out in enumerate(sent):
        target = jnp.bitwise_xor(group, number + 1)
        out[...] = total[:, at(target, lanes)].astype(bf16)


def weight_rest(products, pieces, cots, groups):
    rows, outs = products.shape
    part = (rows, outs // groups)
    return kernel(
        functools.partial(weight_rest_kernel, len(pieces)),
        "weight_rest",
        [VMEM] * (1 + 2 * len(pieces)),
        [shaped(part, f32)] + [shaped(part, bf16)] * (groups - 1),
        [pltpu.VMEM((rows, outs), f32)],
    )(products, *pieces, *cots)


def weight_sum_kernel(kept, *rest):
    received, (mine, sent, total) = rest[:-3], rest[-3:]
    value = kept[...]
    for part in received:
        value = value + part[...].astype(f32)
    total[...] = value
    half = my_half()
    mine[...] = total[:, at(half, BLOCK)]
    sent[...] = total[:, at(1 - half, BLOCK)].astype(bf16)


def weight_sum(kept, received):
    rows, lanes = kept.shape
    return kernel(
        weight_sum_kernel,
        "weight_sum",
        [VMEM] * (1 + len(received)),
        [shaped((rows, BLOCK), f32), shaped((rows, BLOCK), bf16)],
        [pltpu.VMEM((rows, lanes), f32)],
        flops=COST_SUM,
    )(kept, *received)


def swapped(value, axis, bits):
    count = lax.axis_size(axis)
    return lax.ppermute(value, axis, [(source, source ^ bits) for source in range(count)])


def rotated(value, axis, steps):
    count = lax.axis_size(axis)
    return lax.ppermute(
        value, axis, [(source, (source + steps) % count) for source in range(count)]
    )


def moved(value, axis, steps):
    count = lax.axis_size(axis)
    first, last = (max(0, -steps), min(count, count - steps))
    return lax.ppermute(value, axis, [(source, source + steps) for source in range(first, last)])


def after(*values):
    return lax.optimization_barrier(values)


def per_device(queries, key_states, value_states, out_cotangent, out_weight, block_clip):
    sequences = lax.axis_size("dp")
    groups = lax.axis_size("ctx") // 2
    short = sequences == 4 and groups in (2, 4)
    cotangent = out_cotangent[0]

    swap_kv, own, swap_query, query = pack(
        block_clip, queries[0], key_states[0], value_states[0]
    )
    swap_kv, cot_early = after(swap_kv, cotangent)
    partner = swapped(swap_kv, "ctx", 1)
    halo = rotated(own, "ctx", 2)
    both_own, d_turned_own, weight = own_cotangents(cotangent, out_weight, query)
    cots = [cotangent]
    if short:
        cots += [swapped(cot_early, "dp", n) for n in (1, 2)]

    partner, both_own, swap_query, cot_late = after(partner, both_own, swap_query, cotangent)
    cot_partner = swapped(cot_late, "ctx", 1)
    halo_other = rotated(partner, "ctx", 2)
    query_partner = swapped(swap_query, "ctx", 1)
    halo, both_own, *cots = after(halo, both_own, *cots)
    next_own = moved(both_own, "ctx", -2)
    if short:
        cots.append(swapped(cots[2], "dp", 1))
    keys_all, query_all, mask, clip_row = gathered(
        own, partner, halo, halo_other, query, query_partner
    )
    weights, single, totals, att, att_own, att_swap, *pieces = forward(
        4 if short else 0, keys_all, query_all, mask, clip_row
    )
    if short:
        cot_across = swapped(cot_partner, "dp", 2)
    weights, cot_partner, *pieces = after(weights, cot_partner, *pieces)

    if short:
        pieces[1:] = [swapped(pieces[n], "dp", n) for n in (1, 2, 3)]
    both_partner, stats = cotangents(
        cot_partner, weight, query_partner, att, d_turned_own, totals
    )
    both_partner, next_own, *cots = after(both_partner, next_own, *cots)
    next_partner = rotated(both_partner, "ctx", -2)
    dq_own, swap, own_grads, partner_grads = own_gradients(
        keys_all, both_own, both_partner, weights, single, stats, att_swap
    )
    own_grads, swap, *pieces = after(own_grads, swap, *pieces)

    if short:
        own_grads, cot_partner, cot_across = after(own_grads, cot_partner, cot_across)
        later = [cot_partner, swapped(cot_partner, "dp", 1), cot_across]
        later.append(swapped(cot_across, "dp", 1))
        products = weight_products(pieces, cots)
        products, *later = after(products, *later)
        kept, *sent = weight_rest(products, pieces, later, groups)
        arrived = [swapped(part, "ctx", 2 * (n + 1)) for n, part in enumerate(sent)]
        kept, own_grads = after(kept, own_grads)
    received = swapped(swap, "ctx", 1)
    kv_own, kv_swap = next_gradients(
        groups, own, partner, next_own, next_partner, own_grads, partner_grads
    )
    kv_rest = swapped(kv_swap, "ctx", 1)
    kv_own, received = after(kv_own, received)
    sublayer_out, query_grad, att_full = output_rows(att_own, received, dq_own, weight)
    if short:
        kept, kv_own, sublayer_out, *arrived = after(kept, kv_own, sublayer_out, *arrived)
        kept, sent = weight_sum(kept, arrived)
        arrived = swapped(sent, "ctx", 1)
    if not short:
        product = lax.dot_general(
            cotangent, att_full, (((0,), (1,)), ((), ())), preferred_element_type=f32
        ).astype(bf16)
        sequence_grad = lax.psum_scatter(product, "ctx", scatter_dimension=0, tiled=True)
        weight_grad = lax.psum_scatter(
            sequence_grad.astype(f32), "dp", scatter_dimension=1, tiled=True
        )
        kept = jnp.zeros((PIECE_ROWS, BLOCK), f32)
        arrived = kept.astype(bf16)
    key_grad, value_grad, placed_weight = place(kv_own, kv_rest, kept, arrived)
    if short:
        weight_grad = placed_weight
    return (
        sublayer_out[None],
        query_grad[None],
        key_grad[None],
        value_grad[None],
        weight_grad,
    )


def solution(mesh):
    return jax.shard_map(
        per_device,
        mesh=mesh,
        in_specs=(
            P("dp", "ctx", None),
            P("dp", "ctx", None),
            P("dp", "ctx", None),
            P("dp", "ctx", None),
            P(),
            P("dp", "ctx"),
        ),
        out_specs=(
            P("dp", "ctx", None),
            P("dp", "ctx", None),
            P("dp", "ctx", None),
            P("dp", "ctx", None),
            P("ctx", "dp"),
        ),
        check_vma=False,
    )
```

```python
import functools
import math

import jax
import jax.numpy as jnp
from jax import lax
from jax.experimental import pallas as pl
from jax.experimental.pallas import tpu as pltpu
from jax.sharding import PartitionSpec as P

HEADS = 18
HDIM = 64
BLOCK = 128
WIN = 256
PAIR = 2 * HDIM
WIDTH = HEADS * HDIM
HALF = WIDTH // 2
PAIRS = HEADS // 4
SHARED = PAIRS * PAIR
MIXED = 2 * PAIRS
ROWS = (MIXED + 1) * BLOCK
FIRST_BLOCKS = (0, 2, 5, 7)
HEAD_STARTS = (0, 128, 320, 448)
SINGLE_START = 256
PIECE_ROWS = 160
ATT_ROWS = HEAD_STARTS[-1] + PIECE_ROWS
SEGMENTS = (
    ((0, 0, 128, 0), (0, 128, 32, 256), (1, 0, 128, 128)),
    ((0, 0, 96, 0), (0, 96, 64, 224), (1, 0, 128, 96)),
    ((0, 0, 128, 64), (1, 0, 64, 0), (1, 64, 96, 192)),
    ((0, 0, 128, 32), (1, 0, 32, 0), (1, 32, 128, 160)),
)
CLIP_ROWS = 16
CLIP_STAT = 2 * PAIRS + 2
DELTA_STAT = CLIP_STAT + 2
STAT_ROWS = 24
SENT_ROWS = ROWS + 6 * STAT_ROWS
CHUNKS = 4
SCALING = 1.0 / math.sqrt(HDIM)
COST_GATHER = 2_000_000_000
COST_KEYS = 1_000_000
COST_FIRST = 2_000_000_000
COST_NEXT = 4_000_000_000
COST_SUM = 2_000_000_000
VMEM_LIMIT = 24 * 1024 * 1024

big_negative = -1e30
bf16 = jnp.bfloat16
f32 = jnp.float32

VMEM = pl.BlockSpec(memory_space=pltpu.VMEM)
HBM = pl.BlockSpec(memory_space=pltpu.HBM)


def shaped(shape, dtype):
    return jax.ShapeDtypeStruct(shape, dtype)


def kernel(body, name, ins, outs, scratch=(), spaces=None, flops=1_000_000):
    return pl.pallas_call(
        body,
        out_shape=tuple(outs),
        in_specs=list(ins),
        out_specs=spaces or (VMEM,) * len(outs),
        scratch_shapes=list(scratch),
        compiler_params=pltpu.CompilerParams(vmem_limit_bytes=VMEM_LIMIT),
        cost_estimate=pl.CostEstimate(flops=flops, bytes_accessed=10_000, transcendentals=0),
        name=name,
    )


def in_hbm(value):
    return pltpu.with_memory_space_constraint(value, pltpu.HBM)


def my_half():
    return jnp.bitwise_and(lax.axis_index("ctx"), 1)


def my_group():
    return jnp.right_shift(lax.axis_index("ctx"), 1)


def at(index, size):
    return pl.ds(pl.multiple_of(index * size, size), size)


def span(start, size, unit):
    return pl.ds(pl.multiple_of(start, unit), size)


def rows_of(block):
    return slice(block * BLOCK, (block + 1) * BLOCK)


def columns_of(half, pair):
    return span((FIRST_BLOCKS[pair] + half) * PAIR, PAIR, PAIR)


def head_rows(pair):
    return slice(HEAD_STARTS[pair], HEAD_STARTS[pair] + PAIR)


def single_rows():
    return slice(SINGLE_START, SINGLE_START + HDIM)


def times(a, b, dims):
    return lax.dot_general(a, b, (dims, ((), ())), preferred_element_type=f32)


def is_low():
    return lax.broadcasted_iota(jnp.int32, (1, PAIR), 1) < HDIM


def low_or_high(low_value, high_value):
    return jnp.where(is_low(), low_value, high_value)


def turned(value):
    return pltpu.roll(value, HDIM, 1)


def pack_kernel(query, key, value, swap_kv, own_kv, swap_query, own_query, *scratch):
    query_all, key_all, value_all, mixed, single, sems = scratch
    half = my_half()
    pairs = ((key, key_all), (value, value_all), (query, query_all))
    copies = [pltpu.make_async_copy(a, b, sems.at[n]) for n, (a, b) in enumerate(pairs)]
    for copy in copies:
        copy.start()
    shared = slice(SHARED, SHARED + PAIR)
    for copy in copies:
        copy.wait()
    for side, target in ((1 - half, swap_kv), (half, own_kv)):
        for pair in range(PAIRS):
            target[rows_of(pair)] = key_all[:, columns_of(side, pair)]
            target[rows_of(PAIRS + pair)] = value_all[:, columns_of(side, pair)]
    key_shared = key_all[:, shared].astype(f32)
    value_shared = value_all[:, shared].astype(f32)
    mixed[0] = low_or_high(key_shared, turned(value_shared)).astype(bf16)
    mixed[1] = low_or_high(turned(key_shared), value_shared).astype(bf16)
    swap_kv[rows_of(MIXED)] = mixed[1 - half]
    own_kv[rows_of(MIXED)] = mixed[half]
    for pair in range(PAIRS):
        swap_query[rows_of(pair)] = query_all[:, columns_of(1 - half, pair)]
        own_query[rows_of(pair)] = query_all[:, columns_of(half, pair)]
    query_shared = query_all[:, shared].astype(f32)
    single[0] = low_or_high(query_shared, 0.0)
    single[1] = low_or_high(turned(query_shared), 0.0)
    own_query[rows_of(PAIRS)] = single[half].astype(bf16)
    theirs = single[1 - half]
    swap_query[SHARED:] = low_or_high(theirs[:HDIM], turned(theirs[HDIM:])).astype(bf16)


def pack(query, key, value):
    wide = pltpu.VMEM((BLOCK, WIDTH), bf16)
    return kernel(
        pack_kernel,
        "pack",
        [HBM] * 3,
        [shaped((ROWS, PAIR), bf16)] * 2
        + [shaped((HALF, PAIR), bf16), shaped((SHARED + PAIR, PAIR), bf16)],
        [
            wide,
            wide,
            wide,
            pltpu.VMEM((2, BLOCK, PAIR), bf16),
            pltpu.VMEM((2, BLOCK, PAIR), f32),
            pltpu.SemaphoreType.DMA((3,)),
        ],
    )(in_hbm(query), in_hbm(key), in_hbm(value))


def label_kernel(clip, own_kv, out):
    out[:ROWS] = own_kv[...]
    clip_rows = jnp.broadcast_to(clip[...].astype(f32), (CLIP_ROWS, PAIR))
    out[ROWS:] = clip_rows.astype(bf16)


def label(clip, own_kv):
    return kernel(
        label_kernel,
        "label",
        [VMEM] * 2,
        [shaped((ROWS + CLIP_ROWS, PAIR), bf16)],
    )(clip, own_kv)[0]


def label_query_kernel(query, own, halo, out):
    out[:HALF] = query[...]
    out[HALF : HALF + CLIP_ROWS] = own[ROWS:]
    out[HALF + CLIP_ROWS :] = halo[ROWS:]


def label_query(query, own, halo):
    return kernel(
        label_query_kernel,
        "label_query",
        [VMEM] * 3,
        [shaped((HALF + 2 * CLIP_ROWS, PAIR), bf16)],
    )(query, own, halo)[0]


def unpacked_single(packed):
    packed = packed.astype(f32)
    top, bottom = low_or_high(packed, 0.0), low_or_high(turned(packed), 0.0)
    return jnp.concatenate([top, bottom], axis=0).astype(bf16)


def join_query(target, d_turned, single, query, query_single, d_pairs, d_shared):
    half = my_half()
    for pair in range(PAIRS):
        d_pair = d_pairs[:, pair * PAIR : (pair + 1) * PAIR].astype(bf16)
        target[rows_of(pair)] = query[rows_of(pair)]
        target[rows_of(PAIRS + pair)] = d_pair
        d_turned[head_rows(pair)] = d_pair.T
    single[0] = low_or_high(0.0, turned(d_shared)).astype(bf16)
    single[1] = low_or_high(0.0, d_shared).astype(bf16)
    d_single = single[half]
    target[rows_of(MIXED)] = query_single + d_single
    d_turned[single_rows()] = d_single.T[HDIM:]


def own_cotangent_kernel(cotangent, weight, query, both, d_turned, kept, rows, single, sems):
    half = my_half()
    chunk = rows.shape[1] // CHUNKS
    copies = [pltpu.make_async_copy(cotangent, rows, sems.at[CHUNKS])]
    for number in range(CHUNKS):
        part = pl.ds(number * chunk, chunk)
        copies.append(pltpu.make_async_copy(weight.at[part], kept.at[part], sems.at[number]))
    for copy in copies:
        copy.start()
    copies[0].wait()
    pairs = shared = None
    for number in range(CHUNKS):
        copies[number + 1].wait()
        part = slice(number * chunk, (number + 1) * chunk)
        columns = [kept[part, columns_of(half, pair)] for pair in range(PAIRS)]
        wide = times(rows[:, part], jnp.concatenate(columns, axis=1), ((1,), (0,)))
        narrow = times(rows[:, part], kept[part, SHARED : SHARED + PAIR], ((1,), (0,)))
        pairs = wide if pairs is None else pairs + wide
        shared = narrow if shared is None else shared + narrow
    join_query(both, d_turned, single, query, query[rows_of(PAIRS)], pairs, shared)


def own_cotangents(cotangent, weight, query):
    return kernel(
        own_cotangent_kernel,
        "own_cotangents",
        [HBM, HBM, VMEM],
        [shaped((ROWS, PAIR), bf16), shaped((HALF, BLOCK), bf16), shaped(weight.shape, bf16)],
        [
            pltpu.VMEM(cotangent.shape, bf16),
            pltpu.VMEM((2, BLOCK, PAIR), bf16),
            pltpu.SemaphoreType.DMA((CHUNKS + 1,)),
        ],
    )(in_hbm(cotangent), in_hbm(weight), query)


def cotangent_kernel(
    cotangent, weight, query, att, d_turned_own, totals, both, stats, d_turned, d_all, single
):
    half = my_half()
    rows = cotangent[...]
    columns = [weight[:, columns_of(half, pair)] for pair in range(PAIRS)]
    pairs = times(rows, jnp.concatenate(columns, axis=1), ((1,), (0,)))
    shared = times(rows, weight[:, SHARED : SHARED + PAIR], ((1,), (0,)))
    query_single = unpacked_single(query[SHARED:HALF])
    join_query(both, d_turned, single, query, query_single, pairs, shared)
    d_all[:, at(half, BLOCK)] = d_turned_own[...]
    d_all[:, at(1 - half, BLOCK)] = d_turned[...]
    stats[...] = totals[...]
    for query_block in range(2):
        steps = rows_of(query_block)
        for pair in range(PAIRS):
            which = head_rows(pair)
            dots = d_all[which, steps].astype(f32) * att[which, steps].astype(f32)
            row = DELTA_STAT + 2 * pair + query_block
            stats[row : row + 1, :BLOCK] = jnp.sum(dots[:HDIM], axis=0, keepdims=True)
            stats[row : row + 1, BLOCK:] = jnp.sum(dots[HDIM:], axis=0, keepdims=True)
        which = single_rows()
        dots = d_all[which, steps].astype(f32) * att[which, steps].astype(f32)
        row = DELTA_STAT + 2 * PAIRS + query_block
        stats[row : row + 1, :BLOCK] = jnp.sum(dots, axis=0, keepdims=True)
    rest = jnp.concatenate([stats[:, :BLOCK], stats[:, BLOCK:]], axis=0)
    for number in range(3):
        begin = ROWS + 2 * STAT_ROWS * number
        part = rest.astype(bf16)
        both[begin : begin + 2 * STAT_ROWS] = part
        rest = rest - part.astype(f32)


def stats_of(both):
    parts = []
    for number in range(3):
        begin = ROWS + 2 * STAT_ROWS * number
        parts.append(both[begin : begin + 2 * STAT_ROWS].astype(f32))
    total = (parts[0] + parts[1]) + parts[2]
    return jnp.concatenate([total[:STAT_ROWS], total[STAT_ROWS:]], axis=1)


def cotangents(cotangent, weight, query, att, d_turned_own, totals):
    return kernel(
        cotangent_kernel,
        "cotangents",
        [VMEM] * 6,
        [shaped((SENT_ROWS, PAIR), bf16), shaped((STAT_ROWS, 2 * BLOCK), f32)],
        [
            pltpu.VMEM((HALF, BLOCK), bf16),
            pltpu.VMEM((HALF, 2 * BLOCK), bf16),
            pltpu.VMEM((2, BLOCK, PAIR), bf16),
        ],
    )(cotangent, weight, query, att, d_turned_own, totals)


def gather_blocks(target, offset, own, partner):
    half = my_half()
    for block in range(target.shape[0]):
        target[block, at(offset + half, BLOCK)] = own[rows_of(block)]
        target[block, at(offset + 1 - half, BLOCK)] = partner[rows_of(block)]


def doubled(rows, factor=1.0):
    first = low_or_high(factor, 0.0).astype(bf16)
    second = low_or_high(0.0, factor).astype(bf16)
    return jnp.concatenate([rows * first, rows * second], axis=0)


def diagonal(pair):
    return jnp.concatenate([pair[:HDIM, :BLOCK], pair[HDIM:, BLOCK:]], axis=0)


def triangles():
    row = lax.broadcasted_iota(jnp.int32, (BLOCK, BLOCK), 0)
    lane = lax.broadcasted_iota(jnp.int32, (BLOCK, BLOCK), 1)
    older = jnp.where(row > lane, 1.0, 0.0)
    return older, jnp.ones((BLOCK, BLOCK), f32), 1.0 - older


def hidden(scores, visible):
    if scores.shape[1] > visible.shape[1]:
        visible = jnp.concatenate([visible, visible], axis=1)
    return jnp.where(visible > 0.5, scores, big_negative)


def gather_kernel(
    own, partner, halo, halo_other, query_own, query_partner, keys_all, query_all, mask, clip_row, clips
):
    half = my_half()
    gather_blocks(keys_all, 0, halo, halo_other)
    gather_blocks(keys_all, 2, own, partner)
    for pair in range(PAIRS):
        query_all[pair, at(half, BLOCK)] = query_own[rows_of(pair)]
        query_all[pair, at(1 - half, BLOCK)] = query_partner[rows_of(pair)]
    query_all[PAIRS, at(half, BLOCK)] = query_own[rows_of(PAIRS)]
    query_all[PAIRS, at(1 - half, BLOCK)] = unpacked_single(query_partner[SHARED:HALF])
    clips[at(half, CLIP_ROWS)] = halo[ROWS:]
    clips[at(1 - half, CLIP_ROWS)] = query_partner[HALF + CLIP_ROWS :]
    clips[at(2 + half, CLIP_ROWS)] = own[ROWS:]
    clips[at(3 - half, CLIP_ROWS)] = query_partner[HALF : HALF + CLIP_ROWS]

    def clip_of(block):
        return clips[block * CLIP_ROWS : (block + 1) * CLIP_ROWS].astype(f32)[0:1]

    for query_block in range(2):
        query_clip = clip_of(2 + query_block)
        for step, shape in enumerate(triangles()):
            block = query_block + step
            same = jnp.where(clip_of(block) == query_clip, 1.0, 0.0)
            present = jnp.where(2 * my_group() - 2 + block >= 0, 1.0, 0.0)
            mask[query_block, rows_of(step)] = shape * same * present
        clip_row[:, rows_of(query_block)] = query_clip


def gathered(*sources):
    return kernel(
        gather_kernel,
        "gathered",
        [VMEM] * 6,
        [
            shaped((MIXED + 1, 4 * BLOCK, PAIR), bf16),
            shaped((PAIRS + 1, 2 * BLOCK, PAIR), bf16),
            shaped((2, WIN + BLOCK, BLOCK), f32),
            shaped((1, 2 * BLOCK), f32),
            shaped((4 * CLIP_ROWS, PAIR), bf16),
        ],
        flops=COST_GATHER,
    )(*sources)


def staggered(items, *stages):
    values = [None] * len(items)
    for step in range(len(items) + 2 * len(stages) - 2):
        for number, stage in enumerate(stages):
            index = step - 2 * number
            if 0 <= index < len(items):
                values[index] = stage(*items[index], values[index])


def forward_kernel(
    pieces_wanted,
    keys_all,
    query_all,
    mask,
    clip_row,
    weights_out,
    single_out,
    totals,
    att,
    att_own,
    att_swap,
    *pieces,
):
    half = my_half()
    totals[CLIP_STAT : CLIP_STAT + 1] = clip_row[...]

    def softmax(scores, row):
        lanes = slice(0, scores.shape[1])
        maximum = jnp.max(scores, axis=0, keepdims=True)
        powers = jnp.exp(scores - maximum)
        total = jnp.sum(powers, axis=0, keepdims=True)
        totals[row : row + 1, lanes] = maximum + jnp.log(total)
        return (powers * (1.0 / total)).astype(bf16)

    def keys_of(query_block):
        return slice(query_block * BLOCK, query_block * BLOCK + WIN + BLOCK)

    def score(pair, query_block, _):
        rows = query_all[pair, rows_of(query_block)]
        if pair < PAIRS:
            key_rows, rows = keys_all[pair, keys_of(query_block)], doubled(rows, SCALING)
        else:
            key_rows = keys_all[MIXED, keys_of(query_block)]
            rows = rows * low_or_high(SCALING, 0.0).astype(bf16)
        return times(key_rows, rows, ((1,), (1,)))

    def weigh(pair, query_block, scores):
        return softmax(hidden(scores, mask[query_block]), 2 * pair + query_block)

    def mix(pair, query_block, weights):
        steps = rows_of(query_block)
        if pair < PAIRS:
            weights_out[pair, query_block] = weights
            mixed = times(keys_all[PAIRS + pair, keys_of(query_block)], weights, ((0,), (0,)))
            att[head_rows(pair), steps] = diagonal(mixed).astype(bf16)
        else:
            single_out[query_block] = weights
            mixed = times(keys_all[MIXED, keys_of(query_block)], weights, ((0,), (0,)))
            att[single_rows(), steps] = mixed[HDIM:].astype(bf16)

    items = [(pair, query_block) for pair in range(PAIRS + 1) for query_block in range(2)]
    staggered(items, score, weigh, mix)

    att[HALF:] = jnp.zeros((ATT_ROWS - HALF, 2 * BLOCK), bf16)
    att_own[...] = att[:HALF, at(half, BLOCK)]
    att_swap[...] = att[:HALF, at(1 - half, BLOCK)]
    for number, piece in enumerate(pieces):
        target = jnp.bitwise_xor(lax.axis_index("dp"), number)
        late = 32 * jnp.maximum(target - 2, 0)
        begin = jnp.where(half == 0, 160 * target - late, 128 * target + late)
        piece[...] = att[span(begin, PIECE_ROWS, 32), :]


def forward(pieces_wanted, *sources):
    piece = (PIECE_ROWS, 2 * BLOCK)
    return kernel(
        functools.partial(forward_kernel, pieces_wanted),
        "forward",
        [VMEM] * 4,
        [
            shaped((PAIRS, 2, WIN + BLOCK, 2 * BLOCK), bf16),
            shaped((2, WIN + BLOCK, BLOCK), bf16),
            shaped((STAT_ROWS, 2 * BLOCK), f32),
            shaped((ATT_ROWS, 2 * BLOCK), bf16),
            shaped((HALF, BLOCK), bf16),
            shaped((HALF, BLOCK), bf16),
        ]
        + [shaped(piece, bf16)] * pieces_wanted,
    )(*sources)


def own_kernel(
    keys_all,
    both_own,
    both_partner,
    weights_in,
    single_in,
    stats,
    att_swap,
    dq_own,
    swap,
    own_grads,
    partner_grads,
    query_all,
    dq_all,
    grads,
):
    half = my_half()
    gather_blocks(query_all, 0, both_own, both_partner)

    def delta_of(row, lanes):
        return stats[DELTA_STAT + row : DELTA_STAT + row + 1, :lanes]

    def accumulate(block, query_block, value):
        if query_block == 1:
            grads[block] = value
        else:
            grads[block, :BLOCK] += value

    def keys_of(query_block):
        return slice(query_block * BLOCK, query_block * BLOCK + WIN + BLOCK)

    def operands(pair, query_block):
        steps = rows_of(query_block)
        if pair < PAIRS:
            query_rows = doubled(query_all[pair, steps], SCALING)
            return query_rows, doubled(query_all[PAIRS + pair, steps]), weights_in[pair, query_block]
        rows = query_all[MIXED, steps]
        query_rows = rows * low_or_high(SCALING, 0.0).astype(bf16)
        d_rows = rows * low_or_high(0.0, 1.0).astype(bf16)
        return query_rows, d_rows, single_in[query_block]

    def d_weights_of(pair, query_block, _):
        block = PAIRS + pair if pair < PAIRS else MIXED
        _, d_rows, _ = operands(pair, query_block)
        return times(keys_all[block, keys_of(query_block)], d_rows, ((1,), (1,)))

    def d_scores_of(pair, query_block, d_weights):
        _, _, weights = operands(pair, query_block)
        delta = delta_of(2 * pair + query_block, d_weights.shape[1])
        return (weights.astype(f32) * (d_weights - delta)).astype(bf16)

    def products(pair, query_block, d_scores):
        query_rows, d_rows, weights = operands(pair, query_block)
        mine = slice(WIN - query_block * BLOCK, WIN + BLOCK)
        steps = rows_of(query_block)
        block = pair if pair < PAIRS else MIXED
        dq = times(keys_all[block, keys_of(query_block)], d_scores, ((0,), (0,)))
        dk = times(d_scores[mine], query_rows, ((1,), (0,)))
        dv = times(weights[mine], d_rows, ((1,), (0,)))
        if pair < PAIRS:
            dq_all[head_rows(pair), steps] = (diagonal(dq) * SCALING).astype(bf16)
            accumulate(pair, query_block, dk)
            accumulate(PAIRS + pair, query_block, dv)
        else:
            dq_all[single_rows(), steps] = (dq[:HDIM] * SCALING).astype(bf16)
            accumulate(MIXED, query_block, dk + dv)

    items = [(pair, query_block) for pair in range(PAIRS + 1) for query_block in (1, 0)]
    staggered(items, d_weights_of, d_scores_of, products)
    dq_own[...] = dq_all[:, at(half, BLOCK)]
    swap[:, :BLOCK] = att_swap[...]
    swap[:, BLOCK:] = dq_all[:, at(1 - half, BLOCK)]
    for block in range(MIXED + 1):
        own_grads[rows_of(block)] = grads[block, at(half, BLOCK)]
        partner_grads[rows_of(block)] = grads[block, at(1 - half, BLOCK)]


def own_gradients(*sources):
    return kernel(
        own_kernel,
        "own_gradients",
        [VMEM] * 7,
        [shaped((HALF, BLOCK), bf16), shaped((HALF, 2 * BLOCK), bf16)]
        + [shaped((ROWS, PAIR), f32)] * 2,
        [
            pltpu.VMEM((MIXED + 1, 2 * BLOCK, PAIR), bf16),
            pltpu.VMEM((HALF, 2 * BLOCK), bf16),
            pltpu.VMEM((MIXED + 1, 2 * BLOCK, PAIR), f32),
        ],
    )(*sources)


def next_kernel(
    groups,
    own,
    partner,
    both_own,
    both_partner,
    own_grads,
    partner_grads,
    clips,
    mine,
    swap,
    keys_all,
    query_all,
    mask,
    grads,
    stats,
):
    half = my_half()
    stats[...] = stats_of(both_partner)
    gather_blocks(keys_all, 0, own, partner)
    gather_blocks(query_all, 0, both_own, both_partner)
    for block in range(MIXED + 1):
        grads[block, at(half, BLOCK)] = own_grads[rows_of(block)]
        grads[block, at(1 - half, BLOCK)] = partner_grads[rows_of(block)]
    present = jnp.where(my_group() < groups - 1, 1.0, 0.0)
    older, every, _ = triangles()
    for query_block, block, shape in ((0, 0, older), (0, 1, every), (1, 1, older)):
        query_clip = stats[CLIP_STAT : CLIP_STAT + 1, rows_of(query_block)]
        key_clip = clips[(2 + block) * CLIP_ROWS : (3 + block) * CLIP_ROWS].astype(f32)[0:1]
        same = jnp.where(key_clip == query_clip, 1.0, 0.0)
        mask[query_block, rows_of(block)] = shape * same * present

    def operands(pair, query_block):
        steps = rows_of(query_block)
        if pair < PAIRS:
            query_rows = doubled(query_all[pair, steps], SCALING)
            return query_rows, doubled(query_all[PAIRS + pair, steps])
        rows = query_all[MIXED, steps]
        query_rows = rows * low_or_high(SCALING, 0.0).astype(bf16)
        return query_rows, rows * low_or_high(0.0, 1.0).astype(bf16)

    def score(pair, query_block, _):
        keys = slice(query_block * BLOCK, WIN)
        query_rows, d_rows = operands(pair, query_block)
        key_block, value_block = (pair, PAIRS + pair) if pair < PAIRS else (MIXED, MIXED)
        scores = times(keys_all[key_block, keys], query_rows, ((1,), (1,)))
        return scores, times(keys_all[value_block, keys], d_rows, ((1,), (1,)))

    def weigh(pair, query_block, values):
        scores, d_weights = values
        row = 2 * pair + query_block
        lanes = slice(0, scores.shape[1])
        scores = hidden(scores, mask[query_block, query_block * BLOCK : WIN])
        weights = jnp.exp(scores - stats[row : row + 1, lanes]).astype(bf16)
        delta = stats[DELTA_STAT + row : DELTA_STAT + row + 1, lanes]
        return weights, (weights.astype(f32) * (d_weights - delta)).astype(bf16)

    def products(pair, query_block, values):
        weights, d_scores = values
        keys = slice(query_block * BLOCK, WIN)
        query_rows, d_rows = operands(pair, query_block)
        dk = times(d_scores, query_rows, ((1,), (0,)))
        dv = times(weights, d_rows, ((1,), (0,)))
        if pair < PAIRS:
            grads[pair, keys] += dk
            grads[PAIRS + pair, keys] += dv
        else:
            grads[MIXED, keys] += dk + dv

    items = [(pair, query_block) for pair in range(PAIRS + 1) for query_block in range(2)]
    staggered(items, score, weigh, products)
    for block in range(MIXED + 1):
        mine[rows_of(block)] = grads[block, at(half, BLOCK)].astype(bf16)
        swap[rows_of(block)] = grads[block, at(1 - half, BLOCK)].astype(bf16)


def next_gradients(groups, *sources):
    return kernel(
        functools.partial(next_kernel, groups),
        "next_gradients",
        [VMEM] * 7,
        [shaped((ROWS, PAIR), bf16)] * 2,
        [
            pltpu.VMEM((MIXED + 1, 2 * BLOCK, PAIR), bf16),
            pltpu.VMEM((MIXED + 1, 2 * BLOCK, PAIR), bf16),
            pltpu.VMEM((2, 2 * BLOCK, BLOCK), f32),
            pltpu.VMEM((MIXED + 1, 2 * BLOCK, PAIR), f32),
            pltpu.VMEM((STAT_ROWS, 2 * BLOCK), f32),
        ],
        flops=COST_NEXT,
    )(*sources)


def join_halves(full, halves, mine, theirs):
    half = my_half()
    halves[half] = mine
    halves[1 - half] = theirs
    for side in range(2):
        for pair in range(PAIRS):
            full[rows_of(FIRST_BLOCKS[pair] + side)] = halves[side, head_rows(pair)]
        begin = SHARED + side * HDIM
        full[begin : begin + HDIM] = halves[side, single_rows()]


def output_kernel(att_own, received, dq_mine, weight, out, query_out, full, dq_all, halves, query, sem):
    join_halves(dq_all, halves, dq_mine[...], received[:, BLOCK:])
    for block in range(WIDTH // PAIR):
        query[:, block * PAIR : (block + 1) * PAIR] = dq_all[rows_of(block)].T
    copy = pltpu.make_async_copy(query, query_out, sem)
    copy.start()
    join_halves(full, halves, att_own[...], received[:, :BLOCK])
    out[...] = times(weight[...], full[...], ((1,), (0,))).T.astype(bf16)
    copy.wait()


def output_rows(att_own, received, dq_mine, weight):
    return kernel(
        output_kernel,
        "output",
        [VMEM] * 4,
        [
            shaped((BLOCK, weight.shape[0]), bf16),
            shaped((BLOCK, WIDTH), bf16),
            shaped((WIDTH, BLOCK), bf16),
        ],
        [
            pltpu.VMEM((WIDTH, BLOCK), bf16),
            pltpu.VMEM((2, HALF, BLOCK), bf16),
            pltpu.VMEM((BLOCK, WIDTH), bf16),
            pltpu.SemaphoreType.DMA,
        ],
        (VMEM, HBM, VMEM),
    )(att_own, received, dq_mine, weight)


def place_kernel(
    mine, theirs, kept, arrived, key_out, value_out, weight_out, key, value, mixed, parts, total, sems
):
    half = my_half()
    moves = [(total, weight_out), (key, key_out), (value, value_out)]
    copies = [pltpu.make_async_copy(a, b, sems.at[n]) for n, (a, b) in enumerate(moves)]
    for side, source in ((half, mine), (1 - half, theirs)):
        for pair in range(PAIRS):
            key[:, columns_of(side, pair)] = source[rows_of(pair)]
            value[:, columns_of(side, pair)] = source[rows_of(PAIRS + pair)]
        mixed[side] = source[rows_of(MIXED)].astype(f32)
    shared = slice(SHARED, SHARED + PAIR)
    key[:, shared] = low_or_high(mixed[0], turned(mixed[1])).astype(bf16)
    copies[1].start()
    value[:, shared] = low_or_high(turned(mixed[0]), mixed[1]).astype(bf16)
    copies[2].start()
    parts[half] = kept[...]
    parts[1 - half] = arrived[...].astype(f32)
    for sequence, segments in enumerate(SEGMENTS):

        @pl.when(lax.axis_index("dp") == sequence)
        def _():
            for side, source, size, target in segments:
                total[target : target + size] = parts[side, source : source + size]

    copies[0].start()
    for copy in copies:
        copy.wait()


def place(*sources):
    weight_rows = 2 * HALF // len(SEGMENTS)
    wide = pltpu.VMEM((BLOCK, WIDTH), bf16)
    *grads, weight = kernel(
        place_kernel,
        "place",
        [VMEM] * 4,
        [shaped((BLOCK, WIDTH), bf16)] * 2 + [shaped((weight_rows, BLOCK), f32)],
        [
            wide,
            wide,
            pltpu.VMEM((2, BLOCK, PAIR), f32),
            pltpu.VMEM((2, PIECE_ROWS, BLOCK), f32),
            pltpu.VMEM((weight_rows, BLOCK), f32),
            pltpu.SemaphoreType.DMA((3,)),
        ],
        (HBM,) * 3,
    )(*sources)
    return *grads, weight.T


def weight_kernel(count, *refs):
    pieces, cots, products = refs[:count], refs[count : 2 * count], refs[-1]
    half = my_half()
    att = jnp.concatenate([piece[:, at(half, BLOCK)] for piece in pieces], axis=1)
    products[...] = times(att, jnp.concatenate([cot[...] for cot in cots], axis=0), ((1,), (0,)))


def weight_products(pieces, cots):
    return kernel(
        functools.partial(weight_kernel, len(pieces)),
        "weight_products",
        [VMEM] * (2 * len(pieces)),
        [shaped((pieces[0].shape[0], cots[0].shape[1]), f32)],
        flops=COST_FIRST,
    )(*pieces, *cots)[0]


def weight_rest_kernel(count, products, *refs):
    pieces, cots = refs[:count], refs[count : 2 * count]
    kept, *sent = refs[2 * count :]
    total = sent.pop()
    half = my_half()
    att = jnp.concatenate([piece[:, at(1 - half, BLOCK)] for piece in pieces], axis=1)
    cot = jnp.concatenate([cot[...] for cot in cots], axis=0)
    total[...] = products[...] + times(att, cot, ((1,), (0,)))
    group = my_group()
    lanes = kept.shape[1]
    kept[...] = total[:, at(group, lanes)]
    for number, out in enumerate(sent):
        target = jnp.bitwise_xor(group, number + 1)
        out[...] = total[:, at(target, lanes)].astype(bf16)


def weight_rest(products, pieces, cots, groups):
    rows, outs = products.shape
    part = (rows, outs // groups)
    return kernel(
        functools.partial(weight_rest_kernel, len(pieces)),
        "weight_rest",
        [VMEM] * (1 + 2 * len(pieces)),
        [shaped(part, f32)] + [shaped(part, bf16)] * (groups - 1),
        [pltpu.VMEM((rows, outs), f32)],
    )(products, *pieces, *cots)


def weight_sum_kernel(kept, *rest):
    received, (mine, sent, total) = rest[:-3], rest[-3:]
    value = kept[...]
    for part in received:
        value = value + part[...].astype(f32)
    total[...] = value
    half = my_half()
    mine[...] = total[:, at(half, BLOCK)]
    sent[...] = total[:, at(1 - half, BLOCK)].astype(bf16)


def weight_sum(kept, received):
    rows, lanes = kept.shape
    return kernel(
        weight_sum_kernel,
        "weight_sum",
        [VMEM] * (1 + len(received)),
        [shaped((rows, BLOCK), f32), shaped((rows, BLOCK), bf16)],
        [pltpu.VMEM((rows, lanes), f32)],
        flops=COST_SUM,
    )(kept, *received)


def swapped(value, axis, bits):
    count = lax.axis_size(axis)
    return lax.ppermute(value, axis, [(source, source ^ bits) for source in range(count)])


def rotated(value, axis, steps):
    count = lax.axis_size(axis)
    return lax.ppermute(
        value, axis, [(source, (source + steps) % count) for source in range(count)]
    )


def moved(value, axis, steps):
    count = lax.axis_size(axis)
    first, last = (max(0, -steps), min(count, count - steps))
    return lax.ppermute(value, axis, [(source, source + steps) for source in range(first, last)])


def after(*values):
    return lax.optimization_barrier(values)


def per_device(queries, key_states, value_states, out_cotangent, out_weight, block_clip):
    sequences = lax.axis_size("dp")
    groups = lax.axis_size("ctx") // 2
    short = sequences == 4 and groups in (2, 4)
    cotangent = out_cotangent[0]

    swap_kv, own_kv, swap_query, query = pack(queries[0], key_states[0], value_states[0])
    swap_kv, cot_early, clip = after(swap_kv, cotangent, block_clip)
    own = label(clip, own_kv)
    partner = swapped(swap_kv, "ctx", 1)
    halo = rotated(own, "ctx", 2)
    both_own, d_turned_own, weight = own_cotangents(cotangent, out_weight, query)
    cots = [cotangent]
    if short:
        cots += [swapped(cot_early, "dp", n) for n in (1, 2)]

    partner, both_own, swap_query, cot_late = after(partner, both_own, swap_query, cotangent)
    cot_partner = swapped(cot_late, "ctx", 1)
    halo_other = rotated(partner, "ctx", 2)
    query_partner = swapped(label_query(swap_query, own, halo), "ctx", 1)
    halo, both_own, *cots = after(halo, both_own, *cots)
    next_own = moved(both_own, "ctx", -2)
    if short:
        cots.append(swapped(cots[2], "dp", 1))
    keys_all, query_all, mask, clip_row, clips = gathered(
        own, partner, halo, halo_other, query, query_partner
    )
    weights, single, totals, att, att_own, att_swap, *pieces = forward(
        4 if short else 0, keys_all, query_all, mask, clip_row
    )
    if short:
        cot_across = swapped(cot_partner, "dp", 2)
    weights, cot_partner, *pieces = after(weights, cot_partner, *pieces)

    if short:
        pieces[1:] = [swapped(pieces[n], "dp", n) for n in (1, 2, 3)]
    both_partner, stats = cotangents(
        cot_partner, weight, query_partner, att, d_turned_own, totals
    )
    both_partner, next_own, *cots = after(both_partner, next_own, *cots)
    next_partner = rotated(both_partner, "ctx", -2)
    dq_own, swap, own_grads, partner_grads = own_gradients(
        keys_all, both_own, both_partner, weights, single, stats, att_swap
    )
    own_grads, swap, *pieces = after(own_grads, swap, *pieces)

    if short:
        own_grads, cot_partner, cot_across = after(own_grads, cot_partner, cot_across)
        later = [cot_partner, swapped(cot_partner, "dp", 1), cot_across]
        later.append(swapped(cot_across, "dp", 1))
        products = weight_products(pieces, cots)
        products, swap = after(products, swap)
        kept, *sent = weight_rest(products, pieces, later, groups)
        arrived = [swapped(part, "ctx", 2 * (n + 1)) for n, part in enumerate(sent)]
        kept, own_grads = after(kept, own_grads)
    received = swapped(swap, "ctx", 1)
    kv_own, kv_swap = next_gradients(
        groups, own, partner, next_own, next_partner, own_grads, partner_grads, clips
    )
    kv_rest = swapped(kv_swap, "ctx", 1)
    kv_own, received = after(kv_own, received)
    sublayer_out, query_grad, att_full = output_rows(att_own, received, dq_own, weight)
    if short:
        kept, kv_own, sublayer_out, *arrived = after(kept, kv_own, sublayer_out, *arrived)
        kept, sent = weight_sum(kept, arrived)
        arrived = swapped(sent, "ctx", 1)
    if not short:
        product = lax.dot_general(
            cotangent, att_full, (((0,), (1,)), ((), ())), preferred_element_type=f32
        ).astype(bf16)
        sequence_grad = lax.psum_scatter(product, "ctx", scatter_dimension=0, tiled=True)
        weight_grad = lax.psum_scatter(
            sequence_grad.astype(f32), "dp", scatter_dimension=1, tiled=True
        )
        kept = jnp.zeros((PIECE_ROWS, BLOCK), f32)
        arrived = kept.astype(bf16)
    key_grad, value_grad, placed_weight = place(kv_own, kv_rest, kept, arrived)
    if short:
        weight_grad = placed_weight
    return (
        sublayer_out[None],
        query_grad[None],
        key_grad[None],
        value_grad[None],
        weight_grad,
    )


def solution(mesh):
    return jax.shard_map(
        per_device,
        mesh=mesh,
        in_specs=(
            P("dp", "ctx", None),
            P("dp", "ctx", None),
            P("dp", "ctx", None),
            P("dp", "ctx", None),
            P(),
            P("dp", "ctx"),
        ),
        out_specs=(
            P("dp", "ctx", None),
            P("dp", "ctx", None),
            P("dp", "ctx", None),
            P("dp", "ctx", None),
            P("ctx", "dp"),
        ),
        check_vma=False,
    )
```

```python
import functools
import math

import jax
import jax.numpy as jnp
from jax import lax
from jax.experimental import pallas as pl
from jax.experimental.pallas import tpu as pltpu
from jax.sharding import PartitionSpec as P

HEADS = 18
HDIM = 64
BLOCK = 128
WIN = 256
PAIR = 2 * HDIM
WIDTH = HEADS * HDIM
HALF = WIDTH // 2
PAIRS = HEADS // 4
SHARED = PAIRS * PAIR
MIXED = 2 * PAIRS
ROWS = (MIXED + 1) * BLOCK
FIRST_BLOCKS = (0, 2, 5, 7)
HEAD_STARTS = (0, 128, 320, 448)
SINGLE_START = 256
PIECE_ROWS = 160
ATT_ROWS = HEAD_STARTS[-1] + PIECE_ROWS
SEGMENTS = (
    ((0, 0, 128, 0), (0, 128, 32, 256), (1, 0, 128, 128)),
    ((0, 0, 96, 0), (0, 96, 64, 224), (1, 0, 128, 96)),
    ((0, 0, 128, 64), (1, 0, 64, 0), (1, 64, 96, 192)),
    ((0, 0, 128, 32), (1, 0, 32, 0), (1, 32, 128, 160)),
)
CLIP_ROWS = 16
CLIP_STAT = 2 * PAIRS + 2
DELTA_STAT = CLIP_STAT + 2
STAT_ROWS = 24
SENT_ROWS = ROWS + 6 * STAT_ROWS
CHUNKS = 4
SCALING = 1.0 / math.sqrt(HDIM)
COST_GATHER = 1_500_000_000
COST_KEYS = 1_000_000
COST_FIRST = 2_000_000_000
COST_NEXT = 4_000_000_000
COST_SUM = 2_000_000_000
VMEM_LIMIT = 24 * 1024 * 1024

big_negative = -1e30
bf16 = jnp.bfloat16
f32 = jnp.float32

VMEM = pl.BlockSpec(memory_space=pltpu.VMEM)
HBM = pl.BlockSpec(memory_space=pltpu.HBM)


def shaped(shape, dtype):
    return jax.ShapeDtypeStruct(shape, dtype)


def kernel(body, name, ins, outs, scratch=(), spaces=None, flops=1_000_000):
    return pl.pallas_call(
        body,
        out_shape=tuple(outs),
        in_specs=list(ins),
        out_specs=spaces or (VMEM,) * len(outs),
        scratch_shapes=list(scratch),
        compiler_params=pltpu.CompilerParams(vmem_limit_bytes=VMEM_LIMIT),
        cost_estimate=pl.CostEstimate(flops=flops, bytes_accessed=10_000, transcendentals=0),
        name=name,
    )


def in_hbm(value):
    return pltpu.with_memory_space_constraint(value, pltpu.HBM)


def my_half():
    return jnp.bitwise_and(lax.axis_index("ctx"), 1)


def my_group():
    return jnp.right_shift(lax.axis_index("ctx"), 1)


def at(index, size):
    return pl.ds(pl.multiple_of(index * size, size), size)


def span(start, size, unit):
    return pl.ds(pl.multiple_of(start, unit), size)


def rows_of(block):
    return slice(block * BLOCK, (block + 1) * BLOCK)


def columns_of(half, pair):
    return span((FIRST_BLOCKS[pair] + half) * PAIR, PAIR, PAIR)


def head_rows(pair):
    return slice(HEAD_STARTS[pair], HEAD_STARTS[pair] + PAIR)


def single_rows():
    return slice(SINGLE_START, SINGLE_START + HDIM)


def times(a, b, dims):
    return lax.dot_general(a, b, (dims, ((), ())), preferred_element_type=f32)


def is_low():
    return lax.broadcasted_iota(jnp.int32, (1, PAIR), 1) < HDIM


def low_or_high(low_value, high_value):
    return jnp.where(is_low(), low_value, high_value)


def turned(value):
    return pltpu.roll(value, HDIM, 1)


def pack_kernel(query, key, value, swap_kv, own_kv, swap_query, own_query, *scratch):
    query_all, key_all, value_all, mixed, single, sems = scratch
    half = my_half()
    pairs = ((key, key_all), (value, value_all), (query, query_all))
    copies = [pltpu.make_async_copy(a, b, sems.at[n]) for n, (a, b) in enumerate(pairs)]
    for copy in copies:
        copy.start()
    shared = slice(SHARED, SHARED + PAIR)
    for copy in copies:
        copy.wait()
    for side, target in ((1 - half, swap_kv), (half, own_kv)):
        for pair in range(PAIRS):
            target[rows_of(pair)] = key_all[:, columns_of(side, pair)]
            target[rows_of(PAIRS + pair)] = value_all[:, columns_of(side, pair)]
    key_shared = key_all[:, shared].astype(f32)
    value_shared = value_all[:, shared].astype(f32)
    mixed[0] = low_or_high(key_shared, turned(value_shared)).astype(bf16)
    mixed[1] = low_or_high(turned(key_shared), value_shared).astype(bf16)
    swap_kv[rows_of(MIXED)] = mixed[1 - half]
    own_kv[rows_of(MIXED)] = mixed[half]
    for pair in range(PAIRS):
        swap_query[rows_of(pair)] = query_all[:, columns_of(1 - half, pair)]
        own_query[rows_of(pair)] = query_all[:, columns_of(half, pair)]
    query_shared = query_all[:, shared].astype(f32)
    single[0] = low_or_high(query_shared, 0.0)
    single[1] = low_or_high(turned(query_shared), 0.0)
    own_query[rows_of(PAIRS)] = single[half].astype(bf16)
    theirs = single[1 - half]
    swap_query[SHARED:] = low_or_high(theirs[:HDIM], turned(theirs[HDIM:])).astype(bf16)


def pack(query, key, value):
    wide = pltpu.VMEM((BLOCK, WIDTH), bf16)
    return kernel(
        pack_kernel,
        "pack",
        [HBM] * 3,
        [shaped((ROWS, PAIR), bf16)] * 2
        + [shaped((HALF, PAIR), bf16), shaped((SHARED + PAIR, PAIR), bf16)],
        [
            wide,
            wide,
            wide,
            pltpu.VMEM((2, BLOCK, PAIR), bf16),
            pltpu.VMEM((2, BLOCK, PAIR), f32),
            pltpu.SemaphoreType.DMA((3,)),
        ],
    )(in_hbm(query), in_hbm(key), in_hbm(value))


def label_kernel(clip, own_kv, out):
    out[:ROWS] = own_kv[...]
    clip_rows = jnp.broadcast_to(clip[...].astype(f32), (CLIP_ROWS, PAIR))
    out[ROWS:] = clip_rows.astype(bf16)


def label(clip, own_kv):
    return kernel(
        label_kernel,
        "label",
        [VMEM] * 2,
        [shaped((ROWS + CLIP_ROWS, PAIR), bf16)],
    )(clip, own_kv)[0]


def label_query_kernel(query, own, halo, out):
    out[:HALF] = query[...]
    out[HALF : HALF + CLIP_ROWS] = own[ROWS:]
    out[HALF + CLIP_ROWS :] = halo[ROWS:]


def label_query(query, own, halo):
    return kernel(
        label_query_kernel,
        "label_query",
        [VMEM] * 3,
        [shaped((HALF + 2 * CLIP_ROWS, PAIR), bf16)],
    )(query, own, halo)[0]


def unpacked_single(packed):
    packed = packed.astype(f32)
    top, bottom = low_or_high(packed, 0.0), low_or_high(turned(packed), 0.0)
    return jnp.concatenate([top, bottom], axis=0).astype(bf16)


def join_query(target, d_turned, single, query, query_single, d_pairs, d_shared):
    half = my_half()
    for pair in range(PAIRS):
        d_pair = d_pairs[:, pair * PAIR : (pair + 1) * PAIR].astype(bf16)
        target[rows_of(pair)] = query[rows_of(pair)]
        target[rows_of(PAIRS + pair)] = d_pair
        d_turned[head_rows(pair)] = d_pair.T
    single[0] = low_or_high(0.0, turned(d_shared)).astype(bf16)
    single[1] = low_or_high(0.0, d_shared).astype(bf16)
    d_single = single[half]
    target[rows_of(MIXED)] = query_single + d_single
    d_turned[single_rows()] = d_single.T[HDIM:]


def own_cotangent_kernel(cotangent, weight, query, both, d_turned, kept, rows, single, sems):
    half = my_half()
    chunk = rows.shape[1] // CHUNKS
    copies = [pltpu.make_async_copy(cotangent, rows, sems.at[CHUNKS])]
    for number in range(CHUNKS):
        part = pl.ds(number * chunk, chunk)
        copies.append(pltpu.make_async_copy(weight.at[part], kept.at[part], sems.at[number]))
    for copy in copies:
        copy.start()
    copies[0].wait()
    pairs = shared = None
    for number in range(CHUNKS):
        copies[number + 1].wait()
        part = slice(number * chunk, (number + 1) * chunk)
        columns = [kept[part, columns_of(half, pair)] for pair in range(PAIRS)]
        wide = times(rows[:, part], jnp.concatenate(columns, axis=1), ((1,), (0,)))
        narrow = times(rows[:, part], kept[part, SHARED : SHARED + PAIR], ((1,), (0,)))
        pairs = wide if pairs is None else pairs + wide
        shared = narrow if shared is None else shared + narrow
    join_query(both, d_turned, single, query, query[rows_of(PAIRS)], pairs, shared)


def own_cotangents(cotangent, weight, query):
    return kernel(
        own_cotangent_kernel,
        "own_cotangents",
        [HBM, HBM, VMEM],
        [shaped((ROWS, PAIR), bf16), shaped((HALF, BLOCK), bf16), shaped(weight.shape, bf16)],
        [
            pltpu.VMEM(cotangent.shape, bf16),
            pltpu.VMEM((2, BLOCK, PAIR), bf16),
            pltpu.SemaphoreType.DMA((CHUNKS + 1,)),
        ],
    )(in_hbm(cotangent), in_hbm(weight), query)


def cotangent_kernel(
    cotangent, weight, query, att, d_turned_own, totals, both, stats, d_turned, d_all, single
):
    half = my_half()
    rows = cotangent[...]
    columns = [weight[:, columns_of(half, pair)] for pair in range(PAIRS)]
    pairs = times(rows, jnp.concatenate(columns, axis=1), ((1,), (0,)))
    shared = times(rows, weight[:, SHARED : SHARED + PAIR], ((1,), (0,)))
    query_single = unpacked_single(query[SHARED:HALF])
    join_query(both, d_turned, single, query, query_single, pairs, shared)
    d_all[:, at(half, BLOCK)] = d_turned_own[...]
    d_all[:, at(1 - half, BLOCK)] = d_turned[...]
    stats[...] = totals[...]
    for query_block in range(2):
        steps = rows_of(query_block)
        for pair in range(PAIRS):
            which = head_rows(pair)
            dots = d_all[which, steps].astype(f32) * att[which, steps].astype(f32)
            row = DELTA_STAT + 2 * pair + query_block
            stats[row : row + 1, :BLOCK] = jnp.sum(dots[:HDIM], axis=0, keepdims=True)
            stats[row : row + 1, BLOCK:] = jnp.sum(dots[HDIM:], axis=0, keepdims=True)
        which = single_rows()
        dots = d_all[which, steps].astype(f32) * att[which, steps].astype(f32)
        row = DELTA_STAT + 2 * PAIRS + query_block
        stats[row : row + 1, :BLOCK] = jnp.sum(dots, axis=0, keepdims=True)
    rest = jnp.concatenate([stats[:, :BLOCK], stats[:, BLOCK:]], axis=0)
    for number in range(3):
        begin = ROWS + 2 * STAT_ROWS * number
        part = rest.astype(bf16)
        both[begin : begin + 2 * STAT_ROWS] = part
        rest = rest - part.astype(f32)


def stats_of(both):
    parts = []
    for number in range(3):
        begin = ROWS + 2 * STAT_ROWS * number
        parts.append(both[begin : begin + 2 * STAT_ROWS].astype(f32))
    total = (parts[0] + parts[1]) + parts[2]
    return jnp.concatenate([total[:STAT_ROWS], total[STAT_ROWS:]], axis=1)


def cotangents(cotangent, weight, query, att, d_turned_own, totals):
    return kernel(
        cotangent_kernel,
        "cotangents",
        [VMEM] * 6,
        [shaped((SENT_ROWS, PAIR), bf16), shaped((STAT_ROWS, 2 * BLOCK), f32)],
        [
            pltpu.VMEM((HALF, BLOCK), bf16),
            pltpu.VMEM((HALF, 2 * BLOCK), bf16),
            pltpu.VMEM((2, BLOCK, PAIR), bf16),
        ],
    )(cotangent, weight, query, att, d_turned_own, totals)


def gather_blocks(target, offset, own, partner):
    half = my_half()
    for block in range(target.shape[0]):
        target[block, at(offset + half, BLOCK)] = own[rows_of(block)]
        target[block, at(offset + 1 - half, BLOCK)] = partner[rows_of(block)]


def doubled(rows, factor=1.0):
    first = low_or_high(factor, 0.0).astype(bf16)
    second = low_or_high(0.0, factor).astype(bf16)
    return jnp.concatenate([rows * first, rows * second], axis=0)


def diagonal(pair):
    return jnp.concatenate([pair[:HDIM, :BLOCK], pair[HDIM:, BLOCK:]], axis=0)


def triangles():
    row = lax.broadcasted_iota(jnp.int32, (BLOCK, BLOCK), 0)
    lane = lax.broadcasted_iota(jnp.int32, (BLOCK, BLOCK), 1)
    older = jnp.where(row > lane, 1.0, 0.0)
    return older, jnp.ones((BLOCK, BLOCK), f32), 1.0 - older


def hidden(scores, visible):
    if scores.shape[1] > visible.shape[1]:
        visible = jnp.concatenate([visible, visible], axis=1)
    return jnp.where(visible > 0.5, scores, big_negative)


def gather_kernel(
    own, partner, halo, halo_other, query_own, query_partner, keys_all, query_all, mask, clip_row, clips
):
    half = my_half()
    gather_blocks(keys_all, 0, halo, halo_other)
    gather_blocks(keys_all, 2, own, partner)
    for pair in range(PAIRS):
        query_all[pair, at(half, BLOCK)] = query_own[rows_of(pair)]
        query_all[pair, at(1 - half, BLOCK)] = query_partner[rows_of(pair)]
    query_all[PAIRS, at(half, BLOCK)] = query_own[rows_of(PAIRS)]
    query_all[PAIRS, at(1 - half, BLOCK)] = unpacked_single(query_partner[SHARED:HALF])
    clips[at(half, CLIP_ROWS)] = halo[ROWS:]
    clips[at(1 - half, CLIP_ROWS)] = query_partner[HALF + CLIP_ROWS :]
    clips[at(2 + half, CLIP_ROWS)] = own[ROWS:]
    clips[at(3 - half, CLIP_ROWS)] = query_partner[HALF : HALF + CLIP_ROWS]

    def clip_of(block):
        return clips[block * CLIP_ROWS : (block + 1) * CLIP_ROWS].astype(f32)[0:1]

    for query_block in range(2):
        query_clip = clip_of(2 + query_block)
        for step, shape in enumerate(triangles()):
            block = query_block + step
            same = jnp.where(clip_of(block) == query_clip, 1.0, 0.0)
            present = jnp.where(2 * my_group() - 2 + block >= 0, 1.0, 0.0)
            mask[query_block, rows_of(step)] = shape * same * present
        clip_row[:, rows_of(query_block)] = query_clip


def gathered(*sources):
    return kernel(
        gather_kernel,
        "gathered",
        [VMEM] * 6,
        [
            shaped((MIXED + 1, 4 * BLOCK, PAIR), bf16),
            shaped((PAIRS + 1, 2 * BLOCK, PAIR), bf16),
            shaped((2, WIN + BLOCK, BLOCK), f32),
            shaped((1, 2 * BLOCK), f32),
            shaped((4 * CLIP_ROWS, PAIR), bf16),
        ],
        flops=COST_GATHER,
    )(*sources)


def staggered(items, *stages):
    values = [None] * len(items)
    for step in range(len(items) + 2 * len(stages) - 2):
        for number, stage in enumerate(stages):
            index = step - 2 * number
            if 0 <= index < len(items):
                values[index] = stage(*items[index], values[index])


def forward_kernel(
    pieces_wanted,
    keys_all,
    query_all,
    mask,
    clip_row,
    weights_out,
    single_out,
    totals,
    att,
    att_own,
    att_swap,
    *pieces,
):
    half = my_half()
    totals[CLIP_STAT : CLIP_STAT + 1] = clip_row[...]

    def softmax(scores, row):
        lanes = slice(0, scores.shape[1])
        maximum = jnp.max(scores, axis=0, keepdims=True)
        powers = jnp.exp(scores - maximum)
        total = jnp.sum(powers, axis=0, keepdims=True)
        totals[row : row + 1, lanes] = maximum + jnp.log(total)
        return (powers * (1.0 / total)).astype(bf16)

    def keys_of(query_block):
        return slice(query_block * BLOCK, query_block * BLOCK + WIN + BLOCK)

    def score(pair, query_block, _):
        rows = query_all[pair, rows_of(query_block)]
        if pair < PAIRS:
            key_rows, rows = keys_all[pair, keys_of(query_block)], doubled(rows, SCALING)
        else:
            key_rows = keys_all[MIXED, keys_of(query_block)]
            rows = rows * low_or_high(SCALING, 0.0).astype(bf16)
        return times(key_rows, rows, ((1,), (1,)))

    def weigh(pair, query_block, scores):
        return softmax(hidden(scores, mask[query_block]), 2 * pair + query_block)

    def mix(pair, query_block, weights):
        steps = rows_of(query_block)
        if pair < PAIRS:
            weights_out[pair, query_block] = weights
            mixed = times(keys_all[PAIRS + pair, keys_of(query_block)], weights, ((0,), (0,)))
            att[head_rows(pair), steps] = diagonal(mixed).astype(bf16)
        else:
            single_out[query_block] = weights
            mixed = times(keys_all[MIXED, keys_of(query_block)], weights, ((0,), (0,)))
            att[single_rows(), steps] = mixed[HDIM:].astype(bf16)

    items = [(pair, query_block) for pair in range(PAIRS + 1) for query_block in range(2)]
    staggered(items, score, weigh, mix)

    att[HALF:] = jnp.zeros((ATT_ROWS - HALF, 2 * BLOCK), bf16)
    att_own[...] = att[:HALF, at(half, BLOCK)]
    att_swap[...] = att[:HALF, at(1 - half, BLOCK)]
    for number, piece in enumerate(pieces):
        target = jnp.bitwise_xor(lax.axis_index("dp"), number)
        late = 32 * jnp.maximum(target - 2, 0)
        begin = jnp.where(half == 0, 160 * target - late, 128 * target + late)
        piece[...] = att[span(begin, PIECE_ROWS, 32), :]


def forward(pieces_wanted, *sources):
    piece = (PIECE_ROWS, 2 * BLOCK)
    return kernel(
        functools.partial(forward_kernel, pieces_wanted),
        "forward",
        [VMEM] * 4,
        [
            shaped((PAIRS, 2, WIN + BLOCK, 2 * BLOCK), bf16),
            shaped((2, WIN + BLOCK, BLOCK), bf16),
            shaped((STAT_ROWS, 2 * BLOCK), f32),
            shaped((ATT_ROWS, 2 * BLOCK), bf16),
            shaped((HALF, BLOCK), bf16),
            shaped((HALF, BLOCK), bf16),
        ]
        + [shaped(piece, bf16)] * pieces_wanted,
    )(*sources)


def own_kernel(
    keys_all,
    both_own,
    both_partner,
    weights_in,
    single_in,
    stats,
    att_swap,
    dq_own,
    swap,
    own_grads,
    partner_grads,
    query_all,
    dq_all,
    grads,
):
    half = my_half()
    gather_blocks(query_all, 0, both_own, both_partner)

    def delta_of(row, lanes):
        return stats[DELTA_STAT + row : DELTA_STAT + row + 1, :lanes]

    def accumulate(block, query_block, value):
        if query_block == 1:
            grads[block] = value
        else:
            grads[block, :BLOCK] += value

    def keys_of(query_block):
        return slice(query_block * BLOCK, query_block * BLOCK + WIN + BLOCK)

    def operands(pair, query_block):
        steps = rows_of(query_block)
        if pair < PAIRS:
            query_rows = doubled(query_all[pair, steps], SCALING)
            return query_rows, doubled(query_all[PAIRS + pair, steps]), weights_in[pair, query_block]
        rows = query_all[MIXED, steps]
        query_rows = rows * low_or_high(SCALING, 0.0).astype(bf16)
        d_rows = rows * low_or_high(0.0, 1.0).astype(bf16)
        return query_rows, d_rows, single_in[query_block]

    def d_weights_of(pair, query_block, _):
        block = PAIRS + pair if pair < PAIRS else MIXED
        _, d_rows, _ = operands(pair, query_block)
        return times(keys_all[block, keys_of(query_block)], d_rows, ((1,), (1,)))

    def d_scores_of(pair, query_block, d_weights):
        _, _, weights = operands(pair, query_block)
        delta = delta_of(2 * pair + query_block, d_weights.shape[1])
        return (weights.astype(f32) * (d_weights - delta)).astype(bf16)

    def products(pair, query_block, d_scores):
        query_rows, d_rows, weights = operands(pair, query_block)
        mine = slice(WIN - query_block * BLOCK, WIN + BLOCK)
        steps = rows_of(query_block)
        block = pair if pair < PAIRS else MIXED
        dq = times(keys_all[block, keys_of(query_block)], d_scores, ((0,), (0,)))
        dk = times(d_scores[mine], query_rows, ((1,), (0,)))
        dv = times(weights[mine], d_rows, ((1,), (0,)))
        if pair < PAIRS:
            dq_all[head_rows(pair), steps] = (diagonal(dq) * SCALING).astype(bf16)
            accumulate(pair, query_block, dk)
            accumulate(PAIRS + pair, query_block, dv)
        else:
            dq_all[single_rows(), steps] = (dq[:HDIM] * SCALING).astype(bf16)
            accumulate(MIXED, query_block, dk + dv)

    items = [(pair, query_block) for pair in range(PAIRS + 1) for query_block in (1, 0)]
    staggered(items, d_weights_of, d_scores_of, products)
    dq_own[...] = dq_all[:, at(half, BLOCK)]
    swap[:, :BLOCK] = att_swap[...]
    swap[:, BLOCK:] = dq_all[:, at(1 - half, BLOCK)]
    for block in range(MIXED + 1):
        own_grads[rows_of(block)] = grads[block, at(half, BLOCK)]
        partner_grads[rows_of(block)] = grads[block, at(1 - half, BLOCK)]


def own_gradients(*sources):
    return kernel(
        own_kernel,
        "own_gradients",
        [VMEM] * 7,
        [shaped((HALF, BLOCK), bf16), shaped((HALF, 2 * BLOCK), bf16)]
        + [shaped((ROWS, PAIR), f32)] * 2,
        [
            pltpu.VMEM((MIXED + 1, 2 * BLOCK, PAIR), bf16),
            pltpu.VMEM((HALF, 2 * BLOCK), bf16),
            pltpu.VMEM((MIXED + 1, 2 * BLOCK, PAIR), f32),
        ],
    )(*sources)


def next_kernel(
    groups,
    own,
    partner,
    both_own,
    both_partner,
    own_grads,
    partner_grads,
    clips,
    mine,
    swap,
    keys_all,
    query_all,
    mask,
    grads,
    stats,
):
    half = my_half()
    stats[...] = stats_of(both_partner)
    gather_blocks(keys_all, 0, own, partner)
    gather_blocks(query_all, 0, both_own, both_partner)
    for block in range(MIXED + 1):
        grads[block, at(half, BLOCK)] = own_grads[rows_of(block)]
        grads[block, at(1 - half, BLOCK)] = partner_grads[rows_of(block)]
    present = jnp.where(my_group() < groups - 1, 1.0, 0.0)
    older, every, _ = triangles()
    for query_block, block, shape in ((0, 0, older), (0, 1, every), (1, 1, older)):
        query_clip = stats[CLIP_STAT : CLIP_STAT + 1, rows_of(query_block)]
        key_clip = clips[(2 + block) * CLIP_ROWS : (3 + block) * CLIP_ROWS].astype(f32)[0:1]
        same = jnp.where(key_clip == query_clip, 1.0, 0.0)
        mask[query_block, rows_of(block)] = shape * same * present

    def operands(pair, query_block):
        steps = rows_of(query_block)
        if pair < PAIRS:
            query_rows = doubled(query_all[pair, steps], SCALING)
            return query_rows, doubled(query_all[PAIRS + pair, steps])
        rows = query_all[MIXED, steps]
        query_rows = rows * low_or_high(SCALING, 0.0).astype(bf16)
        return query_rows, rows * low_or_high(0.0, 1.0).astype(bf16)

    def score(pair, query_block, _):
        keys = slice(query_block * BLOCK, WIN)
        query_rows, d_rows = operands(pair, query_block)
        key_block, value_block = (pair, PAIRS + pair) if pair < PAIRS else (MIXED, MIXED)
        scores = times(keys_all[key_block, keys], query_rows, ((1,), (1,)))
        return scores, times(keys_all[value_block, keys], d_rows, ((1,), (1,)))

    def weigh(pair, query_block, values):
        scores, d_weights = values
        row = 2 * pair + query_block
        lanes = slice(0, scores.shape[1])
        scores = hidden(scores, mask[query_block, query_block * BLOCK : WIN])
        weights = jnp.exp(scores - stats[row : row + 1, lanes]).astype(bf16)
        delta = stats[DELTA_STAT + row : DELTA_STAT + row + 1, lanes]
        return weights, (weights.astype(f32) * (d_weights - delta)).astype(bf16)

    def products(pair, query_block, values):
        weights, d_scores = values
        keys = slice(query_block * BLOCK, WIN)
        query_rows, d_rows = operands(pair, query_block)
        dk = times(d_scores, query_rows, ((1,), (0,)))
        dv = times(weights, d_rows, ((1,), (0,)))
        if pair < PAIRS:
            grads[pair, keys] += dk
            grads[PAIRS + pair, keys] += dv
        else:
            grads[MIXED, keys] += dk + dv

    items = [(pair, query_block) for pair in range(PAIRS + 1) for query_block in range(2)]
    staggered(items, score, weigh, products)
    for block in range(MIXED + 1):
        mine[rows_of(block)] = grads[block, at(half, BLOCK)].astype(bf16)
        swap[rows_of(block)] = grads[block, at(1 - half, BLOCK)].astype(bf16)


def next_gradients(groups, *sources):
    return kernel(
        functools.partial(next_kernel, groups),
        "next_gradients",
        [VMEM] * 7,
        [shaped((ROWS, PAIR), bf16)] * 2,
        [
            pltpu.VMEM((MIXED + 1, 2 * BLOCK, PAIR), bf16),
            pltpu.VMEM((MIXED + 1, 2 * BLOCK, PAIR), bf16),
            pltpu.VMEM((2, 2 * BLOCK, BLOCK), f32),
            pltpu.VMEM((MIXED + 1, 2 * BLOCK, PAIR), f32),
            pltpu.VMEM((STAT_ROWS, 2 * BLOCK), f32),
        ],
        flops=COST_NEXT,
    )(*sources)


def join_halves(full, halves, mine, theirs):
    half = my_half()
    halves[half] = mine
    halves[1 - half] = theirs
    for side in range(2):
        for pair in range(PAIRS):
            full[rows_of(FIRST_BLOCKS[pair] + side)] = halves[side, head_rows(pair)]
        begin = SHARED + side * HDIM
        full[begin : begin + HDIM] = halves[side, single_rows()]


def output_kernel(att_own, received, dq_mine, weight, out, query_out, full, dq_all, halves, query, sem):
    join_halves(dq_all, halves, dq_mine[...], received[:, BLOCK:])
    for block in range(WIDTH // PAIR):
        query[:, block * PAIR : (block + 1) * PAIR] = dq_all[rows_of(block)].T
    copy = pltpu.make_async_copy(query, query_out, sem)
    copy.start()
    join_halves(full, halves, att_own[...], received[:, :BLOCK])
    out[...] = times(weight[...], full[...], ((1,), (0,))).T.astype(bf16)
    copy.wait()


def output_rows(att_own, received, dq_mine, weight):
    return kernel(
        output_kernel,
        "output",
        [VMEM] * 4,
        [
            shaped((BLOCK, weight.shape[0]), bf16),
            shaped((BLOCK, WIDTH), bf16),
            shaped((WIDTH, BLOCK), bf16),
        ],
        [
            pltpu.VMEM((WIDTH, BLOCK), bf16),
            pltpu.VMEM((2, HALF, BLOCK), bf16),
            pltpu.VMEM((BLOCK, WIDTH), bf16),
            pltpu.SemaphoreType.DMA,
        ],
        (VMEM, HBM, VMEM),
    )(att_own, received, dq_mine, weight)


def place_kernel(
    mine, theirs, kept, arrived, key_out, value_out, weight_out, key, value, mixed, parts, total, sems
):
    half = my_half()
    moves = [(total, weight_out), (key, key_out), (value, value_out)]
    copies = [pltpu.make_async_copy(a, b, sems.at[n]) for n, (a, b) in enumerate(moves)]
    for side, source in ((half, mine), (1 - half, theirs)):
        for pair in range(PAIRS):
            key[:, columns_of(side, pair)] = source[rows_of(pair)]
            value[:, columns_of(side, pair)] = source[rows_of(PAIRS + pair)]
        mixed[side] = source[rows_of(MIXED)].astype(f32)
    shared = slice(SHARED, SHARED + PAIR)
    key[:, shared] = low_or_high(mixed[0], turned(mixed[1])).astype(bf16)
    copies[1].start()
    value[:, shared] = low_or_high(turned(mixed[0]), mixed[1]).astype(bf16)
    copies[2].start()
    parts[half] = kept[...]
    parts[1 - half] = arrived[...].astype(f32)
    for sequence, segments in enumerate(SEGMENTS):

        @pl.when(lax.axis_index("dp") == sequence)
        def _():
            for side, source, size, target in segments:
                total[target : target + size] = parts[side, source : source + size]

    copies[0].start()
    for copy in copies:
        copy.wait()


def place(*sources):
    weight_rows = 2 * HALF // len(SEGMENTS)
    wide = pltpu.VMEM((BLOCK, WIDTH), bf16)
    *grads, weight = kernel(
        place_kernel,
        "place",
        [VMEM] * 4,
        [shaped((BLOCK, WIDTH), bf16)] * 2 + [shaped((weight_rows, BLOCK), f32)],
        [
            wide,
            wide,
            pltpu.VMEM((2, BLOCK, PAIR), f32),
            pltpu.VMEM((2, PIECE_ROWS, BLOCK), f32),
            pltpu.VMEM((weight_rows, BLOCK), f32),
            pltpu.SemaphoreType.DMA((3,)),
        ],
        (HBM,) * 3,
    )(*sources)
    return *grads, weight.T


def weight_kernel(count, *refs):
    pieces, cots, products = refs[:count], refs[count : 2 * count], refs[-1]
    half = my_half()
    att = jnp.concatenate([piece[:, at(half, BLOCK)] for piece in pieces], axis=1)
    products[...] = times(att, jnp.concatenate([cot[...] for cot in cots], axis=0), ((1,), (0,)))


def weight_products(pieces, cots):
    return kernel(
        functools.partial(weight_kernel, len(pieces)),
        "weight_products",
        [VMEM] * (2 * len(pieces)),
        [shaped((pieces[0].shape[0], cots[0].shape[1]), f32)],
        flops=COST_FIRST,
    )(*pieces, *cots)[0]


def weight_rest_kernel(count, products, *refs):
    pieces, cots = refs[:count], refs[count : 2 * count]
    kept, *sent = refs[2 * count :]
    total = sent.pop()
    half = my_half()
    att = jnp.concatenate([piece[:, at(1 - half, BLOCK)] for piece in pieces], axis=1)
    cot = jnp.concatenate([cot[...] for cot in cots], axis=0)
    total[...] = products[...] + times(att, cot, ((1,), (0,)))
    group = my_group()
    lanes = kept.shape[1]
    kept[...] = total[:, at(group, lanes)]
    for number, out in enumerate(sent):
        target = jnp.bitwise_xor(group, number + 1)
        out[...] = total[:, at(target, lanes)].astype(bf16)


def weight_rest(products, pieces, cots, groups):
    rows, outs = products.shape
    part = (rows, outs // groups)
    return kernel(
        functools.partial(weight_rest_kernel, len(pieces)),
        "weight_rest",
        [VMEM] * (1 + 2 * len(pieces)),
        [shaped(part, f32)] + [shaped(part, bf16)] * (groups - 1),
        [pltpu.VMEM((rows, outs), f32)],
    )(products, *pieces, *cots)


def weight_sum_kernel(kept, *rest):
    received, (mine, sent, total) = rest[:-3], rest[-3:]
    value = kept[...]
    for part in received:
        value = value + part[...].astype(f32)
    total[...] = value
    half = my_half()
    mine[...] = total[:, at(half, BLOCK)]
    sent[...] = total[:, at(1 - half, BLOCK)].astype(bf16)


def weight_sum(kept, received):
    rows, lanes = kept.shape
    return kernel(
        weight_sum_kernel,
        "weight_sum",
        [VMEM] * (1 + len(received)),
        [shaped((rows, BLOCK), f32), shaped((rows, BLOCK), bf16)],
        [pltpu.VMEM((rows, lanes), f32)],
        flops=COST_SUM,
    )(kept, *received)


def swapped(value, axis, bits):
    count = lax.axis_size(axis)
    return lax.ppermute(value, axis, [(source, source ^ bits) for source in range(count)])


def rotated(value, axis, steps):
    count = lax.axis_size(axis)
    return lax.ppermute(
        value, axis, [(source, (source + steps) % count) for source in range(count)]
    )


def moved(value, axis, steps):
    count = lax.axis_size(axis)
    first, last = (max(0, -steps), min(count, count - steps))
    return lax.ppermute(value, axis, [(source, source + steps) for source in range(first, last)])


def after(*values):
    return lax.optimization_barrier(values)


def per_device(queries, key_states, value_states, out_cotangent, out_weight, block_clip):
    sequences = lax.axis_size("dp")
    groups = lax.axis_size("ctx") // 2
    short = sequences == 4 and groups in (2, 4)
    cotangent = out_cotangent[0]

    swap_kv, own_kv, swap_query, query = pack(queries[0], key_states[0], value_states[0])
    swap_kv, cot_early, clip = after(swap_kv, cotangent, block_clip)
    own = label(clip, own_kv)
    partner = swapped(swap_kv, "ctx", 1)
    halo = rotated(own, "ctx", 2)
    both_own, d_turned_own, weight = own_cotangents(cotangent, out_weight, query)
    cots = [cotangent]
    if short:
        cots += [swapped(cot_early, "dp", n) for n in (1, 2)]

    partner, both_own, swap_query, cot_late = after(partner, both_own, swap_query, cotangent)
    cot_partner = swapped(cot_late, "ctx", 1)
    halo_other = rotated(partner, "ctx", 2)
    query_partner = swapped(label_query(swap_query, own, halo), "ctx", 1)
    halo, both_own, *cots = after(halo, both_own, *cots)
    next_own = moved(both_own, "ctx", -2)
    if short:
        cots.append(swapped(cots[2], "dp", 1))
    keys_all, query_all, mask, clip_row, clips = gathered(
        own, partner, halo, halo_other, query, query_partner
    )
    weights, single, totals, att, att_own, att_swap, *pieces = forward(
        4 if short else 0, keys_all, query_all, mask, clip_row
    )
    if short:
        cot_across = swapped(cot_partner, "dp", 2)
    weights, cot_partner, *pieces = after(weights, cot_partner, *pieces)

    if short:
        pieces[1:] = [swapped(pieces[n], "dp", n) for n in (1, 2, 3)]
    both_partner, stats = cotangents(
        cot_partner, weight, query_partner, att, d_turned_own, totals
    )
    both_partner, next_own, *cots = after(both_partner, next_own, *cots)
    next_partner = rotated(both_partner, "ctx", -2)
    dq_own, swap, own_grads, partner_grads = own_gradients(
        keys_all, both_own, both_partner, weights, single, stats, att_swap
    )
    own_grads, swap, *pieces = after(own_grads, swap, *pieces)

    if short:
        own_grads, cot_partner, cot_across = after(own_grads, cot_partner, cot_across)
        later = [cot_partner, swapped(cot_partner, "dp", 1), cot_across]
        later.append(swapped(cot_across, "dp", 1))
        products = weight_products(pieces, cots)
        products, swap = after(products, swap)
        kept, *sent = weight_rest(products, pieces, later, groups)
        arrived = [swapped(part, "ctx", 2 * (n + 1)) for n, part in enumerate(sent)]
        kept, own_grads = after(kept, own_grads)
    received = swapped(swap, "ctx", 1)
    kv_own, kv_swap = next_gradients(
        groups, own, partner, next_own, next_partner, own_grads, partner_grads, clips
    )
    kv_rest = swapped(kv_swap, "ctx", 1)
    kv_own, received = after(kv_own, received)
    sublayer_out, query_grad, att_full = output_rows(att_own, received, dq_own, weight)
    if short:
        kept, kv_own, sublayer_out, *arrived = after(kept, kv_own, sublayer_out, *arrived)
        kept, sent = weight_sum(kept, arrived)
        arrived = swapped(sent, "ctx", 1)
    if not short:
        product = lax.dot_general(
            cotangent, att_full, (((0,), (1,)), ((), ())), preferred_element_type=f32
        ).astype(bf16)
        sequence_grad = lax.psum_scatter(product, "ctx", scatter_dimension=0, tiled=True)
        weight_grad = lax.psum_scatter(
            sequence_grad.astype(f32), "dp", scatter_dimension=1, tiled=True
        )
        kept = jnp.zeros((PIECE_ROWS, BLOCK), f32)
        arrived = kept.astype(bf16)
    key_grad, value_grad, placed_weight = place(kv_own, kv_rest, kept, arrived)
    if short:
        weight_grad = placed_weight
    return (
        sublayer_out[None],
        query_grad[None],
        key_grad[None],
        value_grad[None],
        weight_grad,
    )


def solution(mesh):
    return jax.shard_map(
        per_device,
        mesh=mesh,
        in_specs=(
            P("dp", "ctx", None),
            P("dp", "ctx", None),
            P("dp", "ctx", None),
            P("dp", "ctx", None),
            P(),
            P("dp", "ctx"),
        ),
        out_specs=(
            P("dp", "ctx", None),
            P("dp", "ctx", None),
            P("dp", "ctx", None),
            P("dp", "ctx", None),
            P("ctx", "dp"),
        ),
        check_vma=False,
    )
```

```python
import functools
import math

import jax
import jax.numpy as jnp
from jax import lax
from jax.experimental import pallas as pl
from jax.experimental.pallas import tpu as pltpu
from jax.sharding import PartitionSpec as P

HEADS = 18
HDIM = 64
BLOCK = 128
WIN = 256
PAIR = 2 * HDIM
WIDTH = HEADS * HDIM
HALF = WIDTH // 2
PAIRS = HEADS // 4
SHARED = PAIRS * PAIR
MIXED = 2 * PAIRS
ROWS = (MIXED + 1) * BLOCK
FIRST_BLOCKS = (0, 2, 5, 7)
HEAD_STARTS = (0, 128, 320, 448)
SINGLE_START = 256
PIECE_ROWS = 160
ATT_ROWS = HEAD_STARTS[-1] + PIECE_ROWS
SEGMENTS = (
    ((0, 0, 128, 0), (0, 128, 32, 256), (1, 0, 128, 128)),
    ((0, 0, 96, 0), (0, 96, 64, 224), (1, 0, 128, 96)),
    ((0, 0, 128, 64), (1, 0, 64, 0), (1, 64, 96, 192)),
    ((0, 0, 128, 32), (1, 0, 32, 0), (1, 32, 128, 160)),
)
CLIP_ROWS = 16
CLIP_STAT = 2 * PAIRS + 2
DELTA_STAT = CLIP_STAT + 2
STAT_ROWS = 24
SENT_ROWS = ROWS + 6 * STAT_ROWS
CHUNKS = 4
SCALING = 1.0 / math.sqrt(HDIM)
COST_GATHER = 1_500_000_000
COST_KEYS = 1_000_000
COST_FIRST = 2_000_000_000
COST_NEXT = 4_000_000_000
COST_SUM = 2_000_000_000
VMEM_LIMIT = 24 * 1024 * 1024

big_negative = -1e30
bf16 = jnp.bfloat16
f32 = jnp.float32

VMEM = pl.BlockSpec(memory_space=pltpu.VMEM)
HBM = pl.BlockSpec(memory_space=pltpu.HBM)


def shaped(shape, dtype):
    return jax.ShapeDtypeStruct(shape, dtype)


def kernel(body, name, ins, outs, scratch=(), spaces=None, flops=1_000_000):
    return pl.pallas_call(
        body,
        out_shape=tuple(outs),
        in_specs=list(ins),
        out_specs=spaces or (VMEM,) * len(outs),
        scratch_shapes=list(scratch),
        compiler_params=pltpu.CompilerParams(vmem_limit_bytes=VMEM_LIMIT),
        cost_estimate=pl.CostEstimate(flops=flops, bytes_accessed=10_000, transcendentals=0),
        name=name,
    )


def in_hbm(value):
    return pltpu.with_memory_space_constraint(value, pltpu.HBM)


def my_half():
    return jnp.bitwise_and(lax.axis_index("ctx"), 1)


def my_group():
    return jnp.right_shift(lax.axis_index("ctx"), 1)


def at(index, size):
    return pl.ds(pl.multiple_of(index * size, size), size)


def span(start, size, unit):
    return pl.ds(pl.multiple_of(start, unit), size)


def rows_of(block):
    return slice(block * BLOCK, (block + 1) * BLOCK)


def columns_of(half, pair):
    return span((FIRST_BLOCKS[pair] + half) * PAIR, PAIR, PAIR)


def head_rows(pair):
    return slice(HEAD_STARTS[pair], HEAD_STARTS[pair] + PAIR)


def single_rows():
    return slice(SINGLE_START, SINGLE_START + HDIM)


def times(a, b, dims):
    return lax.dot_general(a, b, (dims, ((), ())), preferred_element_type=f32)


def is_low():
    return lax.broadcasted_iota(jnp.int32, (1, PAIR), 1) < HDIM


def low_or_high(low_value, high_value):
    return jnp.where(is_low(), low_value, high_value)


def turned(value):
    return pltpu.roll(value, HDIM, 1)


def pack_kernel(query, key, value, swap_kv, own_kv, swap_query, own_query, *scratch):
    query_all, key_all, value_all, mixed, single, sems = scratch
    half = my_half()
    pairs = ((key, key_all), (value, value_all), (query, query_all))
    copies = [pltpu.make_async_copy(a, b, sems.at[n]) for n, (a, b) in enumerate(pairs)]
    for copy in copies:
        copy.start()
    shared = slice(SHARED, SHARED + PAIR)
    for copy in copies[:2]:
        copy.wait()
    for side, target in ((1 - half, swap_kv), (half, own_kv)):
        for pair in range(PAIRS):
            target[rows_of(pair)] = key_all[:, columns_of(side, pair)]
            target[rows_of(PAIRS + pair)] = value_all[:, columns_of(side, pair)]
    key_shared = key_all[:, shared].astype(f32)
    value_shared = value_all[:, shared].astype(f32)
    mixed[0] = low_or_high(key_shared, turned(value_shared)).astype(bf16)
    mixed[1] = low_or_high(turned(key_shared), value_shared).astype(bf16)
    swap_kv[rows_of(MIXED)] = mixed[1 - half]
    own_kv[rows_of(MIXED)] = mixed[half]
    copies[2].wait()
    for pair in range(PAIRS):
        swap_query[rows_of(pair)] = query_all[:, columns_of(1 - half, pair)]
        own_query[rows_of(pair)] = query_all[:, columns_of(half, pair)]
    query_shared = query_all[:, shared].astype(f32)
    single[0] = low_or_high(query_shared, 0.0)
    single[1] = low_or_high(turned(query_shared), 0.0)
    own_query[rows_of(PAIRS)] = single[half].astype(bf16)
    theirs = single[1 - half]
    swap_query[SHARED:] = low_or_high(theirs[:HDIM], turned(theirs[HDIM:])).astype(bf16)


def pack(query, key, value):
    wide = pltpu.VMEM((BLOCK, WIDTH), bf16)
    return kernel(
        pack_kernel,
        "pack",
        [HBM] * 3,
        [shaped((ROWS, PAIR), bf16)] * 2
        + [shaped((HALF, PAIR), bf16), shaped((SHARED + PAIR, PAIR), bf16)],
        [
            wide,
            wide,
            wide,
            pltpu.VMEM((2, BLOCK, PAIR), bf16),
            pltpu.VMEM((2, BLOCK, PAIR), f32),
            pltpu.SemaphoreType.DMA((3,)),
        ],
    )(in_hbm(query), in_hbm(key), in_hbm(value))


def label_kernel(clip, own_kv, out):
    out[:ROWS] = own_kv[...]
    clip_rows = jnp.broadcast_to(clip[...].astype(f32), (CLIP_ROWS, PAIR))
    out[ROWS:] = clip_rows.astype(bf16)


def label(clip, own_kv):
    return kernel(
        label_kernel,
        "label",
        [VMEM] * 2,
        [shaped((ROWS + CLIP_ROWS, PAIR), bf16)],
    )(clip, own_kv)[0]


def label_query_kernel(query, own, halo, out):
    out[:HALF] = query[...]
    out[HALF : HALF + CLIP_ROWS] = own[ROWS:]
    out[HALF + CLIP_ROWS :] = halo[ROWS:]


def label_query(query, own, halo):
    return kernel(
        label_query_kernel,
        "label_query",
        [VMEM] * 3,
        [shaped((HALF + 2 * CLIP_ROWS, PAIR), bf16)],
    )(query, own, halo)[0]


def unpacked_single(packed):
    packed = packed.astype(f32)
    top, bottom = low_or_high(packed, 0.0), low_or_high(turned(packed), 0.0)
    return jnp.concatenate([top, bottom], axis=0).astype(bf16)


def join_query(target, d_turned, single, query, query_single, d_pairs, d_shared):
    half = my_half()
    for pair in range(PAIRS):
        d_pair = d_pairs[:, pair * PAIR : (pair + 1) * PAIR].astype(bf16)
        target[rows_of(pair)] = query[rows_of(pair)]
        target[rows_of(PAIRS + pair)] = d_pair
        d_turned[head_rows(pair)] = d_pair.T
    single[0] = low_or_high(0.0, turned(d_shared)).astype(bf16)
    single[1] = low_or_high(0.0, d_shared).astype(bf16)
    d_single = single[half]
    target[rows_of(MIXED)] = query_single + d_single
    d_turned[single_rows()] = d_single.T[HDIM:]


def own_cotangent_kernel(cotangent, weight, query, both, d_turned, kept, rows, single, sems):
    half = my_half()
    chunk = rows.shape[1] // CHUNKS
    copies = [pltpu.make_async_copy(cotangent, rows, sems.at[CHUNKS])]
    for number in range(CHUNKS):
        part = pl.ds(number * chunk, chunk)
        copies.append(pltpu.make_async_copy(weight.at[part], kept.at[part], sems.at[number]))
    for copy in copies:
        copy.start()
    copies[0].wait()
    pairs = shared = None
    for number in range(CHUNKS):
        copies[number + 1].wait()
        part = slice(number * chunk, (number + 1) * chunk)
        columns = [kept[part, columns_of(half, pair)] for pair in range(PAIRS)]
        wide = times(rows[:, part], jnp.concatenate(columns, axis=1), ((1,), (0,)))
        narrow = times(rows[:, part], kept[part, SHARED : SHARED + PAIR], ((1,), (0,)))
        pairs = wide if pairs is None else pairs + wide
        shared = narrow if shared is None else shared + narrow
    join_query(both, d_turned, single, query, query[rows_of(PAIRS)], pairs, shared)


def own_cotangents(cotangent, weight, query):
    return kernel(
        own_cotangent_kernel,
        "own_cotangents",
        [HBM, HBM, VMEM],
        [shaped((ROWS, PAIR), bf16), shaped((HALF, BLOCK), bf16), shaped(weight.shape, bf16)],
        [
            pltpu.VMEM(cotangent.shape, bf16),
            pltpu.VMEM((2, BLOCK, PAIR), bf16),
            pltpu.SemaphoreType.DMA((CHUNKS + 1,)),
        ],
    )(in_hbm(cotangent), in_hbm(weight), query)


def cotangent_kernel(
    cotangent, weight, query, att, d_turned_own, totals, both, stats, d_turned, d_all, single
):
    half = my_half()
    rows = cotangent[...]
    columns = [weight[:, columns_of(half, pair)] for pair in range(PAIRS)]
    pairs = times(rows, jnp.concatenate(columns, axis=1), ((1,), (0,)))
    shared = times(rows, weight[:, SHARED : SHARED + PAIR], ((1,), (0,)))
    query_single = unpacked_single(query[SHARED:HALF])
    join_query(both, d_turned, single, query, query_single, pairs, shared)
    d_all[:, at(half, BLOCK)] = d_turned_own[...]
    d_all[:, at(1 - half, BLOCK)] = d_turned[...]
    stats[...] = totals[...]
    for query_block in range(2):
        steps = rows_of(query_block)
        for pair in range(PAIRS):
            which = head_rows(pair)
            dots = d_all[which, steps].astype(f32) * att[which, steps].astype(f32)
            row = DELTA_STAT + 2 * pair + query_block
            stats[row : row + 1, :BLOCK] = jnp.sum(dots[:HDIM], axis=0, keepdims=True)
            stats[row : row + 1, BLOCK:] = jnp.sum(dots[HDIM:], axis=0, keepdims=True)
        which = single_rows()
        dots = d_all[which, steps].astype(f32) * att[which, steps].astype(f32)
        row = DELTA_STAT + 2 * PAIRS + query_block
        stats[row : row + 1, :BLOCK] = jnp.sum(dots, axis=0, keepdims=True)
    rest = jnp.concatenate([stats[:, :BLOCK], stats[:, BLOCK:]], axis=0)
    for number in range(3):
        begin = ROWS + 2 * STAT_ROWS * number
        part = rest.astype(bf16)
        both[begin : begin + 2 * STAT_ROWS] = part
        rest = rest - part.astype(f32)


def stats_of(both):
    parts = []
    for number in range(3):
        begin = ROWS + 2 * STAT_ROWS * number
        parts.append(both[begin : begin + 2 * STAT_ROWS].astype(f32))
    total = (parts[0] + parts[1]) + parts[2]
    return jnp.concatenate([total[:STAT_ROWS], total[STAT_ROWS:]], axis=1)


def cotangents(cotangent, weight, query, att, d_turned_own, totals):
    return kernel(
        cotangent_kernel,
        "cotangents",
        [VMEM] * 6,
        [shaped((SENT_ROWS, PAIR), bf16), shaped((STAT_ROWS, 2 * BLOCK), f32)],
        [
            pltpu.VMEM((HALF, BLOCK), bf16),
            pltpu.VMEM((HALF, 2 * BLOCK), bf16),
            pltpu.VMEM((2, BLOCK, PAIR), bf16),
        ],
    )(cotangent, weight, query, att, d_turned_own, totals)


def gather_blocks(target, offset, own, partner):
    half = my_half()
    for block in range(target.shape[0]):
        target[block, at(offset + half, BLOCK)] = own[rows_of(block)]
        target[block, at(offset + 1 - half, BLOCK)] = partner[rows_of(block)]


def doubled(rows, factor=1.0):
    first = low_or_high(factor, 0.0).astype(bf16)
    second = low_or_high(0.0, factor).astype(bf16)
    return jnp.concatenate([rows * first, rows * second], axis=0)


def diagonal(pair):
    return jnp.concatenate([pair[:HDIM, :BLOCK], pair[HDIM:, BLOCK:]], axis=0)


def triangles():
    row = lax.broadcasted_iota(jnp.int32, (BLOCK, BLOCK), 0)
    lane = lax.broadcasted_iota(jnp.int32, (BLOCK, BLOCK), 1)
    older = jnp.where(row > lane, 1.0, 0.0)
    return older, jnp.ones((BLOCK, BLOCK), f32), 1.0 - older


def hidden(scores, visible):
    if scores.shape[1] > visible.shape[1]:
        visible = jnp.concatenate([visible, visible], axis=1)
    return jnp.where(visible > 0.5, scores, big_negative)


def gather_kernel(
    own, partner, halo, halo_other, query_own, query_partner, keys_all, query_all, mask, clip_row, clips
):
    half = my_half()
    gather_blocks(keys_all, 0, halo, halo_other)
    gather_blocks(keys_all, 2, own, partner)
    for pair in range(PAIRS):
        query_all[pair, at(half, BLOCK)] = query_own[rows_of(pair)]
        query_all[pair, at(1 - half, BLOCK)] = query_partner[rows_of(pair)]
    query_all[PAIRS, at(half, BLOCK)] = query_own[rows_of(PAIRS)]
    query_all[PAIRS, at(1 - half, BLOCK)] = unpacked_single(query_partner[SHARED:HALF])
    clips[at(half, CLIP_ROWS)] = halo[ROWS:]
    clips[at(1 - half, CLIP_ROWS)] = query_partner[HALF + CLIP_ROWS :]
    clips[at(2 + half, CLIP_ROWS)] = own[ROWS:]
    clips[at(3 - half, CLIP_ROWS)] = query_partner[HALF : HALF + CLIP_ROWS]

    def clip_of(block):
        return clips[block * CLIP_ROWS : (block + 1) * CLIP_ROWS].astype(f32)[0:1]

    for query_block in range(2):
        query_clip = clip_of(2 + query_block)
        for step, shape in enumerate(triangles()):
            block = query_block + step
            same = jnp.where(clip_of(block) == query_clip, 1.0, 0.0)
            present = jnp.where(2 * my_group() - 2 + block >= 0, 1.0, 0.0)
            mask[query_block, rows_of(step)] = shape * same * present
        clip_row[:, rows_of(query_block)] = query_clip


def gathered(*sources):
    return kernel(
        gather_kernel,
        "gathered",
        [VMEM] * 6,
        [
            shaped((MIXED + 1, 4 * BLOCK, PAIR), bf16),
            shaped((PAIRS + 1, 2 * BLOCK, PAIR), bf16),
            shaped((2, WIN + BLOCK, BLOCK), f32),
            shaped((1, 2 * BLOCK), f32),
            shaped((4 * CLIP_ROWS, PAIR), bf16),
        ],
        flops=COST_GATHER,
    )(*sources)


def staggered(items, apart, *stages):
    values = [None] * len(items)
    for step in range(len(items) + apart * (len(stages) - 1)):
        for number, stage in enumerate(stages):
            index = step - apart * number
            if 0 <= index < len(items):
                values[index] = stage(*items[index], values[index])


def forward_kernel(
    pieces_wanted,
    keys_all,
    query_all,
    mask,
    clip_row,
    weights_out,
    single_out,
    totals,
    att,
    att_own,
    att_swap,
    *pieces,
):
    half = my_half()
    totals[CLIP_STAT : CLIP_STAT + 1] = clip_row[...]

    def softmax(scores, row):
        lanes = slice(0, scores.shape[1])
        maximum = jnp.max(scores, axis=0, keepdims=True)
        powers = jnp.exp(scores - maximum)
        total = jnp.sum(powers, axis=0, keepdims=True)
        totals[row : row + 1, lanes] = maximum + jnp.log(total)
        return (powers * (1.0 / total)).astype(bf16)

    def keys_of(query_block):
        return slice(query_block * BLOCK, query_block * BLOCK + WIN + BLOCK)

    def score(pair, query_block, _):
        rows = query_all[pair, rows_of(query_block)]
        if pair < PAIRS:
            key_rows, rows = keys_all[pair, keys_of(query_block)], doubled(rows, SCALING)
        else:
            key_rows = keys_all[MIXED, keys_of(query_block)]
            rows = rows * low_or_high(SCALING, 0.0).astype(bf16)
        return times(key_rows, rows, ((1,), (1,)))

    def weigh(pair, query_block, scores):
        return softmax(hidden(scores, mask[query_block]), 2 * pair + query_block)

    def mix(pair, query_block, weights):
        steps = rows_of(query_block)
        if pair < PAIRS:
            weights_out[pair, query_block] = weights
            mixed = times(keys_all[PAIRS + pair, keys_of(query_block)], weights, ((0,), (0,)))
            att[head_rows(pair), steps] = diagonal(mixed).astype(bf16)
        else:
            single_out[query_block] = weights
            mixed = times(keys_all[MIXED, keys_of(query_block)], weights, ((0,), (0,)))
            att[single_rows(), steps] = mixed[HDIM:].astype(bf16)

    items = [(pair, query_block) for pair in range(PAIRS + 1) for query_block in range(2)]
    staggered(items, 3, score, weigh, mix)

    att[HALF:] = jnp.zeros((ATT_ROWS - HALF, 2 * BLOCK), bf16)
    att_own[...] = att[:HALF, at(half, BLOCK)]
    att_swap[...] = att[:HALF, at(1 - half, BLOCK)]
    for number, piece in enumerate(pieces):
        target = jnp.bitwise_xor(lax.axis_index("dp"), number)
        late = 32 * jnp.maximum(target - 2, 0)
        begin = jnp.where(half == 0, 160 * target - late, 128 * target + late)
        piece[...] = att[span(begin, PIECE_ROWS, 32), :]


def forward(pieces_wanted, *sources):
    piece = (PIECE_ROWS, 2 * BLOCK)
    return kernel(
        functools.partial(forward_kernel, pieces_wanted),
        "forward",
        [VMEM] * 4,
        [
            shaped((PAIRS, 2, WIN + BLOCK, 2 * BLOCK), bf16),
            shaped((2, WIN + BLOCK, BLOCK), bf16),
            shaped((STAT_ROWS, 2 * BLOCK), f32),
            shaped((ATT_ROWS, 2 * BLOCK), bf16),
            shaped((HALF, BLOCK), bf16),
            shaped((HALF, BLOCK), bf16),
        ]
        + [shaped(piece, bf16)] * pieces_wanted,
    )(*sources)


def own_kernel(
    keys_all,
    both_own,
    both_partner,
    weights_in,
    single_in,
    stats,
    att_swap,
    dq_own,
    swap,
    own_grads,
    partner_grads,
    query_all,
    dq_all,
    grads,
):
    half = my_half()
    gather_blocks(query_all, 0, both_own, both_partner)

    def delta_of(row, lanes):
        return stats[DELTA_STAT + row : DELTA_STAT + row + 1, :lanes]

    def accumulate(block, query_block, value):
        if query_block == 1:
            grads[block] = value
        else:
            grads[block, :BLOCK] += value

    def keys_of(query_block):
        return slice(query_block * BLOCK, query_block * BLOCK + WIN + BLOCK)

    def operands(pair, query_block):
        steps = rows_of(query_block)
        if pair < PAIRS:
            query_rows = doubled(query_all[pair, steps], SCALING)
            return query_rows, doubled(query_all[PAIRS + pair, steps]), weights_in[pair, query_block]
        rows = query_all[MIXED, steps]
        query_rows = rows * low_or_high(SCALING, 0.0).astype(bf16)
        d_rows = rows * low_or_high(0.0, 1.0).astype(bf16)
        return query_rows, d_rows, single_in[query_block]

    def d_weights_of(pair, query_block, _):
        block = PAIRS + pair if pair < PAIRS else MIXED
        _, d_rows, _ = operands(pair, query_block)
        return times(keys_all[block, keys_of(query_block)], d_rows, ((1,), (1,)))

    def d_scores_of(pair, query_block, d_weights):
        _, _, weights = operands(pair, query_block)
        delta = delta_of(2 * pair + query_block, d_weights.shape[1])
        return (weights.astype(f32) * (d_weights - delta)).astype(bf16)

    def products(pair, query_block, d_scores):
        query_rows, d_rows, weights = operands(pair, query_block)
        mine = slice(WIN - query_block * BLOCK, WIN + BLOCK)
        steps = rows_of(query_block)
        block = pair if pair < PAIRS else MIXED
        dq = times(keys_all[block, keys_of(query_block)], d_scores, ((0,), (0,)))
        dk = times(d_scores[mine], query_rows, ((1,), (0,)))
        dv = times(weights[mine], d_rows, ((1,), (0,)))
        if pair < PAIRS:
            dq_all[head_rows(pair), steps] = (diagonal(dq) * SCALING).astype(bf16)
            accumulate(pair, query_block, dk)
            accumulate(PAIRS + pair, query_block, dv)
        else:
            dq_all[single_rows(), steps] = (dq[:HDIM] * SCALING).astype(bf16)
            accumulate(MIXED, query_block, dk + dv)

    items = [(pair, query_block) for pair in range(PAIRS + 1) for query_block in (1, 0)]
    staggered(items, 2, d_weights_of, d_scores_of, products)
    dq_own[...] = dq_all[:, at(half, BLOCK)]
    swap[:, :BLOCK] = att_swap[...]
    swap[:, BLOCK:] = dq_all[:, at(1 - half, BLOCK)]
    for block in range(MIXED + 1):
        own_grads[rows_of(block)] = grads[block, at(half, BLOCK)]
        partner_grads[rows_of(block)] = grads[block, at(1 - half, BLOCK)]


def own_gradients(*sources):
    return kernel(
        own_kernel,
        "own_gradients",
        [VMEM] * 7,
        [shaped((HALF, BLOCK), bf16), shaped((HALF, 2 * BLOCK), bf16)]
        + [shaped((ROWS, PAIR), f32)] * 2,
        [
            pltpu.VMEM((MIXED + 1, 2 * BLOCK, PAIR), bf16),
            pltpu.VMEM((HALF, 2 * BLOCK), bf16),
            pltpu.VMEM((MIXED + 1, 2 * BLOCK, PAIR), f32),
        ],
    )(*sources)


def next_kernel(
    groups,
    own,
    partner,
    both_own,
    both_partner,
    own_grads,
    partner_grads,
    clips,
    mine,
    swap,
    keys_all,
    query_all,
    mask,
    grads,
    stats,
):
    half = my_half()
    stats[...] = stats_of(both_partner)
    gather_blocks(keys_all, 0, own, partner)
    gather_blocks(query_all, 0, both_own, both_partner)
    for block in range(MIXED + 1):
        grads[block, at(half, BLOCK)] = own_grads[rows_of(block)]
        grads[block, at(1 - half, BLOCK)] = partner_grads[rows_of(block)]
    present = jnp.where(my_group() < groups - 1, 1.0, 0.0)
    older, every, _ = triangles()
    for query_block, block, shape in ((0, 0, older), (0, 1, every), (1, 1, older)):
        query_clip = stats[CLIP_STAT : CLIP_STAT + 1, rows_of(query_block)]
        key_clip = clips[(2 + block) * CLIP_ROWS : (3 + block) * CLIP_ROWS].astype(f32)[0:1]
        same = jnp.where(key_clip == query_clip, 1.0, 0.0)
        mask[query_block, rows_of(block)] = shape * same * present

    def operands(pair, query_block):
        steps = rows_of(query_block)
        if pair < PAIRS:
            query_rows = doubled(query_all[pair, steps], SCALING)
            return query_rows, doubled(query_all[PAIRS + pair, steps])
        rows = query_all[MIXED, steps]
        query_rows = rows * low_or_high(SCALING, 0.0).astype(bf16)
        return query_rows, rows * low_or_high(0.0, 1.0).astype(bf16)

    def score(pair, query_block, _):
        keys = slice(query_block * BLOCK, WIN)
        query_rows, d_rows = operands(pair, query_block)
        key_block, value_block = (pair, PAIRS + pair) if pair < PAIRS else (MIXED, MIXED)
        scores = times(keys_all[key_block, keys], query_rows, ((1,), (1,)))
        return scores, times(keys_all[value_block, keys], d_rows, ((1,), (1,)))

    def weigh(pair, query_block, values):
        scores, d_weights = values
        row = 2 * pair + query_block
        lanes = slice(0, scores.shape[1])
        scores = hidden(scores, mask[query_block, query_block * BLOCK : WIN])
        weights = jnp.exp(scores - stats[row : row + 1, lanes]).astype(bf16)
        delta = stats[DELTA_STAT + row : DELTA_STAT + row + 1, lanes]
        return weights, (weights.astype(f32) * (d_weights - delta)).astype(bf16)

    def products(pair, query_block, values):
        weights, d_scores = values
        keys = slice(query_block * BLOCK, WIN)
        query_rows, d_rows = operands(pair, query_block)
        dk = times(d_scores, query_rows, ((1,), (0,)))
        dv = times(weights, d_rows, ((1,), (0,)))
        if pair < PAIRS:
            grads[pair, keys] += dk
            grads[PAIRS + pair, keys] += dv
        else:
            grads[MIXED, keys] += dk + dv

    items = [(pair, query_block) for pair in range(PAIRS + 1) for query_block in range(2)]
    staggered(items, 2, score, weigh, products)
    for block in range(MIXED + 1):
        mine[rows_of(block)] = grads[block, at(half, BLOCK)].astype(bf16)
        swap[rows_of(block)] = grads[block, at(1 - half, BLOCK)].astype(bf16)


def next_gradients(groups, *sources):
    return kernel(
        functools.partial(next_kernel, groups),
        "next_gradients",
        [VMEM] * 7,
        [shaped((ROWS, PAIR), bf16)] * 2,
        [
            pltpu.VMEM((MIXED + 1, 2 * BLOCK, PAIR), bf16),
            pltpu.VMEM((MIXED + 1, 2 * BLOCK, PAIR), bf16),
            pltpu.VMEM((2, 2 * BLOCK, BLOCK), f32),
            pltpu.VMEM((MIXED + 1, 2 * BLOCK, PAIR), f32),
            pltpu.VMEM((STAT_ROWS, 2 * BLOCK), f32),
        ],
        flops=COST_NEXT,
    )(*sources)


def join_halves(full, halves, mine, theirs):
    half = my_half()
    halves[half] = mine
    halves[1 - half] = theirs
    for side in range(2):
        for pair in range(PAIRS):
            full[rows_of(FIRST_BLOCKS[pair] + side)] = halves[side, head_rows(pair)]
        begin = SHARED + side * HDIM
        full[begin : begin + HDIM] = halves[side, single_rows()]


def output_kernel(att_own, received, dq_mine, weight, out, query_out, full, dq_all, halves, query, sem):
    join_halves(dq_all, halves, dq_mine[...], received[:, BLOCK:])
    for block in range(WIDTH // PAIR):
        query[:, block * PAIR : (block + 1) * PAIR] = dq_all[rows_of(block)].T
    copy = pltpu.make_async_copy(query, query_out, sem)
    copy.start()
    join_halves(full, halves, att_own[...], received[:, :BLOCK])
    out[...] = times(weight[...], full[...], ((1,), (0,))).T.astype(bf16)
    copy.wait()


def output_rows(att_own, received, dq_mine, weight):
    return kernel(
        output_kernel,
        "output",
        [VMEM] * 4,
        [
            shaped((BLOCK, weight.shape[0]), bf16),
            shaped((BLOCK, WIDTH), bf16),
            shaped((WIDTH, BLOCK), bf16),
        ],
        [
            pltpu.VMEM((WIDTH, BLOCK), bf16),
            pltpu.VMEM((2, HALF, BLOCK), bf16),
            pltpu.VMEM((BLOCK, WIDTH), bf16),
            pltpu.SemaphoreType.DMA,
        ],
        (VMEM, HBM, VMEM),
    )(att_own, received, dq_mine, weight)


def place_kernel(
    mine, theirs, kept, arrived, key_out, value_out, weight_out, key, value, mixed, parts, total, sems
):
    half = my_half()
    moves = [(total, weight_out), (key, key_out), (value, value_out)]
    copies = [pltpu.make_async_copy(a, b, sems.at[n]) for n, (a, b) in enumerate(moves)]
    for side, source in ((half, mine), (1 - half, theirs)):
        for pair in range(PAIRS):
            key[:, columns_of(side, pair)] = source[rows_of(pair)]
            value[:, columns_of(side, pair)] = source[rows_of(PAIRS + pair)]
        mixed[side] = source[rows_of(MIXED)].astype(f32)
    shared = slice(SHARED, SHARED + PAIR)
    key[:, shared] = low_or_high(mixed[0], turned(mixed[1])).astype(bf16)
    copies[1].start()
    value[:, shared] = low_or_high(turned(mixed[0]), mixed[1]).astype(bf16)
    copies[2].start()
    parts[half] = kept[...]
    parts[1 - half] = arrived[...].astype(f32)
    for sequence, segments in enumerate(SEGMENTS):

        @pl.when(lax.axis_index("dp") == sequence)
        def _():
            for side, source, size, target in segments:
                total[target : target + size] = parts[side, source : source + size]

    copies[0].start()
    for copy in copies:
        copy.wait()


def place(*sources):
    weight_rows = 2 * HALF // len(SEGMENTS)
    wide = pltpu.VMEM((BLOCK, WIDTH), bf16)
    *grads, weight = kernel(
        place_kernel,
        "place",
        [VMEM] * 4,
        [shaped((BLOCK, WIDTH), bf16)] * 2 + [shaped((weight_rows, BLOCK), f32)],
        [
            wide,
            wide,
            pltpu.VMEM((2, BLOCK, PAIR), f32),
            pltpu.VMEM((2, PIECE_ROWS, BLOCK), f32),
            pltpu.VMEM((weight_rows, BLOCK), f32),
            pltpu.SemaphoreType.DMA((3,)),
        ],
        (HBM,) * 3,
    )(*sources)
    return *grads, weight.T


def weight_kernel(count, *refs):
    pieces, cots, products = refs[:count], refs[count : 2 * count], refs[-1]
    half = my_half()
    att = jnp.concatenate([piece[:, at(half, BLOCK)] for piece in pieces], axis=1)
    products[...] = times(att, jnp.concatenate([cot[...] for cot in cots], axis=0), ((1,), (0,)))


def weight_products(pieces, cots):
    return kernel(
        functools.partial(weight_kernel, len(pieces)),
        "weight_products",
        [VMEM] * (2 * len(pieces)),
        [shaped((pieces[0].shape[0], cots[0].shape[1]), f32)],
        flops=COST_FIRST,
    )(*pieces, *cots)[0]


def weight_rest_kernel(count, products, *refs):
    pieces, cots = refs[:count], refs[count : 2 * count]
    kept, *sent = refs[2 * count :]
    total = sent.pop()
    half = my_half()
    att = jnp.concatenate([piece[:, at(1 - half, BLOCK)] for piece in pieces], axis=1)
    cot = jnp.concatenate([cot[...] for cot in cots], axis=0)
    total[...] = products[...] + times(att, cot, ((1,), (0,)))
    group = my_group()
    lanes = kept.shape[1]
    kept[...] = total[:, at(group, lanes)]
    for number, out in enumerate(sent):
        target = jnp.bitwise_xor(group, number + 1)
        out[...] = total[:, at(target, lanes)].astype(bf16)


def weight_rest(products, pieces, cots, groups):
    rows, outs = products.shape
    part = (rows, outs // groups)
    return kernel(
        functools.partial(weight_rest_kernel, len(pieces)),
        "weight_rest",
        [VMEM] * (1 + 2 * len(pieces)),
        [shaped(part, f32)] + [shaped(part, bf16)] * (groups - 1),
        [pltpu.VMEM((rows, outs), f32)],
    )(products, *pieces, *cots)


def weight_sum_kernel(kept, *rest):
    received, (mine, sent, total) = rest[:-3], rest[-3:]
    value = kept[...]
    for part in received:
        value = value + part[...].astype(f32)
    total[...] = value
    half = my_half()
    mine[...] = total[:, at(half, BLOCK)]
    sent[...] = total[:, at(1 - half, BLOCK)].astype(bf16)


def weight_sum(kept, received):
    rows, lanes = kept.shape
    return kernel(
        weight_sum_kernel,
        "weight_sum",
        [VMEM] * (1 + len(received)),
        [shaped((rows, BLOCK), f32), shaped((rows, BLOCK), bf16)],
        [pltpu.VMEM((rows, lanes), f32)],
        flops=COST_SUM,
    )(kept, *received)


def swapped(value, axis, bits):
    count = lax.axis_size(axis)
    return lax.ppermute(value, axis, [(source, source ^ bits) for source in range(count)])


def rotated(value, axis, steps):
    count = lax.axis_size(axis)
    return lax.ppermute(
        value, axis, [(source, (source + steps) % count) for source in range(count)]
    )


def moved(value, axis, steps):
    count = lax.axis_size(axis)
    first, last = (max(0, -steps), min(count, count - steps))
    return lax.ppermute(value, axis, [(source, source + steps) for source in range(first, last)])


def after(*values):
    return lax.optimization_barrier(values)


def per_device(queries, key_states, value_states, out_cotangent, out_weight, block_clip):
    sequences = lax.axis_size("dp")
    groups = lax.axis_size("ctx") // 2
    short = sequences == 4 and groups in (2, 4)
    cotangent = out_cotangent[0]

    swap_kv, own_kv, swap_query, query = pack(queries[0], key_states[0], value_states[0])
    swap_kv, cot_early, clip = after(swap_kv, cotangent, block_clip)
    own = label(clip, own_kv)
    partner = swapped(swap_kv, "ctx", 1)
    halo = rotated(own, "ctx", 2)
    both_own, d_turned_own, weight = own_cotangents(cotangent, out_weight, query)
    cots = [cotangent]
    if short:
        cots += [swapped(cot_early, "dp", n) for n in (1, 2)]

    partner, both_own, swap_query, cot_late = after(partner, both_own, swap_query, cotangent)
    cot_partner = swapped(cot_late, "ctx", 1)
    halo_other = rotated(partner, "ctx", 2)
    query_partner = swapped(label_query(swap_query, own, halo), "ctx", 1)
    halo, both_own, *cots = after(halo, both_own, *cots)
    next_own = moved(both_own, "ctx", -2)
    if short:
        cots.append(swapped(cots[2], "dp", 1))
    keys_all, query_all, mask, clip_row, clips = gathered(
        own, partner, halo, halo_other, query, query_partner
    )
    weights, single, totals, att, att_own, att_swap, *pieces = forward(
        4 if short else 0, keys_all, query_all, mask, clip_row
    )
    if short:
        cot_across = swapped(cot_partner, "dp", 2)
    weights, cot_partner, *pieces = after(weights, cot_partner, *pieces)

    if short:
        pieces[1:] = [swapped(pieces[n], "dp", n) for n in (1, 2, 3)]
    both_partner, stats = cotangents(
        cot_partner, weight, query_partner, att, d_turned_own, totals
    )
    both_partner, next_own, *cots = after(both_partner, next_own, *cots)
    next_partner = rotated(both_partner, "ctx", -2)
    dq_own, swap, own_grads, partner_grads = own_gradients(
        keys_all, both_own, both_partner, weights, single, stats, att_swap
    )
    own_grads, swap, *pieces = after(own_grads, swap, *pieces)

    if short:
        own_grads, cot_partner, cot_across = after(own_grads, cot_partner, cot_across)
        later = [cot_partner, swapped(cot_partner, "dp", 1), cot_across]
        later.append(swapped(cot_across, "dp", 1))
        products = weight_products(pieces, cots)
        products, swap = after(products, swap)
        kept, *sent = weight_rest(products, pieces, later, groups)
        arrived = [swapped(part, "ctx", 2 * (n + 1)) for n, part in enumerate(sent)]
        kept, own_grads = after(kept, own_grads)
    received = swapped(swap, "ctx", 1)
    kv_own, kv_swap = next_gradients(
        groups, own, partner, next_own, next_partner, own_grads, partner_grads, clips
    )
    kv_rest = swapped(kv_swap, "ctx", 1)
    kv_own, received = after(kv_own, received)
    sublayer_out, query_grad, att_full = output_rows(att_own, received, dq_own, weight)
    if short:
        kept, kv_own, sublayer_out, *arrived = after(kept, kv_own, sublayer_out, *arrived)
        kept, sent = weight_sum(kept, arrived)
        arrived = swapped(sent, "ctx", 1)
    if not short:
        product = lax.dot_general(
            cotangent, att_full, (((0,), (1,)), ((), ())), preferred_element_type=f32
        ).astype(bf16)
        sequence_grad = lax.psum_scatter(product, "ctx", scatter_dimension=0, tiled=True)
        weight_grad = lax.psum_scatter(
            sequence_grad.astype(f32), "dp", scatter_dimension=1, tiled=True
        )
        kept = jnp.zeros((PIECE_ROWS, BLOCK), f32)
        arrived = kept.astype(bf16)
    key_grad, value_grad, placed_weight = place(kv_own, kv_rest, kept, arrived)
    if short:
        weight_grad = placed_weight
    return (
        sublayer_out[None],
        query_grad[None],
        key_grad[None],
        value_grad[None],
        weight_grad,
    )


def solution(mesh):
    return jax.shard_map(
        per_device,
        mesh=mesh,
        in_specs=(
            P("dp", "ctx", None),
            P("dp", "ctx", None),
            P("dp", "ctx", None),
            P("dp", "ctx", None),
            P(),
            P("dp", "ctx"),
        ),
        out_specs=(
            P("dp", "ctx", None),
            P("dp", "ctx", None),
            P("dp", "ctx", None),
            P("dp", "ctx", None),
            P("ctx", "dp"),
        ),
        check_vma=False,
    )
```

```python
import functools
import math

import jax
import jax.numpy as jnp
from jax import lax
from jax.experimental import pallas as pl
from jax.experimental.pallas import tpu as pltpu
from jax.sharding import PartitionSpec as P

HEADS = 18
HDIM = 64
BLOCK = 128
WIN = 256
PAIR = 2 * HDIM
WIDTH = HEADS * HDIM
HALF = WIDTH // 2
PAIRS = HEADS // 4
SHARED = PAIRS * PAIR
MIXED = 2 * PAIRS
ROWS = (MIXED + 1) * BLOCK
FIRST_BLOCKS = (0, 2, 5, 7)
HEAD_STARTS = (0, 128, 320, 448)
SINGLE_START = 256
PIECE_ROWS = 160
ATT_ROWS = HEAD_STARTS[-1] + PIECE_ROWS
SEGMENTS = (
    ((0, 0, 128, 0), (0, 128, 32, 256), (1, 0, 128, 128)),
    ((0, 0, 96, 0), (0, 96, 64, 224), (1, 0, 128, 96)),
    ((0, 0, 128, 64), (1, 0, 64, 0), (1, 64, 96, 192)),
    ((0, 0, 128, 32), (1, 0, 32, 0), (1, 32, 128, 160)),
)
CLIP_ROWS = 16
CLIP_STAT = 2 * PAIRS + 2
DELTA_STAT = CLIP_STAT + 2
STAT_ROWS = 24
SENT_ROWS = ROWS + 6 * STAT_ROWS
CHUNKS = 4
SCALING = 1.0 / math.sqrt(HDIM)
COST_GATHER = 1_500_000_000
COST_KEYS = 1_000_000
COST_FIRST = 2_000_000_000
COST_NEXT = 4_000_000_000
COST_SUM = 2_000_000_000
VMEM_LIMIT = 24 * 1024 * 1024

big_negative = -1e30
bf16 = jnp.bfloat16
f32 = jnp.float32

VMEM = pl.BlockSpec(memory_space=pltpu.VMEM)
HBM = pl.BlockSpec(memory_space=pltpu.HBM)


def shaped(shape, dtype):
    return jax.ShapeDtypeStruct(shape, dtype)


def kernel(body, name, ins, outs, scratch=(), spaces=None, flops=1_000_000):
    return pl.pallas_call(
        body,
        out_shape=tuple(outs),
        in_specs=list(ins),
        out_specs=spaces or (VMEM,) * len(outs),
        scratch_shapes=list(scratch),
        compiler_params=pltpu.CompilerParams(vmem_limit_bytes=VMEM_LIMIT),
        cost_estimate=pl.CostEstimate(flops=flops, bytes_accessed=10_000, transcendentals=0),
        name=name,
    )


def in_hbm(value):
    return pltpu.with_memory_space_constraint(value, pltpu.HBM)


def my_half():
    return jnp.bitwise_and(lax.axis_index("ctx"), 1)


def my_group():
    return jnp.right_shift(lax.axis_index("ctx"), 1)


def at(index, size):
    return pl.ds(pl.multiple_of(index * size, size), size)


def span(start, size, unit):
    return pl.ds(pl.multiple_of(start, unit), size)


def rows_of(block):
    return slice(block * BLOCK, (block + 1) * BLOCK)


def columns_of(half, pair):
    return span((FIRST_BLOCKS[pair] + half) * PAIR, PAIR, PAIR)


def head_rows(pair):
    return slice(HEAD_STARTS[pair], HEAD_STARTS[pair] + PAIR)


def single_rows():
    return slice(SINGLE_START, SINGLE_START + HDIM)


def times(a, b, dims):
    return lax.dot_general(a, b, (dims, ((), ())), preferred_element_type=f32)


def is_low():
    return lax.broadcasted_iota(jnp.int32, (1, PAIR), 1) < HDIM


def low_or_high(low_value, high_value):
    return jnp.where(is_low(), low_value, high_value)


def turned(value):
    return pltpu.roll(value, HDIM, 1)


def pack_kernel(query, key, value, swap_kv, own_kv, swap_query, own_query, *scratch):
    query_all, key_all, value_all, mixed, single, sems = scratch
    half = my_half()
    pairs = ((key, key_all), (value, value_all), (query, query_all))
    copies = [pltpu.make_async_copy(a, b, sems.at[n]) for n, (a, b) in enumerate(pairs)]
    for copy in copies:
        copy.start()
    shared = slice(SHARED, SHARED + PAIR)
    for copy in copies[:2]:
        copy.wait()
    for side, target in ((1 - half, swap_kv), (half, own_kv)):
        for pair in range(PAIRS):
            target[rows_of(pair)] = key_all[:, columns_of(side, pair)]
            target[rows_of(PAIRS + pair)] = value_all[:, columns_of(side, pair)]
    key_shared = key_all[:, shared].astype(f32)
    value_shared = value_all[:, shared].astype(f32)
    mixed[0] = low_or_high(key_shared, turned(value_shared)).astype(bf16)
    mixed[1] = low_or_high(turned(key_shared), value_shared).astype(bf16)
    swap_kv[rows_of(MIXED)] = mixed[1 - half]
    own_kv[rows_of(MIXED)] = mixed[half]
    copies[2].wait()
    for pair in range(PAIRS):
        swap_query[rows_of(pair)] = query_all[:, columns_of(1 - half, pair)]
        own_query[rows_of(pair)] = query_all[:, columns_of(half, pair)]
    query_shared = query_all[:, shared].astype(f32)
    single[0] = low_or_high(query_shared, 0.0)
    single[1] = low_or_high(turned(query_shared), 0.0)
    own_query[rows_of(PAIRS)] = single[half].astype(bf16)
    theirs = single[1 - half]
    swap_query[SHARED:] = low_or_high(theirs[:HDIM], turned(theirs[HDIM:])).astype(bf16)


def pack(query, key, value):
    wide = pltpu.VMEM((BLOCK, WIDTH), bf16)
    return kernel(
        pack_kernel,
        "pack",
        [HBM] * 3,
        [shaped((ROWS, PAIR), bf16)] * 2
        + [shaped((HALF, PAIR), bf16), shaped((SHARED + PAIR, PAIR), bf16)],
        [
            wide,
            wide,
            wide,
            pltpu.VMEM((2, BLOCK, PAIR), bf16),
            pltpu.VMEM((2, BLOCK, PAIR), f32),
            pltpu.SemaphoreType.DMA((3,)),
        ],
    )(in_hbm(query), in_hbm(key), in_hbm(value))


def label_kernel(clip, own_kv, out):
    out[:ROWS] = own_kv[...]
    clip_rows = jnp.broadcast_to(clip[...].astype(f32), (CLIP_ROWS, PAIR))
    out[ROWS:] = clip_rows.astype(bf16)


def label(clip, own_kv):
    return kernel(
        label_kernel,
        "label",
        [VMEM] * 2,
        [shaped((ROWS + CLIP_ROWS, PAIR), bf16)],
    )(clip, own_kv)[0]


def label_query_kernel(query, own, halo, out):
    out[:HALF] = query[...]
    out[HALF : HALF + CLIP_ROWS] = own[ROWS:]
    out[HALF + CLIP_ROWS :] = halo[ROWS:]


def label_query(query, own, halo):
    return kernel(
        label_query_kernel,
        "label_query",
        [VMEM] * 3,
        [shaped((HALF + 2 * CLIP_ROWS, PAIR), bf16)],
    )(query, own, halo)[0]


def unpacked_single(packed):
    packed = packed.astype(f32)
    top, bottom = low_or_high(packed, 0.0), low_or_high(turned(packed), 0.0)
    return jnp.concatenate([top, bottom], axis=0).astype(bf16)


def join_query(target, d_turned, single, query, query_single, d_pairs, d_shared):
    half = my_half()
    for pair in range(PAIRS):
        d_pair = d_pairs[:, pair * PAIR : (pair + 1) * PAIR].astype(bf16)
        target[rows_of(pair)] = query[rows_of(pair)]
        target[rows_of(PAIRS + pair)] = d_pair
        d_turned[head_rows(pair)] = d_pair.T
    single[0] = low_or_high(0.0, turned(d_shared)).astype(bf16)
    single[1] = low_or_high(0.0, d_shared).astype(bf16)
    d_single = single[half]
    target[rows_of(MIXED)] = query_single + d_single
    d_turned[single_rows()] = d_single.T[HDIM:]


def own_cotangent_kernel(cotangent, weight, query, both, d_turned, kept, rows, single, sems):
    half = my_half()
    chunk = rows.shape[1] // CHUNKS
    copies = [pltpu.make_async_copy(cotangent, rows, sems.at[CHUNKS])]
    for number in range(CHUNKS):
        part = pl.ds(number * chunk, chunk)
        copies.append(pltpu.make_async_copy(weight.at[part], kept.at[part], sems.at[number]))
    for copy in copies:
        copy.start()
    copies[0].wait()
    pairs = shared = None
    for number in range(CHUNKS):
        copies[number + 1].wait()
        part = slice(number * chunk, (number + 1) * chunk)
        columns = [kept[part, columns_of(half, pair)] for pair in range(PAIRS)]
        wide = times(rows[:, part], jnp.concatenate(columns, axis=1), ((1,), (0,)))
        narrow = times(rows[:, part], kept[part, SHARED : SHARED + PAIR], ((1,), (0,)))
        pairs = wide if pairs is None else pairs + wide
        shared = narrow if shared is None else shared + narrow
    join_query(both, d_turned, single, query, query[rows_of(PAIRS)], pairs, shared)


def own_cotangents(cotangent, weight, query):
    return kernel(
        own_cotangent_kernel,
        "own_cotangents",
        [HBM, HBM, VMEM],
        [shaped((ROWS, PAIR), bf16), shaped((HALF, BLOCK), bf16), shaped(weight.shape, bf16)],
        [
            pltpu.VMEM(cotangent.shape, bf16),
            pltpu.VMEM((2, BLOCK, PAIR), bf16),
            pltpu.SemaphoreType.DMA((CHUNKS + 1,)),
        ],
    )(in_hbm(cotangent), in_hbm(weight), query)


def cotangent_kernel(
    cotangent, weight, query, att, d_turned_own, totals, both, stats, d_turned, d_all, single
):
    half = my_half()
    rows = cotangent[...]
    columns = [weight[:, columns_of(half, pair)] for pair in range(PAIRS)]
    pairs = times(rows, jnp.concatenate(columns, axis=1), ((1,), (0,)))
    shared = times(rows, weight[:, SHARED : SHARED + PAIR], ((1,), (0,)))
    query_single = unpacked_single(query[SHARED:HALF])
    join_query(both, d_turned, single, query, query_single, pairs, shared)
    d_all[:, at(half, BLOCK)] = d_turned_own[...]
    d_all[:, at(1 - half, BLOCK)] = d_turned[...]
    stats[...] = totals[...]
    for query_block in range(2):
        steps = rows_of(query_block)
        for pair in range(PAIRS):
            which = head_rows(pair)
            dots = d_all[which, steps].astype(f32) * att[which, steps].astype(f32)
            row = DELTA_STAT + 2 * pair + query_block
            stats[row : row + 1, :BLOCK] = jnp.sum(dots[:HDIM], axis=0, keepdims=True)
            stats[row : row + 1, BLOCK:] = jnp.sum(dots[HDIM:], axis=0, keepdims=True)
        which = single_rows()
        dots = d_all[which, steps].astype(f32) * att[which, steps].astype(f32)
        row = DELTA_STAT + 2 * PAIRS + query_block
        stats[row : row + 1, :BLOCK] = jnp.sum(dots, axis=0, keepdims=True)
    rest = jnp.concatenate([stats[:, :BLOCK], stats[:, BLOCK:]], axis=0)
    for number in range(3):
        begin = ROWS + 2 * STAT_ROWS * number
        part = rest.astype(bf16)
        both[begin : begin + 2 * STAT_ROWS] = part
        rest = rest - part.astype(f32)


def stats_of(both):
    parts = []
    for number in range(3):
        begin = ROWS + 2 * STAT_ROWS * number
        parts.append(both[begin : begin + 2 * STAT_ROWS].astype(f32))
    total = (parts[0] + parts[1]) + parts[2]
    return jnp.concatenate([total[:STAT_ROWS], total[STAT_ROWS:]], axis=1)


def cotangents(cotangent, weight, query, att, d_turned_own, totals):
    return kernel(
        cotangent_kernel,
        "cotangents",
        [VMEM] * 6,
        [shaped((SENT_ROWS, PAIR), bf16), shaped((STAT_ROWS, 2 * BLOCK), f32)],
        [
            pltpu.VMEM((HALF, BLOCK), bf16),
            pltpu.VMEM((HALF, 2 * BLOCK), bf16),
            pltpu.VMEM((2, BLOCK, PAIR), bf16),
        ],
    )(cotangent, weight, query, att, d_turned_own, totals)


def gather_blocks(target, offset, own, partner):
    half = my_half()
    for block in range(target.shape[0]):
        target[block, at(offset + half, BLOCK)] = own[rows_of(block)]
        target[block, at(offset + 1 - half, BLOCK)] = partner[rows_of(block)]


def doubled(rows, factor=1.0):
    first = low_or_high(factor, 0.0).astype(bf16)
    second = low_or_high(0.0, factor).astype(bf16)
    return jnp.concatenate([rows * first, rows * second], axis=0)


def diagonal(pair):
    return jnp.concatenate([pair[:HDIM, :BLOCK], pair[HDIM:, BLOCK:]], axis=0)


def triangles():
    row = lax.broadcasted_iota(jnp.int32, (BLOCK, BLOCK), 0)
    lane = lax.broadcasted_iota(jnp.int32, (BLOCK, BLOCK), 1)
    older = jnp.where(row > lane, 1.0, 0.0)
    return older, jnp.ones((BLOCK, BLOCK), f32), 1.0 - older


def hidden(scores, visible):
    if scores.shape[1] > visible.shape[1]:
        visible = jnp.concatenate([visible, visible], axis=1)
    return jnp.where(visible > 0.5, scores, big_negative)


def gather_kernel(
    own, partner, halo, halo_other, query_own, query_partner, keys_all, query_all, mask, clip_row, clips
):
    half = my_half()
    gather_blocks(keys_all, 0, halo, halo_other)
    gather_blocks(keys_all, 2, own, partner)
    for pair in range(PAIRS):
        query_all[pair, at(half, BLOCK)] = query_own[rows_of(pair)]
        query_all[pair, at(1 - half, BLOCK)] = query_partner[rows_of(pair)]
    query_all[PAIRS, at(half, BLOCK)] = query_own[rows_of(PAIRS)]
    query_all[PAIRS, at(1 - half, BLOCK)] = unpacked_single(query_partner[SHARED:HALF])
    clips[at(half, CLIP_ROWS)] = halo[ROWS:]
    clips[at(1 - half, CLIP_ROWS)] = query_partner[HALF + CLIP_ROWS :]
    clips[at(2 + half, CLIP_ROWS)] = own[ROWS:]
    clips[at(3 - half, CLIP_ROWS)] = query_partner[HALF : HALF + CLIP_ROWS]

    def clip_of(block):
        return clips[block * CLIP_ROWS : (block + 1) * CLIP_ROWS].astype(f32)[0:1]

    for query_block in range(2):
        query_clip = clip_of(2 + query_block)
        for step, shape in enumerate(triangles()):
            block = query_block + step
            same = jnp.where(clip_of(block) == query_clip, 1.0, 0.0)
            present = jnp.where(2 * my_group() - 2 + block >= 0, 1.0, 0.0)
            mask[query_block, rows_of(step)] = shape * same * present
        clip_row[:, rows_of(query_block)] = query_clip


def gathered(*sources):
    return kernel(
        gather_kernel,
        "gathered",
        [VMEM] * 6,
        [
            shaped((MIXED + 1, 4 * BLOCK, PAIR), bf16),
            shaped((PAIRS + 1, 2 * BLOCK, PAIR), bf16),
            shaped((2, WIN + BLOCK, BLOCK), f32),
            shaped((1, 2 * BLOCK), f32),
            shaped((4 * CLIP_ROWS, PAIR), bf16),
        ],
        flops=COST_GATHER,
    )(*sources)


def staggered(items, apart, *stages):
    values = [None] * len(items)
    for step in range(len(items) + apart * (len(stages) - 1)):
        for number, stage in enumerate(stages):
            index = step - apart * number
            if 0 <= index < len(items):
                values[index] = stage(*items[index], values[index])


def forward_kernel(
    pieces_wanted,
    keys_all,
    query_all,
    mask,
    clip_row,
    weights_out,
    single_out,
    totals,
    att,
    att_own,
    att_swap,
    *pieces,
):
    half = my_half()
    totals[CLIP_STAT : CLIP_STAT + 1] = clip_row[...]

    def softmax(scores, row):
        lanes = slice(0, scores.shape[1])
        maximum = jnp.max(scores, axis=0, keepdims=True)
        powers = jnp.exp(scores - maximum)
        total = jnp.sum(powers, axis=0, keepdims=True)
        totals[row : row + 1, lanes] = maximum + jnp.log(total)
        return (powers * (1.0 / total)).astype(bf16)

    def keys_of(query_block):
        return slice(query_block * BLOCK, query_block * BLOCK + WIN + BLOCK)

    def score(pair, query_block, _):
        rows = query_all[pair, rows_of(query_block)]
        if pair < PAIRS:
            key_rows, rows = keys_all[pair, keys_of(query_block)], doubled(rows, SCALING)
        else:
            key_rows = keys_all[MIXED, keys_of(query_block)]
            rows = rows * low_or_high(SCALING, 0.0).astype(bf16)
        return times(key_rows, rows, ((1,), (1,)))

    def weigh(pair, query_block, scores):
        return softmax(hidden(scores, mask[query_block]), 2 * pair + query_block)

    def mix(pair, query_block, weights):
        steps = rows_of(query_block)
        if pair < PAIRS:
            weights_out[pair, query_block] = weights
            mixed = times(keys_all[PAIRS + pair, keys_of(query_block)], weights, ((0,), (0,)))
            att[head_rows(pair), steps] = diagonal(mixed).astype(bf16)
        else:
            single_out[query_block] = weights
            mixed = times(keys_all[MIXED, keys_of(query_block)], weights, ((0,), (0,)))
            att[single_rows(), steps] = mixed[HDIM:].astype(bf16)

    items = [(pair, query_block) for pair in range(PAIRS + 1) for query_block in range(2)]
    staggered(items, 4, score, weigh, mix)

    att[HALF:] = jnp.zeros((ATT_ROWS - HALF, 2 * BLOCK), bf16)
    att_own[...] = att[:HALF, at(half, BLOCK)]
    att_swap[...] = att[:HALF, at(1 - half, BLOCK)]
    for number, piece in enumerate(pieces):
        target = jnp.bitwise_xor(lax.axis_index("dp"), number)
        late = 32 * jnp.maximum(target - 2, 0)
        begin = jnp.where(half == 0, 160 * target - late, 128 * target + late)
        piece[...] = att[span(begin, PIECE_ROWS, 32), :]


def forward(pieces_wanted, *sources):
    piece = (PIECE_ROWS, 2 * BLOCK)
    return kernel(
        functools.partial(forward_kernel, pieces_wanted),
        "forward",
        [VMEM] * 4,
        [
            shaped((PAIRS, 2, WIN + BLOCK, 2 * BLOCK), bf16),
            shaped((2, WIN + BLOCK, BLOCK), bf16),
            shaped((STAT_ROWS, 2 * BLOCK), f32),
            shaped((ATT_ROWS, 2 * BLOCK), bf16),
            shaped((HALF, BLOCK), bf16),
            shaped((HALF, BLOCK), bf16),
        ]
        + [shaped(piece, bf16)] * pieces_wanted,
    )(*sources)


def own_kernel(
    keys_all,
    both_own,
    both_partner,
    weights_in,
    single_in,
    stats,
    att_swap,
    dq_own,
    swap,
    own_grads,
    partner_grads,
    query_all,
    dq_all,
    grads,
):
    half = my_half()
    gather_blocks(query_all, 0, both_own, both_partner)

    def delta_of(row, lanes):
        return stats[DELTA_STAT + row : DELTA_STAT + row + 1, :lanes]

    def accumulate(block, query_block, value):
        if query_block == 1:
            grads[block] = value
        else:
            grads[block, :BLOCK] += value

    def keys_of(query_block):
        return slice(query_block * BLOCK, query_block * BLOCK + WIN + BLOCK)

    def operands(pair, query_block):
        steps = rows_of(query_block)
        if pair < PAIRS:
            query_rows = doubled(query_all[pair, steps], SCALING)
            return query_rows, doubled(query_all[PAIRS + pair, steps]), weights_in[pair, query_block]
        rows = query_all[MIXED, steps]
        query_rows = rows * low_or_high(SCALING, 0.0).astype(bf16)
        d_rows = rows * low_or_high(0.0, 1.0).astype(bf16)
        return query_rows, d_rows, single_in[query_block]

    def d_weights_of(pair, query_block, _):
        block = PAIRS + pair if pair < PAIRS else MIXED
        _, d_rows, _ = operands(pair, query_block)
        return times(keys_all[block, keys_of(query_block)], d_rows, ((1,), (1,)))

    def d_scores_of(pair, query_block, d_weights):
        _, _, weights = operands(pair, query_block)
        delta = delta_of(2 * pair + query_block, d_weights.shape[1])
        return (weights.astype(f32) * (d_weights - delta)).astype(bf16)

    def products(pair, query_block, d_scores):
        query_rows, d_rows, weights = operands(pair, query_block)
        mine = slice(WIN - query_block * BLOCK, WIN + BLOCK)
        steps = rows_of(query_block)
        block = pair if pair < PAIRS else MIXED
        dq = times(keys_all[block, keys_of(query_block)], d_scores, ((0,), (0,)))
        dk = times(d_scores[mine], query_rows, ((1,), (0,)))
        dv = times(weights[mine], d_rows, ((1,), (0,)))
        if pair < PAIRS:
            dq_all[head_rows(pair), steps] = (diagonal(dq) * SCALING).astype(bf16)
            accumulate(pair, query_block, dk)
            accumulate(PAIRS + pair, query_block, dv)
        else:
            dq_all[single_rows(), steps] = (dq[:HDIM] * SCALING).astype(bf16)
            accumulate(MIXED, query_block, dk + dv)

    items = [(pair, query_block) for pair in range(PAIRS + 1) for query_block in (1, 0)]
    staggered(items, 2, d_weights_of, d_scores_of, products)
    dq_own[...] = dq_all[:, at(half, BLOCK)]
    swap[:, :BLOCK] = att_swap[...]
    swap[:, BLOCK:] = dq_all[:, at(1 - half, BLOCK)]
    for block in range(MIXED + 1):
        own_grads[rows_of(block)] = grads[block, at(half, BLOCK)]
        partner_grads[rows_of(block)] = grads[block, at(1 - half, BLOCK)]


def own_gradients(*sources):
    return kernel(
        own_kernel,
        "own_gradients",
        [VMEM] * 7,
        [shaped((HALF, BLOCK), bf16), shaped((HALF, 2 * BLOCK), bf16)]
        + [shaped((ROWS, PAIR), f32)] * 2,
        [
            pltpu.VMEM((MIXED + 1, 2 * BLOCK, PAIR), bf16),
            pltpu.VMEM((HALF, 2 * BLOCK), bf16),
            pltpu.VMEM((MIXED + 1, 2 * BLOCK, PAIR), f32),
        ],
    )(*sources)


def next_kernel(
    groups,
    own,
    partner,
    both_own,
    both_partner,
    own_grads,
    partner_grads,
    clips,
    mine,
    swap,
    keys_all,
    query_all,
    mask,
    grads,
    stats,
):
    half = my_half()
    stats[...] = stats_of(both_partner)
    gather_blocks(keys_all, 0, own, partner)
    gather_blocks(query_all, 0, both_own, both_partner)
    for block in range(MIXED + 1):
        grads[block, at(half, BLOCK)] = own_grads[rows_of(block)]
        grads[block, at(1 - half, BLOCK)] = partner_grads[rows_of(block)]
    present = jnp.where(my_group() < groups - 1, 1.0, 0.0)
    older, every, _ = triangles()
    for query_block, block, shape in ((0, 0, older), (0, 1, every), (1, 1, older)):
        query_clip = stats[CLIP_STAT : CLIP_STAT + 1, rows_of(query_block)]
        key_clip = clips[(2 + block) * CLIP_ROWS : (3 + block) * CLIP_ROWS].astype(f32)[0:1]
        same = jnp.where(key_clip == query_clip, 1.0, 0.0)
        mask[query_block, rows_of(block)] = shape * same * present

    def operands(pair, query_block):
        steps = rows_of(query_block)
        if pair < PAIRS:
            query_rows = doubled(query_all[pair, steps], SCALING)
            return query_rows, doubled(query_all[PAIRS + pair, steps])
        rows = query_all[MIXED, steps]
        query_rows = rows * low_or_high(SCALING, 0.0).astype(bf16)
        return query_rows, rows * low_or_high(0.0, 1.0).astype(bf16)

    def score(pair, query_block, _):
        keys = slice(query_block * BLOCK, WIN)
        query_rows, d_rows = operands(pair, query_block)
        key_block, value_block = (pair, PAIRS + pair) if pair < PAIRS else (MIXED, MIXED)
        scores = times(keys_all[key_block, keys], query_rows, ((1,), (1,)))
        return scores, times(keys_all[value_block, keys], d_rows, ((1,), (1,)))

    def weigh(pair, query_block, values):
        scores, d_weights = values
        row = 2 * pair + query_block
        lanes = slice(0, scores.shape[1])
        scores = hidden(scores, mask[query_block, query_block * BLOCK : WIN])
        weights = jnp.exp(scores - stats[row : row + 1, lanes]).astype(bf16)
        delta = stats[DELTA_STAT + row : DELTA_STAT + row + 1, lanes]
        return weights, (weights.astype(f32) * (d_weights - delta)).astype(bf16)

    def products(pair, query_block, values):
        weights, d_scores = values
        keys = slice(query_block * BLOCK, WIN)
        query_rows, d_rows = operands(pair, query_block)
        dk = times(d_scores, query_rows, ((1,), (0,)))
        dv = times(weights, d_rows, ((1,), (0,)))
        if pair < PAIRS:
            grads[pair, keys] += dk
            grads[PAIRS + pair, keys] += dv
        else:
            grads[MIXED, keys] += dk + dv

    items = [(pair, query_block) for pair in range(PAIRS + 1) for query_block in range(2)]
    staggered(items, 2, score, weigh, products)
    for block in range(MIXED + 1):
        mine[rows_of(block)] = grads[block, at(half, BLOCK)].astype(bf16)
        swap[rows_of(block)] = grads[block, at(1 - half, BLOCK)].astype(bf16)


def next_gradients(groups, *sources):
    return kernel(
        functools.partial(next_kernel, groups),
        "next_gradients",
        [VMEM] * 7,
        [shaped((ROWS, PAIR), bf16)] * 2,
        [
            pltpu.VMEM((MIXED + 1, 2 * BLOCK, PAIR), bf16),
            pltpu.VMEM((MIXED + 1, 2 * BLOCK, PAIR), bf16),
            pltpu.VMEM((2, 2 * BLOCK, BLOCK), f32),
            pltpu.VMEM((MIXED + 1, 2 * BLOCK, PAIR), f32),
            pltpu.VMEM((STAT_ROWS, 2 * BLOCK), f32),
        ],
        flops=COST_NEXT,
    )(*sources)


def join_halves(full, halves, mine, theirs):
    half = my_half()
    halves[half] = mine
    halves[1 - half] = theirs
    for side in range(2):
        for pair in range(PAIRS):
            full[rows_of(FIRST_BLOCKS[pair] + side)] = halves[side, head_rows(pair)]
        begin = SHARED + side * HDIM
        full[begin : begin + HDIM] = halves[side, single_rows()]


def output_kernel(att_own, received, dq_mine, weight, out, query_out, full, dq_all, halves, query, sem):
    join_halves(dq_all, halves, dq_mine[...], received[:, BLOCK:])
    for block in range(WIDTH // PAIR):
        query[:, block * PAIR : (block + 1) * PAIR] = dq_all[rows_of(block)].T
    copy = pltpu.make_async_copy(query, query_out, sem)
    copy.start()
    join_halves(full, halves, att_own[...], received[:, :BLOCK])
    out[...] = times(weight[...], full[...], ((1,), (0,))).T.astype(bf16)
    copy.wait()


def output_rows(att_own, received, dq_mine, weight):
    return kernel(
        output_kernel,
        "output",
        [VMEM] * 4,
        [
            shaped((BLOCK, weight.shape[0]), bf16),
            shaped((BLOCK, WIDTH), bf16),
            shaped((WIDTH, BLOCK), bf16),
        ],
        [
            pltpu.VMEM((WIDTH, BLOCK), bf16),
            pltpu.VMEM((2, HALF, BLOCK), bf16),
            pltpu.VMEM((BLOCK, WIDTH), bf16),
            pltpu.SemaphoreType.DMA,
        ],
        (VMEM, HBM, VMEM),
    )(att_own, received, dq_mine, weight)


def place_kernel(
    mine, theirs, kept, arrived, key_out, value_out, weight_out, key, value, mixed, parts, total, sems
):
    half = my_half()
    moves = [(total, weight_out), (key, key_out), (value, value_out)]
    copies = [pltpu.make_async_copy(a, b, sems.at[n]) for n, (a, b) in enumerate(moves)]
    for side, source in ((half, mine), (1 - half, theirs)):
        for pair in range(PAIRS):
            key[:, columns_of(side, pair)] = source[rows_of(pair)]
            value[:, columns_of(side, pair)] = source[rows_of(PAIRS + pair)]
        mixed[side] = source[rows_of(MIXED)].astype(f32)
    shared = slice(SHARED, SHARED + PAIR)
    key[:, shared] = low_or_high(mixed[0], turned(mixed[1])).astype(bf16)
    copies[1].start()
    value[:, shared] = low_or_high(turned(mixed[0]), mixed[1]).astype(bf16)
    copies[2].start()
    parts[half] = kept[...]
    parts[1 - half] = arrived[...].astype(f32)
    for sequence, segments in enumerate(SEGMENTS):

        @pl.when(lax.axis_index("dp") == sequence)
        def _():
            for side, source, size, target in segments:
                total[target : target + size] = parts[side, source : source + size]

    copies[0].start()
    for copy in copies:
        copy.wait()


def place(*sources):
    weight_rows = 2 * HALF // len(SEGMENTS)
    wide = pltpu.VMEM((BLOCK, WIDTH), bf16)
    *grads, weight = kernel(
        place_kernel,
        "place",
        [VMEM] * 4,
        [shaped((BLOCK, WIDTH), bf16)] * 2 + [shaped((weight_rows, BLOCK), f32)],
        [
            wide,
            wide,
            pltpu.VMEM((2, BLOCK, PAIR), f32),
            pltpu.VMEM((2, PIECE_ROWS, BLOCK), f32),
            pltpu.VMEM((weight_rows, BLOCK), f32),
            pltpu.SemaphoreType.DMA((3,)),
        ],
        (HBM,) * 3,
    )(*sources)
    return *grads, weight.T


def weight_kernel(count, *refs):
    pieces, cots, products = refs[:count], refs[count : 2 * count], refs[-1]
    half = my_half()
    att = jnp.concatenate([piece[:, at(half, BLOCK)] for piece in pieces], axis=1)
    products[...] = times(att, jnp.concatenate([cot[...] for cot in cots], axis=0), ((1,), (0,)))


def weight_products(pieces, cots):
    return kernel(
        functools.partial(weight_kernel, len(pieces)),
        "weight_products",
        [VMEM] * (2 * len(pieces)),
        [shaped((pieces[0].shape[0], cots[0].shape[1]), f32)],
        flops=COST_FIRST,
    )(*pieces, *cots)[0]


def weight_rest_kernel(count, products, *refs):
    pieces, cots = refs[:count], refs[count : 2 * count]
    kept, *sent = refs[2 * count :]
    total = sent.pop()
    half = my_half()
    att = jnp.concatenate([piece[:, at(1 - half, BLOCK)] for piece in pieces], axis=1)
    cot = jnp.concatenate([cot[...] for cot in cots], axis=0)
    total[...] = products[...] + times(att, cot, ((1,), (0,)))
    group = my_group()
    lanes = kept.shape[1]
    kept[...] = total[:, at(group, lanes)]
    for number, out in enumerate(sent):
        target = jnp.bitwise_xor(group, number + 1)
        out[...] = total[:, at(target, lanes)].astype(bf16)


def weight_rest(products, pieces, cots, groups):
    rows, outs = products.shape
    part = (rows, outs // groups)
    return kernel(
        functools.partial(weight_rest_kernel, len(pieces)),
        "weight_rest",
        [VMEM] * (1 + 2 * len(pieces)),
        [shaped(part, f32)] + [shaped(part, bf16)] * (groups - 1),
        [pltpu.VMEM((rows, outs), f32)],
    )(products, *pieces, *cots)


def weight_sum_kernel(kept, *rest):
    received, (mine, sent, total) = rest[:-3], rest[-3:]
    value = kept[...]
    for part in received:
        value = value + part[...].astype(f32)
    total[...] = value
    half = my_half()
    mine[...] = total[:, at(half, BLOCK)]
    sent[...] = total[:, at(1 - half, BLOCK)].astype(bf16)


def weight_sum(kept, received):
    rows, lanes = kept.shape
    return kernel(
        weight_sum_kernel,
        "weight_sum",
        [VMEM] * (1 + len(received)),
        [shaped((rows, BLOCK), f32), shaped((rows, BLOCK), bf16)],
        [pltpu.VMEM((rows, lanes), f32)],
        flops=COST_SUM,
    )(kept, *received)


def swapped(value, axis, bits):
    count = lax.axis_size(axis)
    return lax.ppermute(value, axis, [(source, source ^ bits) for source in range(count)])


def rotated(value, axis, steps):
    count = lax.axis_size(axis)
    return lax.ppermute(
        value, axis, [(source, (source + steps) % count) for source in range(count)]
    )


def moved(value, axis, steps):
    count = lax.axis_size(axis)
    first, last = (max(0, -steps), min(count, count - steps))
    return lax.ppermute(value, axis, [(source, source + steps) for source in range(first, last)])


def after(*values):
    return lax.optimization_barrier(values)


def per_device(queries, key_states, value_states, out_cotangent, out_weight, block_clip):
    sequences = lax.axis_size("dp")
    groups = lax.axis_size("ctx") // 2
    short = sequences == 4 and groups in (2, 4)
    cotangent = out_cotangent[0]

    swap_kv, own_kv, swap_query, query = pack(queries[0], key_states[0], value_states[0])
    swap_kv, cot_early, clip = after(swap_kv, cotangent, block_clip)
    own = label(clip, own_kv)
    partner = swapped(swap_kv, "ctx", 1)
    halo = rotated(own, "ctx", 2)
    both_own, d_turned_own, weight = own_cotangents(cotangent, out_weight, query)
    cots = [cotangent]
    if short:
        cots += [swapped(cot_early, "dp", n) for n in (1, 2)]

    partner, both_own, swap_query, cot_late = after(partner, both_own, swap_query, cotangent)
    cot_partner = swapped(cot_late, "ctx", 1)
    halo_other = rotated(partner, "ctx", 2)
    query_partner = swapped(label_query(swap_query, own, halo), "ctx", 1)
    halo, both_own, *cots = after(halo, both_own, *cots)
    next_own = moved(both_own, "ctx", -2)
    if short:
        cots.append(swapped(cots[2], "dp", 1))
    keys_all, query_all, mask, clip_row, clips = gathered(
        own, partner, halo, halo_other, query, query_partner
    )
    weights, single, totals, att, att_own, att_swap, *pieces = forward(
        4 if short else 0, keys_all, query_all, mask, clip_row
    )
    if short:
        cot_across = swapped(cot_partner, "dp", 2)
    weights, cot_partner, *pieces = after(weights, cot_partner, *pieces)

    if short:
        pieces[1:] = [swapped(pieces[n], "dp", n) for n in (1, 2, 3)]
    both_partner, stats = cotangents(
        cot_partner, weight, query_partner, att, d_turned_own, totals
    )
    both_partner, next_own, *cots = after(both_partner, next_own, *cots)
    next_partner = rotated(both_partner, "ctx", -2)
    dq_own, swap, own_grads, partner_grads = own_gradients(
        keys_all, both_own, both_partner, weights, single, stats, att_swap
    )
    own_grads, swap, *pieces = after(own_grads, swap, *pieces)

    if short:
        own_grads, cot_partner, cot_across = after(own_grads, cot_partner, cot_across)
        later = [cot_partner, swapped(cot_partner, "dp", 1), cot_across]
        later.append(swapped(cot_across, "dp", 1))
        products = weight_products(pieces, cots)
        products, swap = after(products, swap)
        kept, *sent = weight_rest(products, pieces, later, groups)
        arrived = [swapped(part, "ctx", 2 * (n + 1)) for n, part in enumerate(sent)]
        kept, own_grads = after(kept, own_grads)
    received = swapped(swap, "ctx", 1)
    kv_own, kv_swap = next_gradients(
        groups, own, partner, next_own, next_partner, own_grads, partner_grads, clips
    )
    kv_rest = swapped(kv_swap, "ctx", 1)
    kv_own, received = after(kv_own, received)
    sublayer_out, query_grad, att_full = output_rows(att_own, received, dq_own, weight)
    if short:
        kept, kv_own, sublayer_out, *arrived = after(kept, kv_own, sublayer_out, *arrived)
        kept, sent = weight_sum(kept, arrived)
        arrived = swapped(sent, "ctx", 1)
    if not short:
        product = lax.dot_general(
            cotangent, att_full, (((0,), (1,)), ((), ())), preferred_element_type=f32
        ).astype(bf16)
        sequence_grad = lax.psum_scatter(product, "ctx", scatter_dimension=0, tiled=True)
        weight_grad = lax.psum_scatter(
            sequence_grad.astype(f32), "dp", scatter_dimension=1, tiled=True
        )
        kept = jnp.zeros((PIECE_ROWS, BLOCK), f32)
        arrived = kept.astype(bf16)
    key_grad, value_grad, placed_weight = place(kv_own, kv_rest, kept, arrived)
    if short:
        weight_grad = placed_weight
    return (
        sublayer_out[None],
        query_grad[None],
        key_grad[None],
        value_grad[None],
        weight_grad,
    )


def solution(mesh):
    return jax.shard_map(
        per_device,
        mesh=mesh,
        in_specs=(
            P("dp", "ctx", None),
            P("dp", "ctx", None),
            P("dp", "ctx", None),
            P("dp", "ctx", None),
            P(),
            P("dp", "ctx"),
        ),
        out_specs=(
            P("dp", "ctx", None),
            P("dp", "ctx", None),
            P("dp", "ctx", None),
            P("dp", "ctx", None),
            P("ctx", "dp"),
        ),
        check_vma=False,
    )
```
